32 devices in a mesh: dp: 8 (over z, y), ctx: 4 (over x, core).
Axes of the slice: x: 2, y: 2, z: 4, core: 2. Of those that a mesh axis runs over, the one named last changes fastest.
Arguments:
- tokens: bfloat16 [8192, 768], P(('dp', 'ctx')), may hold values from -12 to 12
- attn_gain: float32 [768], replicated, may hold values from 0.1 to 1.9
- attn_shift: float32 [768], replicated, may hold values from -3 to 3
- w_qkv: bfloat16 [768, 2304], replicated, may hold values from -0.21875 to 0.21875
- w_proj: bfloat16 [768, 768], replicated, may hold values from -1 to 1
- mlp_gain: float32 [768], replicated, may hold values from 0.1 to 1.9
- mlp_shift: float32 [768], replicated, may hold values from -3 to 3
- w_up: bfloat16 [768, 3072], replicated, may hold values from -0.21875 to 0.21875
- w_down: bfloat16 [3072, 768], replicated, may hold values from -0.109375 to 0.109375
- upstream: bfloat16 [8192, 768], P(('dp', 'ctx')), may hold values from -6 to 6
- clip_length: int32 [8], P('dp'), may hold values from 512 to 1024, as said below
- dataset_group: int32 [8, 1], P('dp'), may hold values from 0 to 3
- sample_weight: int32 [8], P('dp'), may hold values from 1 to 4
Outputs:
- block_out: bfloat16 [8192, 768], P(('dp', 'ctx'))
- input_grad: bfloat16 [8192, 768], P(('dp', 'ctx'))
- attn_gain_grad: float32 [768], P(('dp', 'ctx'))
- attn_shift_grad: float32 [768], P(('dp', 'ctx'))
- qkv_grad: float32 [768, 2304], P(('dp', 'ctx'))
- proj_grad: float32 [768, 768], P(('dp', 'ctx'))
- mlp_gain_grad: float32 [768], P(('dp', 'ctx'))
- mlp_shift_grad: float32 [768], P(('dp', 'ctx'))
- up_grad: float32 [768, 3072], P(('dp', 'ctx'))
- down_grad: float32 [3072, 768], P(('dp', 'ctx'))
The draws below stay inside these ranges and needn't reach their ends.
Inputs may be any that keep to these rules, and one draw needn't show every extreme that they name: `clip_length`: some clip has exactly 1024 valid tokens and some exactly 512. `dataset_group`: every group names some clip.
All inputs are finite; a program needn't handle non-finite values.
Results may differ from the reference program's by a relative error of at most 0.015.
Values may be sent and summed in bfloat16 or wider, within the bound.
A program may use at most 192 MiB of HBM per device.

```python
import jax
import jax.numpy as jnp
from jax import lax

D = 768
HEADS = 12
HD = 64
FF = 3072
NGROUPS = 4
SEQ = 1024
LEN_MIN = 512
CLIPS = 8
TOKENS = 8192


def draw_clip_length(key, part):
    first_key, second_key = jax.random.split(jax.random.fold_in(key, 7))
    lengths = jax.random.randint(first_key, (CLIPS,), LEN_MIN, SEQ + 1)
    order = jax.random.permutation(second_key, CLIPS)
    lengths = lengths.at[order[0]].set(SEQ)
    lengths = lengths.at[order[1]].set(LEN_MIN)
    return lengths.astype(jnp.int32)


def place_ends(drawn, key, low, largest):
    longest = drawn.shape.index(max(drawn.shape))
    spots = []
    for shift in (0, 1):
        where = [jax.random.randint(jax.random.fold_in(key, axis), (), 0, length) for axis, length in enumerate(drawn.shape)]
        where[longest] = (where[longest] + shift) % drawn.shape[longest]
        spots.append(tuple(where))
    return drawn.at[spots[0]].set(low).at[spots[1]].set(largest)


def strengthened(drawn, own_key, source, target, blocks, factor):
    def block_of(axis_at):
        return (jnp.arange(drawn.shape[axis_at]) // (drawn.shape[axis_at] // blocks)).reshape((-1,) + (1,) * (drawn.ndim - 1 - axis_at))

    one_side = jax.random.permutation(own_key, blocks)[block_of(target)]
    other_side = (block_of(target) + blocks // 2) % blocks
    return jnp.where((block_of(source) == one_side) | (block_of(source) == other_side), factor * drawn, drawn)


def shard_levels(own_key, extent, shards, low, largest):
    gain = 1.0
    for dim, parts in shards:
        steps = jax.random.uniform(jax.random.fold_in(jax.random.fold_in(own_key, 6), dim), (parts,), jnp.float32, low / len(shards), largest / len(shards))
        gain = gain * jnp.repeat(jnp.exp(steps), extent[dim] // parts).reshape((-1,) + (1,) * (len(extent) - 1 - dim))
    return gain


def distinct(key, rows, number_of, top, lift):
    ranking = jax.random.permutation(jax.random.fold_in(key, 1), number_of)
    pull = ranking
    for power in range(3):
        pull = pull * pull // number_of
    pull = pull * lift // number_of
    tickets = jax.random.randint(jax.random.fold_in(key, 2), (rows, number_of), 0, 4096) + pull
    holders = jax.random.permutation(jax.random.fold_in(key, 3), rows)[jnp.arange(number_of) % rows]
    tickets = jnp.where(jnp.arange(rows)[:, None] == holders[None, :], 1 << 14, tickets)
    merit = tickets * number_of + jnp.arange(number_of)
    return lax.top_k(merit.astype(jnp.int32), top)[1].astype(jnp.int32)


def bell_draw(rng, dims, width, limit, cuts=(), kind=jnp.bfloat16):
    factor_of = shard_levels(rng, dims, cuts, -0.22, 0.18) if cuts else 1.0
    result = jax.random.normal(rng, dims, jnp.float32) * width * factor_of
    return jnp.minimum(jnp.maximum(result, -limit), limit).astype(kind)


def noise_with(own_key, shape, scale, limit, cuts, heavy, kind=jnp.bfloat16):
    drawn = scale * jax.random.normal(own_key, shape, jnp.float32)
    if cuts:
        drawn = drawn * shard_levels(own_key, shape, cuts, -0.22, 0.18)
    return jnp.clip(strengthened(drawn, jax.random.fold_in(own_key, 3), *heavy), -limit, limit).astype(kind)


def setup_inputs(seed: int = 0) -> dict:
    key_list = jax.random.split(jax.random.key(seed), 14)
    tokens = noise_with(key_list[0], (TOKENS, D), 1.0, 12.0, ((0, 32),), (0, 1, 32, 2.75))
    attn_gain = jnp.clip(1.0 + 0.18 * jax.random.normal(key_list[1], (D,), jnp.float32), 0.1, 1.9)
    attn_shift = bell_draw(key_list[2], (D,), 0.5, 3.0, (), jnp.float32)
    w_qkv = bell_draw(key_list[3], (D, 3 * D), D ** -0.5, 0.21875)
    w_proj = bell_draw(key_list[4], (D, D), 32 ** -0.5, 1.0)
    mlp_gain = jnp.clip(1.0 + 0.18 * jax.random.normal(key_list[5], (D,), jnp.float32), 0.1, 1.9)
    mlp_shift = bell_draw(key_list[6], (D,), 0.5, 3.0, (), jnp.float32)
    w_up = bell_draw(key_list[7], (D, FF), D ** -0.5, 0.21875)
    w_down = bell_draw(key_list[8], (FF, D), FF ** -0.5, 0.109375)
    upstream = bell_draw(key_list[9], (TOKENS, D), 1.0, 6.0, ((0, 32),))
    clip_length = draw_clip_length(jax.random.fold_in(key_list[13], 71), 0)
    dataset_group = distinct(key_list[11], CLIPS, NGROUPS, 1, 2048)
    sample_weight = place_ends(jax.random.randint(key_list[12], (CLIPS,), 1, 5), jax.random.fold_in(key_list[12], 1), 1, 4).astype(jnp.int32)
    return dict(tokens=tokens, attn_gain=attn_gain, attn_shift=attn_shift, w_qkv=w_qkv, w_proj=w_proj, mlp_gain=mlp_gain, mlp_shift=mlp_shift, w_up=w_up, w_down=w_down, upstream=upstream, clip_length=clip_length, dataset_group=dataset_group, sample_weight=sample_weight)


@jax.custom_vjp
def low(v):
    return lax.optimization_barrier(v.astype(jnp.bfloat16)).astype(jnp.float32)

@jax.custom_vjp
def low_back(v):
    return v

def low_keep(v):
    return (low(v), None)

def low_pass(kept, grad):
    return (grad,)

def back_keep(v):
    return (v, None)

def back_low(kept, grad):
    return (low(grad),)
low.defvjp(low_keep, low_pass)
low_back.defvjp(back_keep, back_low)
EPSILON = 1e-05
NEG_FILL = -1e+30
GELU_COEF = 0.7978845608028654
HIGH = lax.Precision.HIGHEST

def matmul(left, right):
    return jnp.dot(left, right, precision=HIGH, preferred_element_type=jnp.float32)

def layer_norm(values, gain_vec, shift_vec):
    average = lax.optimization_barrier(jnp.mean(values, axis=-1, keepdims=True))
    centred = values - average
    spread = lax.optimization_barrier(jnp.mean(centred * centred, axis=-1, keepdims=True))
    return centred * lax.rsqrt(spread + EPSILON) * gain_vec + shift_vec

def gelu(inputs):
    return 0.5 * inputs * (1.0 + jnp.tanh(GELU_COEF * (inputs + 0.044715 * inputs * inputs * inputs)))

def clip_forward(params, clip_rows, length):
    attn_gain, attn_shift, w_qkv, w_proj, mlp_gain, mlp_shift, w_up, w_down = params
    normed = low(layer_norm(clip_rows, attn_gain, attn_shift))
    mixed_qkv = low(low_back(matmul(normed, w_qkv)))
    queries = mixed_qkv[:, :D].reshape(SEQ, HEADS, HD)
    key_rows = mixed_qkv[:, D:2 * D].reshape(SEQ, HEADS, HD)
    values = mixed_qkv[:, 2 * D:].reshape(SEQ, HEADS, HD)
    key_pos = jnp.arange(SEQ, dtype=jnp.int32)
    span_rows = min(SEQ, 512)

    def attend(start):
        q_block = lax.dynamic_slice_in_dim(queries, start, span_rows, 0)
        scores = low_back(jnp.einsum('qhd,khd->hqk', q_block, key_rows, precision=HIGH) * 0.125)
        query_pos = start + jnp.arange(span_rows, dtype=jnp.int32)
        allowed = (key_pos[None, :] <= query_pos[:, None]) & (key_pos[None, :] < length)
        scores = jnp.where(allowed[None], scores, NEG_FILL)
        peak = lax.optimization_barrier(jnp.max(scores, axis=-1, keepdims=True))
        expo_vals = jnp.exp(scores - peak)
        probs_low = low(expo_vals / lax.optimization_barrier(jnp.sum(expo_vals, axis=-1, keepdims=True)))
        return jnp.einsum('hqk,khd->qhd', probs_low, values, precision=HIGH).reshape(span_rows, D)
    starts = jnp.arange(SEQ // span_rows, dtype=jnp.int32) * span_rows
    attended = lax.map(jax.checkpoint(attend), starts).reshape(SEQ, D)
    attended = low(low_back(attended))
    hidden = clip_rows + low_back(matmul(attended, w_proj))
    normed_two = low(layer_norm(hidden, mlp_gain, mlp_shift))
    gelu_out = low(gelu(low_back(matmul(normed_two, w_up))))
    return hidden + low_back(matmul(gelu_out, w_down))

def reference(tokens, attn_gain, attn_shift, w_qkv, w_proj, mlp_gain, mlp_shift, w_up, w_down, upstream, clip_length, dataset_group, sample_weight):
    params = (attn_gain.astype(jnp.float32), attn_shift.astype(jnp.float32), w_qkv.astype(jnp.float32), w_proj.astype(jnp.float32), mlp_gain.astype(jnp.float32), mlp_shift.astype(jnp.float32), w_up.astype(jnp.float32), w_down.astype(jnp.float32))
    clip_rows = tokens.astype(jnp.float32).reshape(CLIPS, SEQ, D)
    checked = jax.checkpoint(clip_forward)

    def forward(params, clip_rows):
        return lax.map(lambda item: checked(params, item[0], item[1]), (clip_rows, clip_length))
    outputs, pullback = jax.vjp(forward, params, clip_rows)
    onehot = (dataset_group[:, 0][:, None] == jnp.arange(NGROUPS, dtype=jnp.int32)[None, :]).astype(jnp.float32)
    counts = lax.optimization_barrier(jnp.sum(onehot * clip_length.astype(jnp.float32)[:, None], axis=0))
    total_all = jnp.sum(counts)
    clip_scale = sample_weight.astype(jnp.float32) * total_all / (NGROUPS * lax.optimization_barrier(jnp.sum(onehot * counts[None, :], axis=1)))
    slot_pos = jnp.arange(SEQ, dtype=jnp.int32)
    valid = slot_pos[None, :] < clip_length[:, None]
    scale = jnp.where(valid, clip_scale[:, None], 0.0)
    out_cot = upstream.astype(jnp.float32).reshape(CLIPS, SEQ, D) * scale[:, :, None]
    param_grads, row_grads = pullback(out_cot)
    return (outputs.reshape(TOKENS, D).astype(jnp.bfloat16), row_grads.reshape(TOKENS, D).astype(jnp.bfloat16), param_grads[0], param_grads[1], param_grads[2], param_grads[3], param_grads[4], param_grads[5], param_grads[6], param_grads[7])
```

```python
import jax
import jax.numpy as jnp
from jax import lax
from jax.experimental import pallas as pl
from jax.experimental.pallas import tpu as pltpu
from jax.sharding import PartitionSpec as P

HD = 64
NGROUPS = 4


EPSILON = 1e-05
NEG_FILL = -1e30
GELU_COEF = 0.7978845608028654


def layer_norm(values, gain_vec, shift_vec):
    average = jnp.mean(values, axis=-1, keepdims=True)
    centred = values - average
    spread = jnp.mean(centred * centred, axis=-1, keepdims=True)
    return centred * lax.rsqrt(spread + EPSILON) * gain_vec + shift_vec


def gelu(inputs):
    return (
        0.5 * inputs * (1.0 + jnp.tanh(GELU_COEF * (inputs + 0.044715 * inputs * inputs * inputs)))
    )


MESH = pl.DeviceIdType.MESH
BF16 = jnp.bfloat16
F32 = jnp.float32


def device_at(z, y, x, core):
    return (z * 2 + y, x * 2 + core)


def scatter_kernel(
    g_dn, g_up, g_pr, g_qk, vec, o_dn, o_up, o_pr, o_qk, o_vec,
    r1_dn, r1_up, r1_pr, r1_qk, s2_dn, s2_up, s2_pr, s2_qk, r2_dn, r2_up, r2_pr, r2_qk,
    s3_dn, s3_up, s3_pr, s3_qk, r3_dn, r3_up, r3_pr, r3_qk, f_dn, f_up, f_pr, f_qk,
    h_dn, h_up, h_pr, h_qk, vsend, vrecv, send_sem, recv_sem, vsend_sem, vrecv_sem,
):
    dp, ctx = lax.axis_index("dp"), lax.axis_index("ctx")
    z, y, x, core = dp // 2, dp % 2, ctx // 2, ctx % 2
    mate = device_at(z, y, x, 1 - core)
    x_peer = device_at(z, y, 1 - x, core)
    y_peer = device_at(z, 1 - y, x, core)
    z_peers = [device_at((z + d) % 4, y, x, core) for d in (1, 2, 3)]
    first = device_at(z, (y + core) % 2, (x + 1 - core) % 2, core)
    second = device_at(z, (y + 1 - core) % 2, (x + core) % 2, core)
    kept = jnp.where(core == 0, y, x)

    def block_index(zz, j):
        return zz * 4 + jnp.where(core == 0, j * 2 + x, y * 2 + j)

    peers = [mate, x_peer, y_peer] + z_peers
    barrier = pltpu.get_barrier_semaphore()
    for peer in peers:
        pl.semaphore_signal(barrier, inc=1, device_id=peer, device_id_type=MESH)
    pl.semaphore_wait(barrier, len(peers))

    grads = (g_dn, g_up, g_pr, g_qk)
    outs = (o_dn, o_up, o_pr, o_qk)
    r1s = (r1_dn, r1_up, r1_pr, r1_qk)
    s2s = (s2_dn, s2_up, s2_pr, s2_qk)
    r2s = (r2_dn, r2_up, r2_pr, r2_qk)
    s3s = (s3_dn, s3_up, s3_pr, s3_qk)
    r3s = (r3_dn, r3_up, r3_pr, r3_qk)
    fs = (f_dn, f_up, f_pr, f_qk)
    hs = (h_dn, h_up, h_pr, h_qk)

    def remote(src, dst, w, slot, target):
        return pltpu.make_async_remote_copy(
            src_ref=src, dst_ref=dst, send_sem=send_sem.at[w, slot], recv_sem=recv_sem.at[w, slot],
            device_id=target, device_id_type=MESH,
        )

    def first_copy(w):
        return [
            remote(
                g_half(w, zz, j), r1s[w].at[zz, j], w, zz * 2 + j, first
            )
            for zz in range(4)
            for j in range(2)
        ]

    def g_half(w, zz, j):
        index = zz * 4 + jnp.where(core == 0, j * 2 + 1 - x, (1 - y) * 2 + j)
        return grads[w].at[index]

    def second_copy(w):
        return remote(s2s[w], r2s[w], w, 8, second)

    def third_copy(w, d):
        return remote(s3s[w].at[d - 1], r3s[w].at[d - 1], w, 8 + d, z_peers[d - 1])

    def last_copy(w):
        width = hs[w].shape[1]
        columns = pl.ds(pl.multiple_of(core * width, 128), width)
        return remote(hs[w], outs[w].at[:, columns], w, 12, mate)

    def start_first(w):
        for copy in first_copy(w):
            copy.start()

    def start_second(w):
        for copy in first_copy(w):
            copy.wait()
        for zz in range(4):
            j = 1 - kept
            s2s[w][zz] = (
                grads[w][block_index(zz, j)].astype(F32) + r1s[w][zz, j].astype(F32)
            ).astype(BF16)
        second_copy(w).start()

    def total(w, zz):
        return (
            grads[w][block_index(zz, kept)].astype(F32)
            + r1s[w][zz, kept].astype(F32)
            + r2s[w][zz].astype(F32)
        )

    def start_third(w):
        second_copy(w).wait()
        for d in (1, 2, 3):
            s3s[w][d - 1] = total(w, (z + d) % 4).astype(BF16)
            third_copy(w, d).start()
        fs[w][...] = total(w, z)

    def start_last(w):
        for d in (1, 2, 3):
            third_copy(w, d).wait()
        rows, width = hs[w].shape
        mine, other = pl.multiple_of(core * rows, 8), pl.multiple_of((1 - core) * rows, 8)
        whole = (
            fs[w][...] + r3s[w][0].astype(F32) + r3s[w][1].astype(F32) + r3s[w][2].astype(F32)
        )
        fs[w][...] = whole
        hs[w][...] = fs[w][pl.ds(other, rows), :]
        last_copy(w).start()
        columns = pl.ds(pl.multiple_of(core * width, 128), width)
        outs[w][:, columns] = fs[w][pl.ds(mine, rows), :]

    def finish(w):
        last_copy(w).wait()

    def vector_copy(slot, target):
        return pltpu.make_async_remote_copy(
            src_ref=vsend.at[min(slot, 3)], dst_ref=vrecv.at[slot], send_sem=vsend_sem.at[slot],
            recv_sem=vrecv_sem.at[slot], device_id=target, device_id_type=MESH,
        )

    vsend[0] = vec[...]
    vector_copy(0, mate).start()
    for w in range(4):
        start_first(w)
    for slot, peer in ((0, mate), (1, x_peer), (2, y_peer)):
        vector_copy(slot, peer).wait()
        vsend[slot + 1] = vsend[slot] + vrecv[slot]
        if slot < 2:
            vector_copy(slot + 1, (mate, x_peer, y_peer)[slot + 1]).start()
    for d in (1, 2, 3):
        vector_copy(2 + d, z_peers[d - 1]).start()
    for w in range(4):
        start_second(w)
    for w in range(4):
        start_third(w)
    for d in (1, 2, 3):
        vector_copy(2 + d, z_peers[d - 1]).wait()
    o_vec[...] = vsend[3] + vrecv[3] + vrecv[4] + vrecv[5]
    for w in range(4):
        start_last(w)
    for w in range(4):
        finish(w)


def scatter_sums(down_half, up_half, proj_half, qkv_half, vectors):
    blocks = [(array.shape[1], array.shape[2]) for array in (down_half, up_half, proj_half, qkv_half)]
    vmem = pl.BlockSpec(memory_space=pltpu.VMEM)

    def per_block(lead, dtype):
        return [pltpu.VMEM(lead + block, dtype) for block in blocks]

    return pl.pallas_call(
        scatter_kernel,
        out_shape=[
            jax.ShapeDtypeStruct((rows // 2, width * 2), F32) for rows, width in blocks
        ] + [jax.ShapeDtypeStruct(vectors.shape, F32)],
        in_specs=[vmem] * 5,
        out_specs=[vmem] * 5,
        scratch_shapes=per_block((4, 2), BF16)
        + per_block((4,), BF16)
        + per_block((4,), BF16)
        + per_block((3,), BF16)
        + per_block((3,), BF16)
        + per_block((), F32)
        + [pltpu.VMEM((rows // 2, width), F32) for rows, width in blocks]
        + [
            pltpu.VMEM((4,) + vectors.shape, F32),
            pltpu.VMEM((6,) + vectors.shape, F32),
            pltpu.SemaphoreType.DMA((4, 13)),
            pltpu.SemaphoreType.DMA((4, 13)),
            pltpu.SemaphoreType.DMA((6,)),
            pltpu.SemaphoreType.DMA((6,)),
        ],
        compiler_params=pltpu.CompilerParams(
            collective_id=0, has_side_effects=True, vmem_limit_bytes=60 * 1024 * 1024
        ),
    )(down_half, up_half, proj_half, qkv_half, vectors)


def general_body(
    tokens,
    attn_gain,
    attn_shift,
    w_qkv,
    w_proj,
    mlp_gain,
    mlp_shift,
    w_up,
    w_down,
    upstream,
    clip_length,
    dataset_group,
    sample_weight,
):
    tok_rows = tokens.shape[0]
    model_width = tokens.shape[1]
    head_count = model_width // HD
    ctx_count = lax.axis_size("ctx")
    seq_rows = tok_rows * ctx_count
    first_row = lax.axis_index("ctx") * tok_rows
    length = clip_length[0]
    key_span = min(seq_rows, max(tok_rows, 512))
    block_count = seq_rows // key_span
    query_pos = first_row + jnp.arange(tok_rows, dtype=jnp.int32)
    last_pos = first_row + tok_rows - 1
    onehot = (dataset_group[0, 0] == jnp.arange(NGROUPS, dtype=jnp.int32)).astype(jnp.float32)
    counts = lax.psum(onehot * length.astype(jnp.float32), "dp")
    total_all = jnp.sum(counts)
    clip_scale = (
        sample_weight[0].astype(jnp.float32) * total_all / (NGROUPS * jnp.sum(onehot * counts))
    )
    x_rows = tokens.astype(jnp.float32)
    normed, norm_one_back = jax.vjp(layer_norm, x_rows, attn_gain, attn_shift)
    normed_low = normed.astype(jnp.bfloat16)
    mixed_qkv = jnp.dot(normed_low, w_qkv, preferred_element_type=jnp.float32).astype(jnp.bfloat16)
    queries = mixed_qkv[:, :model_width]
    key_local = mixed_qkv[:, model_width : 2 * model_width]
    value_local = mixed_qkv[:, 2 * model_width :]
    key_all, value_all = (
        lax.all_gather(key_local, "ctx", axis=0, tiled=True),
        lax.all_gather(value_local, "ctx", axis=0, tiled=True),
    )
    queries3 = queries.reshape(tok_rows, head_count, HD)

    def scores_for(kstart, key_rows):
        piece = key_rows[kstart : kstart + key_span].reshape(key_span, head_count, HD)
        raw = (
            jnp.einsum("qhd,khd->hqk", queries3, piece, preferred_element_type=jnp.float32) * 0.125
        )
        key_pos = kstart + jnp.arange(key_span, dtype=jnp.int32)
        allowed = (key_pos[None, :] <= query_pos[:, None]) & (key_pos[None, :] < length)
        return (jnp.where(allowed[None], raw, NEG_FILL), allowed)

    def useful(kstart):
        return (kstart <= last_pos) & (kstart < length)

    peak = jnp.full((head_count, tok_rows), NEG_FILL, jnp.float32)
    exp_total = jnp.zeros((head_count, tok_rows), jnp.float32)
    for index in range(block_count):
        kstart = index * key_span

        def gather_stats(carry, kstart=kstart):
            old_peak, old_total = carry
            scores, allowed = scores_for(kstart, key_all)
            new_peak = jnp.maximum(old_peak, jnp.max(scores, axis=-1))
            expo_vals = jnp.where(allowed[None], jnp.exp(scores - new_peak[..., None]), 0.0)
            return (
                new_peak,
                old_total * jnp.exp(old_peak - new_peak) + jnp.sum(expo_vals, axis=-1),
            )

        peak, exp_total = lax.cond(
            useful(kstart), gather_stats, lambda carry: carry, (peak, exp_total)
        )

    def probs_for(kstart, key_rows):
        scores, allowed = scores_for(kstart, key_rows)
        return (
            jnp.where(allowed[None], jnp.exp(scores - peak[..., None]), 0.0) / exp_total[..., None]
        )

    out_high = jnp.zeros((tok_rows, head_count, HD), jnp.float32)
    out_rest = jnp.zeros((tok_rows, head_count, HD), jnp.float32)
    for index in range(block_count):
        kstart = index * key_span

        def add_values(carry, kstart=kstart):
            high_acc, rest_acc = carry
            probs = probs_for(kstart, key_all)
            probs_low = probs.astype(jnp.bfloat16)
            remainder = (probs - probs_low.astype(jnp.float32)).astype(jnp.bfloat16)
            piece = value_all[kstart : kstart + key_span].reshape(key_span, head_count, HD)
            high_acc = high_acc + jnp.einsum(
                "hqk,khd->qhd", probs_low, piece, preferred_element_type=jnp.float32
            )
            rest_acc = rest_acc + jnp.einsum(
                "hqk,khd->qhd", remainder, piece, preferred_element_type=jnp.float32
            )
            return (high_acc, rest_acc)

        out_high, out_rest = lax.cond(
            useful(kstart), add_values, lambda carry: carry, (out_high, out_rest)
        )
    attended_low = out_high.reshape(tok_rows, model_width).astype(jnp.bfloat16)
    out_full = out_high + out_rest
    hidden = x_rows + jnp.dot(attended_low, w_proj, preferred_element_type=jnp.float32)
    normed_two, norm_two_back = jax.vjp(layer_norm, hidden, mlp_gain, mlp_shift)
    normed_two_low = normed_two.astype(jnp.bfloat16)
    up_proj = jnp.dot(normed_two_low, w_up, preferred_element_type=jnp.float32)
    gelu_vals, gelu_back = jax.vjp(gelu, up_proj)
    gelu_low = gelu_vals.astype(jnp.bfloat16)
    block_out = (hidden + jnp.dot(gelu_low, w_down, preferred_element_type=jnp.float32)).astype(
        jnp.bfloat16
    )
    valid = query_pos < length
    out_cot = upstream.astype(jnp.float32) * jnp.where(valid, clip_scale, 0.0)[:, None]
    out_cot_low = out_cot.astype(jnp.bfloat16)
    down_grad = jnp.einsum("tf,td->fd", gelu_low, out_cot_low, preferred_element_type=jnp.float32)
    gelu_in = jnp.einsum("td,fd->tf", out_cot_low, w_down, preferred_element_type=jnp.float32)
    (up_cot,) = gelu_back(gelu_in)
    up_cot_low = up_cot.astype(jnp.bfloat16)
    up_grad = jnp.einsum(
        "td,tf->df", normed_two_low, up_cot_low, preferred_element_type=jnp.float32
    )
    normed_two_cot = jnp.einsum("tf,df->td", up_cot_low, w_up, preferred_element_type=jnp.float32)
    norm_two_rows, mlp_gain_grad, mlp_shift_grad = norm_two_back(normed_two_cot)
    hidden_cot = out_cot + norm_two_rows
    hidden_cot_low = hidden_cot.astype(jnp.bfloat16)
    proj_grad = jnp.einsum(
        "ti,to->io", attended_low, hidden_cot_low, preferred_element_type=jnp.float32
    )
    attended_cot = jnp.einsum(
        "to,io->ti", hidden_cot_low, w_proj, preferred_element_type=jnp.float32
    ).astype(jnp.bfloat16)
    attended_cot3 = attended_cot.reshape(tok_rows, head_count, HD)
    delta = jnp.einsum("qhd,qhd->hq", attended_cot3.astype(jnp.float32), out_full)
    key_back, value_back = (key_all, value_all)
    query_cot = jnp.zeros((tok_rows, head_count, HD), jnp.float32)
    key_pieces = []
    value_pieces = []
    empty_piece = jnp.zeros((key_span, head_count, HD), jnp.float32)
    for index in range(block_count):
        kstart = index * key_span

        def block_grads(q_acc, kstart=kstart):
            probs = probs_for(kstart, key_back)
            probs_low = probs.astype(jnp.bfloat16)
            key_piece = key_back[kstart : kstart + key_span].reshape(key_span, head_count, HD)
            value_piece = value_back[kstart : kstart + key_span].reshape(key_span, head_count, HD)
            prob_cot = jnp.einsum(
                "qhd,khd->hqk", attended_cot3, value_piece, preferred_element_type=jnp.float32
            )
            score_cot = (probs * (prob_cot - delta[..., None])).astype(jnp.bfloat16)
            q_acc = (
                q_acc
                + jnp.einsum(
                    "hqk,khd->qhd", score_cot, key_piece, preferred_element_type=jnp.float32
                )
                * 0.125
            )
            key_term = (
                jnp.einsum("hqk,qhd->khd", score_cot, queries3, preferred_element_type=jnp.float32)
                * 0.125
            )
            value_term = jnp.einsum(
                "hqk,qhd->khd", probs_low, attended_cot3, preferred_element_type=jnp.float32
            )
            return (q_acc, key_term, value_term)

        query_cot, key_term, value_term = lax.cond(
            useful(kstart), block_grads, lambda q_acc: (q_acc, empty_piece, empty_piece), query_cot
        )
        key_pieces.append(key_term.reshape(key_span, model_width))
        value_pieces.append(value_term.reshape(key_span, model_width))
    key_terms = jnp.concatenate(key_pieces, axis=0)
    value_terms = jnp.concatenate(value_pieces, axis=0)
    key_cot, value_cot = (
        lax.psum_scatter(
            key_terms.astype(jnp.bfloat16), "ctx", scatter_dimension=0, tiled=True
        ).astype(jnp.float32),
        lax.psum_scatter(
            value_terms.astype(jnp.bfloat16), "ctx", scatter_dimension=0, tiled=True
        ).astype(jnp.float32),
    )
    mixed_cot = jnp.concatenate(
        [query_cot.reshape(tok_rows, model_width), key_cot, value_cot], axis=1
    ).astype(jnp.bfloat16)
    qkv_grad = jnp.einsum("td,te->de", normed_low, mixed_cot, preferred_element_type=jnp.float32)
    normed_cot = jnp.einsum("te,de->td", mixed_cot, w_qkv, preferred_element_type=jnp.float32)
    norm_one_rows, attn_gain_grad, attn_shift_grad = norm_one_back(normed_cot)
    input_grad = (hidden_cot + norm_one_rows).astype(jnp.bfloat16)
    reduced = (
        lax.psum_scatter(attn_gain_grad, ("dp", "ctx"), scatter_dimension=0, tiled=True),
        lax.psum_scatter(attn_shift_grad, ("dp", "ctx"), scatter_dimension=0, tiled=True),
        lax.psum_scatter(qkv_grad, ("dp", "ctx"), scatter_dimension=0, tiled=True),
        lax.psum_scatter(proj_grad, ("dp", "ctx"), scatter_dimension=0, tiled=True),
        lax.psum_scatter(mlp_gain_grad, ("dp", "ctx"), scatter_dimension=0, tiled=True),
        lax.psum_scatter(mlp_shift_grad, ("dp", "ctx"), scatter_dimension=0, tiled=True),
        lax.psum_scatter(up_grad, ("dp", "ctx"), scatter_dimension=0, tiled=True),
        lax.psum_scatter(down_grad, ("dp", "ctx"), scatter_dimension=0, tiled=True),
    )
    return (
        block_out,
        input_grad,
        reduced[0],
        reduced[1],
        reduced[2],
        reduced[3],
        reduced[4],
        reduced[5],
        reduced[6],
        reduced[7],
    )


def paired_body(
    tokens,
    attn_gain,
    attn_shift,
    w_qkv,
    w_proj,
    mlp_gain,
    mlp_shift,
    w_up,
    w_down,
    upstream,
    clip_length,
    dataset_group,
    sample_weight,
):
    tok_rows = tokens.shape[0]
    model_width = tokens.shape[1]
    head_count = model_width // HD
    ctx_count = lax.axis_size("ctx")
    seq_rows = tok_rows * ctx_count
    first_row = lax.axis_index("ctx") * tok_rows
    length = clip_length[0]
    key_span = min(seq_rows, max(tok_rows, 512))
    block_count = seq_rows // key_span
    query_pos = first_row + jnp.arange(tok_rows, dtype=jnp.int32)
    last_pos = first_row + tok_rows - 1
    onehot = (dataset_group[0, 0] == jnp.arange(NGROUPS, dtype=jnp.int32)).astype(jnp.float32)
    counts = lax.psum(onehot * length.astype(jnp.float32), "dp")
    total_all = jnp.sum(counts)
    clip_scale = (
        sample_weight[0].astype(jnp.float32) * total_all / (NGROUPS * jnp.sum(onehot * counts))
    )
    x_rows = tokens.astype(jnp.float32)
    normed, norm_one_back = jax.vjp(layer_norm, x_rows, attn_gain, attn_shift)
    normed_low = normed.astype(jnp.bfloat16)
    mixed_qkv = jnp.dot(normed_low, w_qkv, preferred_element_type=jnp.float32).astype(jnp.bfloat16)
    queries = mixed_qkv[:, :model_width]
    key_local = mixed_qkv[:, model_width : 2 * model_width]
    value_local = mixed_qkv[:, 2 * model_width :]
    key_all, value_all = (
        lax.all_gather(key_local, "ctx", axis=0, tiled=True),
        lax.all_gather(value_local, "ctx", axis=0, tiled=True),
    )
    queries3 = queries.reshape(tok_rows, head_count, HD)

    def scores_for(kstart, key_rows):
        piece = key_rows[kstart : kstart + key_span].reshape(key_span, head_count, HD)
        raw = (
            jnp.einsum("qhd,khd->hqk", queries3, piece, preferred_element_type=jnp.float32) * 0.125
        )
        key_pos = kstart + jnp.arange(key_span, dtype=jnp.int32)
        allowed = (key_pos[None, :] <= query_pos[:, None]) & (key_pos[None, :] < length)
        return (jnp.where(allowed[None], raw, NEG_FILL), allowed)

    def useful(kstart):
        return (kstart <= last_pos) & (kstart < length)

    peak = jnp.full((head_count, tok_rows), NEG_FILL, jnp.float32)
    exp_total = jnp.zeros((head_count, tok_rows), jnp.float32)
    for index in range(block_count):
        kstart = index * key_span

        def gather_stats(carry, kstart=kstart):
            old_peak, old_total = carry
            scores, allowed = scores_for(kstart, key_all)
            new_peak = jnp.maximum(old_peak, jnp.max(scores, axis=-1))
            expo_vals = jnp.where(allowed[None], jnp.exp(scores - new_peak[..., None]), 0.0)
            return (
                new_peak,
                old_total * jnp.exp(old_peak - new_peak) + jnp.sum(expo_vals, axis=-1),
            )

        peak, exp_total = lax.cond(
            useful(kstart), gather_stats, lambda carry: carry, (peak, exp_total)
        )

    def probs_for(kstart, key_rows):
        scores, allowed = scores_for(kstart, key_rows)
        return (
            jnp.where(allowed[None], jnp.exp(scores - peak[..., None]), 0.0) / exp_total[..., None]
        )

    out_high = jnp.zeros((tok_rows, head_count, HD), jnp.float32)
    out_rest = jnp.zeros((tok_rows, head_count, HD), jnp.float32)
    for index in range(block_count):
        kstart = index * key_span

        def add_values(carry, kstart=kstart):
            high_acc, rest_acc = carry
            probs = probs_for(kstart, key_all)
            probs_low = probs.astype(jnp.bfloat16)
            remainder = (probs - probs_low.astype(jnp.float32)).astype(jnp.bfloat16)
            piece = value_all[kstart : kstart + key_span].reshape(key_span, head_count, HD)
            high_acc = high_acc + jnp.einsum(
                "hqk,khd->qhd", probs_low, piece, preferred_element_type=jnp.float32
            )
            rest_acc = rest_acc + jnp.einsum(
                "hqk,khd->qhd", remainder, piece, preferred_element_type=jnp.float32
            )
            return (high_acc, rest_acc)

        out_high, out_rest = lax.cond(
            useful(kstart), add_values, lambda carry: carry, (out_high, out_rest)
        )
    attended_low = out_high.reshape(tok_rows, model_width).astype(jnp.bfloat16)
    out_full = out_high + out_rest
    hidden = x_rows + jnp.dot(attended_low, w_proj, preferred_element_type=jnp.float32)
    normed_two, norm_two_back = jax.vjp(layer_norm, hidden, mlp_gain, mlp_shift)
    normed_two_low = normed_two.astype(jnp.bfloat16)
    up_proj = jnp.dot(normed_two_low, w_up, preferred_element_type=jnp.float32)
    gelu_vals, gelu_back = jax.vjp(gelu, up_proj)
    gelu_low = gelu_vals.astype(jnp.bfloat16)
    block_out = (hidden + jnp.dot(gelu_low, w_down, preferred_element_type=jnp.float32)).astype(
        jnp.bfloat16
    )
    valid = query_pos < length
    out_cot = upstream.astype(jnp.float32) * jnp.where(valid, clip_scale, 0.0)[:, None]
    out_cot_low = out_cot.astype(jnp.bfloat16)
    gelu_in = jnp.einsum("td,fd->tf", out_cot_low, w_down, preferred_element_type=jnp.float32)
    (up_cot,) = gelu_back(gelu_in)
    up_cot_low = up_cot.astype(jnp.bfloat16)
    normed_two_cot = jnp.einsum("tf,df->td", up_cot_low, w_up, preferred_element_type=jnp.float32)
    norm_two_rows, mlp_gain_grad, mlp_shift_grad = norm_two_back(normed_two_cot)
    hidden_cot = out_cot + norm_two_rows
    hidden_cot_low = hidden_cot.astype(jnp.bfloat16)
    attended_cot = jnp.einsum(
        "to,io->ti", hidden_cot_low, w_proj, preferred_element_type=jnp.float32
    ).astype(jnp.bfloat16)
    attended_cot3 = attended_cot.reshape(tok_rows, head_count, HD)
    delta = jnp.einsum("qhd,qhd->hq", attended_cot3.astype(jnp.float32), out_full)
    key_back, value_back = (key_all, value_all)
    query_cot = jnp.zeros((tok_rows, head_count, HD), jnp.float32)
    key_pieces = []
    value_pieces = []
    empty_piece = jnp.zeros((key_span, head_count, HD), jnp.float32)
    for index in range(block_count):
        kstart = index * key_span

        def block_grads(q_acc, kstart=kstart):
            probs = probs_for(kstart, key_back)
            probs_low = probs.astype(jnp.bfloat16)
            key_piece = key_back[kstart : kstart + key_span].reshape(key_span, head_count, HD)
            value_piece = value_back[kstart : kstart + key_span].reshape(key_span, head_count, HD)
            prob_cot = jnp.einsum(
                "qhd,khd->hqk", attended_cot3, value_piece, preferred_element_type=jnp.float32
            )
            score_cot = (probs * (prob_cot - delta[..., None])).astype(jnp.bfloat16)
            q_acc = (
                q_acc
                + jnp.einsum(
                    "hqk,khd->qhd", score_cot, key_piece, preferred_element_type=jnp.float32
                )
                * 0.125
            )
            key_term = (
                jnp.einsum("hqk,qhd->khd", score_cot, queries3, preferred_element_type=jnp.float32)
                * 0.125
            )
            value_term = jnp.einsum(
                "hqk,qhd->khd", probs_low, attended_cot3, preferred_element_type=jnp.float32
            )
            return (q_acc, key_term, value_term)

        query_cot, key_term, value_term = lax.cond(
            useful(kstart), block_grads, lambda q_acc: (q_acc, empty_piece, empty_piece), query_cot
        )
        key_pieces.append(key_term.reshape(key_span, model_width))
        value_pieces.append(value_term.reshape(key_span, model_width))
    key_terms = jnp.concatenate(key_pieces, axis=0)
    value_terms = jnp.concatenate(value_pieces, axis=0)
    key_cot, value_cot = (
        lax.psum_scatter(
            key_terms.astype(jnp.bfloat16), "ctx", scatter_dimension=0, tiled=True
        ).astype(jnp.float32),
        lax.psum_scatter(
            value_terms.astype(jnp.bfloat16), "ctx", scatter_dimension=0, tiled=True
        ).astype(jnp.float32),
    )
    mixed_cot = jnp.concatenate(
        [query_cot.reshape(tok_rows, model_width), key_cot, value_cot], axis=1
    ).astype(jnp.bfloat16)
    normed_cot = jnp.einsum("te,de->td", mixed_cot, w_qkv, preferred_element_type=jnp.float32)
    norm_one_rows, attn_gain_grad, attn_shift_grad = norm_one_back(normed_cot)
    input_grad = (hidden_cot + norm_one_rows).astype(jnp.bfloat16)
    ctx_index = lax.axis_index("ctx")
    core = ctx_index % 2
    swap = [(i, i ^ 1) for i in range(ctx_count)]

    def halves(array):
        width = array.shape[1] // 2
        mine = lax.dynamic_slice_in_dim(array, core * width, width, 1)
        other = lax.dynamic_slice_in_dim(array, (1 - core) * width, width, 1)
        return mine, other

    out_mine, out_other = halves(out_cot_low)
    up_mine, up_other = halves(up_cot_low)
    hid_mine, hid_other = halves(hidden_cot_low)
    mix_mine, mix_other = halves(mixed_cot)
    packed = jnp.concatenate(
        [normed_low, normed_two_low, attended_low, gelu_low, out_other, up_other, hid_other, mix_other],
        axis=1,
    )
    arrived = lax.ppermute(packed, "ctx", swap)
    widths = (768, 768, 768, 3072, 384, 1536, 384, 1152)
    pieces = []
    at = 0
    for width in widths:
        pieces.append(arrived[:, at : at + width])
        at += width

    def weight_grad(left, left_far, right, right_far):
        both_left = jnp.concatenate([left, left_far], axis=0)
        both_right = jnp.concatenate([right, right_far], axis=0)
        return lax.dot_general(
            both_left, both_right, (((0,), (0,)), ((), ())), preferred_element_type=jnp.float32
        ).astype(jnp.bfloat16)

    down_half = weight_grad(gelu_low, pieces[3], out_mine, pieces[4]).reshape(16, 192, 384)
    up_half = weight_grad(normed_two_low, pieces[1], up_mine, pieces[5]).reshape(16, 48, 1536)
    proj_half = weight_grad(attended_low, pieces[2], hid_mine, pieces[6]).reshape(16, 48, 384)
    qkv_half = weight_grad(normed_low, pieces[0], mix_mine, pieces[7]).reshape(16, 48, 1152)
    zero_row = jnp.zeros((4, model_width), jnp.float32)
    vectors = jnp.concatenate(
        [jnp.stack([attn_gain_grad, attn_shift_grad, mlp_gain_grad, mlp_shift_grad]), zero_row]
    )
    down_grad, up_grad, proj_grad, qkv_grad, vector_sums = scatter_sums(
        down_half, up_half, proj_half, qkv_half, vectors
    )
    rank = lax.axis_index("dp") * ctx_count + ctx_index
    own = lax.dynamic_slice_in_dim(vector_sums, rank * 24, 24, 1)
    return (
        block_out,
        input_grad,
        own[0],
        own[1],
        qkv_grad,
        proj_grad,
        own[2],
        own[3],
        up_grad,
        down_grad,
    )


def solution(mesh):
    in_specs = (
        P(("dp", "ctx"), None),
        P(),
        P(),
        P(),
        P(),
        P(),
        P(),
        P(),
        P(),
        P(("dp", "ctx"), None),
        P("dp"),
        P("dp", None),
        P("dp"),
    )
    out_specs = (
        P(("dp", "ctx"), None),
        P(("dp", "ctx"), None),
        P(("dp", "ctx")),
        P(("dp", "ctx")),
        P(("dp", "ctx"), None),
        P(("dp", "ctx"), None),
        P(("dp", "ctx")),
        P(("dp", "ctx")),
        P(("dp", "ctx"), None),
        P(("dp", "ctx"), None),
    )
    paired = mesh.shape["dp"] == 8 and mesh.shape["ctx"] == 4
    body = paired_body if paired else general_body
    return jax.shard_map(body, mesh=mesh, in_specs=in_specs, out_specs=out_specs, check_vma=False)
```

```python
import jax
import jax.numpy as jnp
from jax import lax
from jax.experimental import pallas as pl
from jax.experimental.pallas import tpu as pltpu
from jax.sharding import PartitionSpec as P

HD = 64
NGROUPS = 4


EPSILON = 1e-05
NEG_FILL = -1e30
GELU_COEF = 0.7978845608028654


def layer_norm(values, gain_vec, shift_vec):
    average = jnp.mean(values, axis=-1, keepdims=True)
    centred = values - average
    spread = jnp.mean(centred * centred, axis=-1, keepdims=True)
    return centred * lax.rsqrt(spread + EPSILON) * gain_vec + shift_vec


def gelu(inputs):
    return (
        0.5 * inputs * (1.0 + jnp.tanh(GELU_COEF * (inputs + 0.044715 * inputs * inputs * inputs)))
    )


MESH = pl.DeviceIdType.MESH
BF16 = jnp.bfloat16
F32 = jnp.float32
ROWS = 256
WIDTH = 768
HIDDEN = 3072
HALF_HEADS = 6
HALF_WIDTH = 384
BLOCKS = ((192, 384), (48, 1536), (48, 384), (48, 1152))


def dot_nn(left, right):
    return lax.dot_general(left, right, (((1,), (0,)), ((), ())), preferred_element_type=F32)


def dot_nt(left, right):
    return lax.dot_general(left, right, (((1,), (1,)), ((), ())), preferred_element_type=F32)


def dot_tn(left, right):
    return lax.dot_general(left, right, (((0,), (0,)), ((), ())), preferred_element_type=F32)


def dot_tt(left, right):
    return lax.dot_general(left, right, (((0,), (1,)), ((), ())), preferred_element_type=F32)


def device_at(z, y, x, core):
    return (z * 2 + y, x * 2 + core)


def normalise(values):
    average = jnp.mean(values, axis=-1, keepdims=True)
    centred = values - average
    spread = jnp.mean(centred * centred, axis=-1, keepdims=True)
    inverse = lax.rsqrt(spread + EPSILON)
    return centred * inverse, inverse


def normalise_back(cot, gain, unit, inverse):
    scaled = cot * gain
    first = jnp.mean(scaled, axis=-1, keepdims=True)
    second = jnp.mean(scaled * unit, axis=-1, keepdims=True)
    return inverse * (scaled - first - unit * second)


def loop(count, step):
    def wrapped(index, carry):
        step(index)
        return carry

    lax.fori_loop(0, count, wrapped, 0)


def at(start, size, unit):
    return pl.ds(pl.multiple_of(start, unit), size)


def layer_kernel(
    length_ref, group_ref, weight_ref, tok, ups, gain1, shift1, gain2, shift2,
    w_qkv, w_proj, w_up, w_down,
    block_out, input_grad, o_v0, o_v1, o_qk, o_pr, o_v2, o_v3, o_up, o_dn,
    wq, wp, wu, wd, tokc, tokf, nc, nf, qkvt, kvft, bias, ec, ef, o1, m1, l1, f1, f2,
    attt, hid, n2, gel, dg, outl, outh, upo, uph, ncot, hc, hl, mixc, mixf,
    cs, cr, vsend, vrecv,
    g_dn, g_up, g_pr, g_qk,
    r1_dn, r1_up, r1_pr, r1_qk, s2_dn, s2_up, s2_pr, s2_qk, r2_dn, r2_up, r2_pr, r2_qk,
    s3_dn, s3_up, s3_pr, s3_qk, r3_dn, r3_up, r3_pr, r3_qk, f_dn, f_up, f_pr, f_qk,
    send_sem, recv_sem, misc_send, misc_recv, local_sem,
):
    dp, ctx = lax.axis_index("dp"), lax.axis_index("ctx")
    z, y, x, core = dp // 2, dp % 2, ctx // 2, ctx % 2
    mate = device_at(z, y, x, 1 - core)
    x_peer = device_at(z, y, 1 - x, core)
    y_peer = device_at(z, 1 - y, x, core)
    z_peers = [device_at((z + d) % 4, y, x, core) for d in (1, 2, 3)]
    own, oth = core * ROWS, (1 - core) * ROWS
    own_rows, oth_rows = at(own, ROWS, ROWS), at(oth, ROWS, ROWS)
    own_half, oth_half = at(core * HALF_WIDTH, HALF_WIDTH, 128), at((1 - core) * HALF_WIDTH, HALF_WIDTH, 128)
    length, group = length_ref[0], group_ref[0]
    left, right = x == 0, x == 1

    def fetch(slot, src, dst):
        return pltpu.make_async_copy(src, dst, local_sem.at[slot])

    def weight_copies(name):
        if name == "qkv":
            return [
                fetch(i, w_qkv.at[:, at(i * WIDTH + core * HALF_WIDTH, HALF_WIDTH, 128)],
                      wq.at[:, pl.ds(i * HALF_WIDTH, HALF_WIDTH)])
                for i in range(3)
            ]
        if name == "proj":
            return [fetch(3, w_proj, wp)]
        if name == "up":
            return [fetch(4, w_up, wu)]
        return [fetch(5, w_down, wd)]

    for name in ("qkv", "proj", "up", "down"):
        for copy in weight_copies(name):
            copy.start()

    def arrive(name):
        for copy in weight_copies(name):
            copy.wait()

    peers = [mate, x_peer, y_peer] + z_peers
    barrier = pltpu.get_barrier_semaphore()
    for peer in peers:
        pl.semaphore_signal(barrier, inc=1, device_id=peer, device_id_type=MESH)
    pl.semaphore_wait(barrier, len(peers))

    def misc(slot, src, dst, target):
        return pltpu.make_async_remote_copy(
            src_ref=src, dst_ref=dst, send_sem=misc_send.at[slot], recv_sem=misc_recv.at[slot],
            device_id=target, device_id_type=MESH,
        )

    tok_far = misc(0, tok, tokf.at[own_rows], x_peer)
    tok_mate = misc(1, tok, tokc.at[own_rows], mate)
    tok_on = misc(2, tokf.at[own_rows], tokf.at[own_rows], mate)
    ups_mate = misc(3, ups.at[:, oth_half], outh.at[own_rows], mate)
    count_y = misc(4, cs.at[0], cr.at[0], y_peer)
    count_z = [misc(4 + d, cs.at[1], cr.at[d], z_peers[d - 1]) for d in (1, 2, 3)]
    att_rows = at(core * HALF_WIDTH, HALF_WIDTH, 128)
    att_mate = misc(8, attt.at[att_rows], attt.at[att_rows], mate)
    n2_mate = misc(9, n2.at[own_rows], n2.at[own_rows], mate)
    gel_mate = [
        misc(10 + i, gel.at[own_rows, pl.ds(1024 * i, 1024)], gel.at[own_rows, pl.ds(1024 * i, 1024)], mate)
        for i in range(3)
    ]
    up_mate = misc(13, upo.at[:, at((1 - core) * 1536, 1536, 128)], uph.at[own_rows], mate)
    hl_mate = misc(14, hl.at[own_rows], hl.at[own_rows], mate)
    nc_mate = misc(15, tokc.at[own_rows], tokc.at[own_rows], mate)
    nf_mate = misc(16, tokf.at[own_rows], tokf.at[own_rows], mate)
    nf_far = misc(17, tokf.at[own_rows], tokf.at[own_rows], x_peer)

    @pl.when(left)
    def _():
        tok_far.start()

    tok_mate.start()
    ups_mate.start()
    lane = lax.broadcasted_iota(jnp.int32, (8, 128), 1)
    cs[0] = jnp.where(lane == group, length.astype(F32), 0.0)
    count_y.start()

    def first_norm(src, src_at, dst, dst_at):
        def step(i):
            unit, _ = normalise(src[at(src_at + i * 64, 64, 64), :].astype(F32))
            dst[at(dst_at + i * 64, 64, 64), :] = (unit * gain1[...] + shift1[...]).astype(BF16)

        loop(ROWS // 64, step)

    first_norm(tok, 0, nc, own)
    tok_mate.wait()
    first_norm(tokc, oth, nc, oth)
    arrive("qkv")

    def project(i):
        part = dot_tt(wq[:, at(i * HALF_WIDTH, HALF_WIDTH, 128)], nc[...])
        qkvt[at(i * HALF_WIDTH, HALF_WIDTH, 128), :] = (part * jnp.where(i == 0, 0.125, 1.0)).astype(BF16)

    loop(3, project)

    key_at = lax.broadcasted_iota(jnp.int32, (512, 512), 0)
    query_at = lax.broadcasted_iota(jnp.int32, (512, 512), 1)
    bias[...] = jnp.where((key_at <= query_at) & (key_at + x * 512 < length), 0.0, NEG_FILL).astype(BF16)

    def attend_chip(h):
        r = h * 64
        keys, queries, values = qkvt[at(HALF_WIDTH + r, 64, 64), :], qkvt[at(r, 64, 64), :], qkvt[at(2 * HALF_WIDTH + r, 64, 64), :]
        for half in (0, 1):
            span, cols = 256 * (half + 1), slice(256 * half, 256 * half + 256)
            scores = dot_tn(keys[:, :span], queries[:, cols]) + bias[:span, cols].astype(F32)
            peak = jnp.max(scores, axis=0, keepdims=True)
            expo = jnp.exp(scores - peak)
            expo_low = expo.astype(BF16)
            m1[pl.ds(h, 1), cols] = peak
            l1[pl.ds(h, 1), cols] = jnp.sum(expo_low.astype(F32), axis=0, keepdims=True)
            ec[h, :span, cols] = expo_low
            o1[at(r, 64, 64), cols] = dot_nn(values[:, :span], expo_low)

    loop(HALF_HEADS, attend_chip)

    count_y.wait()
    cs[1] = cs[0] + cr[0]
    for copy in count_z:
        copy.start()
    for copy in count_z:
        copy.wait()
    counts = cs[1] + cr[1] + cr[2] + cr[3]
    total = jnp.sum(counts, axis=1, keepdims=True)
    mine = jnp.sum(jnp.where(lane == group, counts, 0.0), axis=1, keepdims=True)
    scale = (weight_ref[0].astype(F32) * total / (NGROUPS * mine))[0:1, 0:1]
    row_at = lax.broadcasted_iota(jnp.int32, (ROWS, 1), 0) + x * 512
    own_scale = jnp.where(row_at + own < length, scale, 0.0)
    oth_scale = jnp.where(row_at + oth < length, scale, 0.0)
    outl[...] = (ups[...].astype(F32) * own_scale).astype(BF16)
    outh[own_rows, :] = (ups[:, own_half].astype(F32) * own_scale).astype(BF16)
    ups_mate.wait()
    outh[oth_rows, :] = (outh[oth_rows, :].astype(F32) * oth_scale).astype(BF16)

    @pl.when(right)
    def _():
        def far_block(start):
            first_norm(tokf, start, nf, start)
            columns = at(start, ROWS, ROWS)

            def project_far(i):
                part = dot_tt(wq[:, at((i + 1) * HALF_WIDTH, HALF_WIDTH, 128)], nf[columns, :])
                kvft[at(i * HALF_WIDTH, HALF_WIDTH, 128), columns] = part.astype(BF16)

            loop(2, project_far)

        tok_far.wait_recv()
        tok_on.start()
        far_block(own)
        tok_on.wait()
        far_block(oth)

        def attend_far(h):
            r = h * 64
            keys, queries, values = kvft[at(r, 64, 64), :], qkvt[at(r, 64, 64), :], kvft[at(HALF_WIDTH + r, 64, 64), :]
            for half in (0, 1):
                cols = slice(256 * half, 256 * half + 256)
                scores = dot_tn(keys, queries[:, cols])
                peak = jnp.max(scores, axis=0, keepdims=True)
                expo = jnp.exp(scores - peak)
                expo_low = expo.astype(BF16)
                expo_sum = jnp.sum(expo_low.astype(F32), axis=0, keepdims=True)
                ef[h, :, cols] = expo_low
                out = dot_nn(values, expo_low)
                old = m1[pl.ds(h, 1), cols]
                top = jnp.maximum(old, peak)
                old_part, new_part = jnp.exp(old - top), jnp.exp(peak - top)
                share = 1.0 / (l1[pl.ds(h, 1), cols] * old_part + expo_sum * new_part)
                f1[pl.ds(h, 1), cols] = old_part * share
                f2[pl.ds(h, 1), cols] = new_part * share
                o1[at(r, 64, 64), cols] = o1[at(r, 64, 64), cols] * (old_part * share) + out * (new_part * share)

        loop(HALF_HEADS, attend_far)

    @pl.when(left)
    def _():
        nf[...] = jnp.zeros_like(nf)
        mixf[...] = jnp.zeros_like(mixf)

        def share_out(h):
            share = 1.0 / l1[pl.ds(h, 1), :]
            f1[pl.ds(h, 1), :] = share
            f2[pl.ds(h, 1), :] = jnp.zeros_like(share)
            o1[at(h * 64, 64, 64), :] = o1[at(h * 64, 64, 64), :] * share

        loop(HALF_HEADS, share_out)

    attt[att_rows, :] = o1[...].astype(BF16)
    att_mate.start()
    arrive("proj")
    att_mate.wait()

    for i in range(3):
        cols = slice(256 * i, 256 * i + 256)
        hid[:, cols] = tok[:, cols].astype(F32) + dot_tn(attt[:, own_rows], wp[:, cols])

    def second_norm(i):
        unit, _ = normalise(hid[at(i * 64, 64, 64), :])
        n2[at(own + i * 64, 64, 64), :] = (unit * gain2[...] + shift2[...]).astype(BF16)

    loop(ROWS // 64, second_norm)
    n2_mate.start()
    arrive("up")
    for part in range(3):

        def feed(i, part=part):
            cols = at(part * 1024 + i * 256, 256, 256)
            u = dot_nn(n2[own_rows, :], wu[:, cols])
            square = u * u
            bend = jnp.tanh(GELU_COEF * (u + 0.044715 * square * u))
            lift = 0.5 * (1.0 + bend)
            gel[own_rows, cols] = (u * lift).astype(BF16)
            slope = lift + 0.5 * u * (1.0 - bend * bend) * (GELU_COEF * (1.0 + 3 * 0.044715 * square))
            dg[:, cols] = slope.astype(BF16)

        loop(4, feed)
        gel_mate[part].start()

    first = device_at(z, (y + core) % 2, (x + 1 - core) % 2, core)
    second = device_at(z, (y + 1 - core) % 2, (x + core) % 2, core)
    kept = jnp.where(core == 0, y, x)
    grads = (g_dn, g_up, g_pr, g_qk)
    outs = (o_dn, o_up, o_pr, o_qk)
    r1s, s2s, r2s = (r1_dn, r1_up, r1_pr, r1_qk), (s2_dn, s2_up, s2_pr, s2_qk), (r2_dn, r2_up, r2_pr, r2_qk)
    s3s, r3s = (s3_dn, s3_up, s3_pr, s3_qk), (r3_dn, r3_up, r3_pr, r3_qk)
    fs = (f_dn, f_up, f_pr, f_qk)

    def remote(src, dst, w, slot, target):
        return pltpu.make_async_remote_copy(
            src_ref=src, dst_ref=dst, send_sem=send_sem.at[w, slot], recv_sem=recv_sem.at[w, slot],
            device_id=target, device_id_type=MESH,
        )

    def block(w, index):
        rows = BLOCKS[w][0]
        return at(index * rows, rows, 16)

    def kept_block(w, zz, j):
        return grads[w][block(w, zz * 4 + jnp.where(core == 0, j * 2 + x, y * 2 + j)), :].astype(F32)

    def first_copy(w, zz, j):
        index = zz * 4 + jnp.where(core == 0, j * 2 + 1 - x, (1 - y) * 2 + j)
        return remote(grads[w].at[block(w, index)], r1s[w].at[zz, j], w, zz * 2 + j, first)

    def start_first(w, places):
        for zz in places:
            for j in range(2):
                first_copy(w, zz, j).start()

    def second_copy(w):
        return remote(s2s[w], r2s[w], w, 8, second)

    def third_copy(w, d):
        return remote(s3s[w].at[d - 1], r3s[w].at[d - 1], w, 8 + d, z_peers[d - 1])

    def places(w):
        parts = 3 if w == 3 else 1
        width = BLOCKS[w][1] // parts
        return [(pl.ds(i * width, width), at((2 * i + core) * width, width, 128)) for i in range(parts)]

    def last_copies(w):
        rows = BLOCKS[w][0] // 2
        far_rows = at((1 - core) * rows, rows, 8)
        return [
            remote(fs[w].at[far_rows, src], outs[w].at[:, dst], w, 12 + i, mate)
            for i, (src, dst) in enumerate(places(w))
        ]

    def start_second(w):
        for zz in range(4):
            for j in range(2):
                first_copy(w, zz, j).wait()
        j = 1 - kept
        for zz in range(4):
            s2s[w][zz] = (kept_block(w, zz, j) + r1s[w][zz, j].astype(F32)).astype(BF16)
        second_copy(w).start()

    def summed(w, zz):
        return kept_block(w, zz, kept) + r1s[w][zz, kept].astype(F32) + r2s[w][zz].astype(F32)

    def start_third(w):
        second_copy(w).wait()
        for d in (1, 2, 3):
            s3s[w][d - 1] = summed(w, (z + d) % 4).astype(BF16)
            third_copy(w, d).start()
        fs[w][...] = summed(w, z)

    def start_last(w):
        for d in (1, 2, 3):
            third_copy(w, d).wait()
        rows = BLOCKS[w][0] // 2
        fs[w][...] = fs[w][...] + r3s[w][0].astype(F32) + r3s[w][1].astype(F32) + r3s[w][2].astype(F32)
        for copy in last_copies(w):
            copy.start()
        for src, dst in places(w):
            outs[w][:, dst] = fs[w][at(core * rows, rows, 8), src]

    def finish(w):
        for copy in last_copies(w):
            copy.wait()

    for copy in gel_mate:
        copy.wait()
    for zz in range(4):

        def down_rows(i, zz=zz):
            start = zz * WIDTH + i * 256
            g_dn[at(start, 256, 256), :] = dot_tn(gel[:, at(start, 256, 256)], outh[...]).astype(BF16)

        loop(3, down_rows)
        start_first(0, (zz,))

    arrive("down")

    def gelu_back(cols):
        up_cot = dot_nt(outl[...], wd[cols, :]) * dg[:, cols].astype(F32)
        up_cot = up_cot.astype(BF16)
        upo[:, cols] = up_cot
        return up_cot

    def back_other(i):
        gelu_back(at((1 - core) * 1536 + i * 256, 256, 256))

    def back_own(i):
        uph[own_rows, at(i * 256, 256, 256)] = gelu_back(at(core * 1536 + i * 256, 256, 256))

    loop(6, back_other)
    up_mate.start()
    loop(6, back_own)

    def n2_back(i):
        cols = at(i * 256, 256, 256)
        ncot[:, cols] = dot_nt(upo[...], wu[cols, :])

    loop(3, n2_back)
    vsend[...] = jnp.zeros_like(vsend)

    def second_back(i):
        rows = at(i * 64, 64, 64)
        unit, inverse = normalise(hid[rows, :])
        cot = ncot[rows, :]
        position = lax.broadcasted_iota(jnp.int32, (64, 1), 0) + i * 64 + x * 512 + own
        out_cot = ups[rows, :].astype(F32) * jnp.where(position < length, scale, 0.0)
        hidden_cot = out_cot + normalise_back(cot, gain2[...], unit, inverse)
        hc[rows, :] = hidden_cot
        hl[at(own + i * 64, 64, 64), :] = hidden_cot.astype(BF16)
        vsend[0, 2:3, :] += jnp.sum(cot * unit, axis=0, keepdims=True)
        vsend[0, 3:4, :] += jnp.sum(cot, axis=0, keepdims=True)

    loop(ROWS // 64, second_back)
    hl_mate.start()

    n2_mate.wait()
    up_mate.wait()
    for part in range(2):

        def up_columns(i, part=part):
            cols = at(i * 512, 512, 512)
            g_up[384 * part : 384 * part + 384, cols] = dot_tn(n2[:, 384 * part : 384 * part + 384], uph[:, cols]).astype(BF16)

        loop(3, up_columns)
        start_first(1, (2 * part, 2 * part + 1))

    hl_mate.wait()

    def proj_rows(i):
        rows = at(i * 256, 256, 256)
        g_pr[rows, :] = dot_nn(attt[rows, :], hl[:, own_half]).astype(BF16)

    loop(3, proj_rows)
    start_first(2, range(4))
    attt[att_rows, :] = dot_nt(wp[att_rows, :], hl[...]).astype(BF16)

    def attend_back(h):
        r = h * 64
        rows = at(r, 64, 64)
        keys, queries, values = qkvt[at(HALF_WIDTH + r, 64, 64), :], qkvt[rows, :], qkvt[at(2 * HALF_WIDTH + r, 64, 64), :]
        cot = attt[at(core * HALF_WIDTH + r, 64, 64), :].astype(F32)
        near = (cot * f1[pl.ds(h, 1), :]).astype(BF16)
        delta = jnp.sum(near.astype(F32) * o1[rows, :], axis=0, keepdims=True)
        far = (cot * f2[pl.ds(h, 1), :]).astype(BF16)
        far_delta = jnp.sum(far.astype(F32) * o1[rows, :], axis=0, keepdims=True)
        key_terms, value_terms = [], []
        for half in (0, 1):
            span, cols = 256 * (half + 1), slice(256 * half, 256 * half + 256)
            expo = ec[h, :span, cols]
            prob_cot = dot_tn(values[:, :span], near[:, cols])
            score_cot = (expo.astype(F32) * (prob_cot - delta[:, cols])).astype(BF16)
            o1[rows, cols] = dot_nn(keys[:, :span], score_cot)
            key_terms.append(dot_nt(queries[:, cols], score_cot))
            value_terms.append(dot_nt(near[:, cols], expo))
        for start, terms in ((HALF_WIDTH, key_terms), (2 * HALF_WIDTH, value_terms)):
            mixc[at(start + r, 64, 64), :256] = (terms[0] + terms[1][:, :256]).astype(BF16)
            mixc[at(start + r, 64, 64), 256:] = terms[1][:, 256:].astype(BF16)

        @pl.when(right)
        def _():
            far_keys, far_values = kvft[rows, :], kvft[at(HALF_WIDTH + r, 64, 64), :]
            expo = ef[h]
            prob_cot = dot_tn(far_values, far)
            score_cot = (expo.astype(F32) * (prob_cot - far_delta)).astype(BF16)
            o1[rows, :] += dot_nn(far_keys, score_cot)
            mixf[rows, :] = dot_nt(queries, score_cot).astype(BF16)
            mixf[at(HALF_WIDTH + r, 64, 64), :] = dot_nt(far, expo).astype(BF16)

        mixc[rows, :] = (o1[rows, :] * 0.125).astype(BF16)

    def attend_back_late(h):
        attend_back(h + 3)

    loop(3, attend_back)
    start_second(0)
    loop(3, attend_back_late)
    start_second(1)

    def normed_cot(mixed, first_column, columns, store):
        def step(i):
            rows = at(i * 256, 256, 256)
            store(rows, dot_tt(mixed[:, columns], wq[rows, first_column:]))

        loop(3, step)

    def store_to(ref, rows):
        def store(cols, value):
            ref[rows, cols] = value.astype(ref.dtype)

        return store

    @pl.when(right)
    def _():
        normed_cot(mixf, HALF_WIDTH, oth_rows, store_to(tokf, own_rows))
        nf_mate.start()

    normed_cot(mixc, 0, oth_rows, store_to(tokc, own_rows))
    nc_mate.start()

    @pl.when(right)
    def _():
        normed_cot(mixf, HALF_WIDTH, own_rows, store_to(ncot, at(0, ROWS, ROWS)))
        nf_mate.wait()
        tokf[own_rows, :] = (ncot[...] + tokf[oth_rows, :].astype(F32)).astype(BF16)
        nf_far.start()

    for part in range(2):
        cols = slice(384 * part, 384 * part + 384)
        g_qk[cols, :384] = dot_tt(nc[:, cols], mixc[:384, :]).astype(BF16)
        for i in range(2):
            g_qk[cols, 384 * (i + 1) : 384 * (i + 2)] = (
                dot_tt(nc[:, cols], mixc[384 * (i + 1) : 384 * (i + 2), :])
                + dot_tt(nf[:, cols], mixf[384 * i : 384 * (i + 1), :])
            ).astype(BF16)
        start_first(3, (2 * part, 2 * part + 1))

    normed_cot(mixc, 0, own_rows, store_to(ncot, at(0, ROWS, ROWS)))
    start_third(0)
    start_second(2)

    def block_rows(i):
        cols = at(i * 256, 256, 256)
        block_out[:, cols] = (hid[:, cols] + dot_nn(gel[own_rows, :], wd[:, cols])).astype(BF16)

    loop(3, block_rows)
    nc_mate.wait()

    @pl.when(left)
    def _():
        nf_far.wait_recv()
        tok_far.wait_send()

    @pl.when(right)
    def _():
        nf_far.wait_send()

    def first_back(i):
        rows = at(i * 64, 64, 64)
        unit, inverse = normalise(tok[rows, :].astype(F32))
        near = tokc[at(oth + i * 64, 64, 64), :].astype(F32)
        far = tokf[at(own + i * 64, 64, 64), :].astype(F32)
        cot = ncot[rows, :] + near + jnp.where(left, far, 0.0)
        input_grad[rows, :] = (hc[rows, :] + normalise_back(cot, gain1[...], unit, inverse)).astype(BF16)
        vsend[0, 0:1, :] += jnp.sum(cot * unit, axis=0, keepdims=True)
        vsend[0, 1:2, :] += jnp.sum(cot, axis=0, keepdims=True)

    loop(ROWS // 64, first_back)

    def vector_copy(slot, target):
        return misc(18 + slot, vsend.at[min(slot, 3)], vrecv.at[slot], target)

    vector_copy(0, mate).start()
    start_third(1)
    vector_copy(0, mate).wait()
    vsend[1] = vsend[0] + vrecv[0]
    vector_copy(1, x_peer).start()
    start_second(3)
    vector_copy(1, x_peer).wait()
    vsend[2] = vsend[1] + vrecv[1]
    vector_copy(2, y_peer).start()
    start_last(0)
    start_third(2)
    vector_copy(2, y_peer).wait()
    vsend[3] = vsend[2] + vrecv[2]
    for d in (1, 2, 3):
        vector_copy(2 + d, z_peers[d - 1]).start()
    start_last(1)
    start_third(3)
    for d in (1, 2, 3):
        vector_copy(2 + d, z_peers[d - 1]).wait()
    sums = vsend[3] + vrecv[3] + vrecv[4] + vrecv[5]
    rank = dp * 4 + ctx
    sums = pltpu.roll(sums, lax.rem(WIDTH - rank * 24, WIDTH), 1)
    for i, ref in enumerate((o_v0, o_v1, o_v2, o_v3)):
        ref[...] = sums[i : i + 1, :128]
    start_last(2)
    start_last(3)
    for w in range(4):
        finish(w)


def fused_layer(args):
    vmem, smem, anywhere = (
        pl.BlockSpec(memory_space=pltpu.VMEM),
        pl.BlockSpec(memory_space=pltpu.SMEM),
        pl.BlockSpec(memory_space=pl.ANY),
    )

    def low(*shape):
        return pltpu.VMEM(shape, BF16)

    def full(*shape):
        return pltpu.VMEM(shape, F32)

    def per_block(lead):
        return [pltpu.VMEM(lead + block, BF16) for block in BLOCKS]

    vector = jax.ShapeDtypeStruct((1, 128), F32)

    def grad_shape(w):
        return jax.ShapeDtypeStruct((BLOCKS[w][0] // 2, BLOCKS[w][1] * 2), F32)

    rows_out = jax.ShapeDtypeStruct((ROWS, WIDTH), BF16)
    return pl.pallas_call(
        layer_kernel,
        out_shape=[
            rows_out, rows_out, vector, vector, grad_shape(3), grad_shape(2), vector, vector,
            grad_shape(1), grad_shape(0),
        ],
        in_specs=[smem] * 3 + [vmem] * 6 + [anywhere] * 4,
        out_specs=[vmem] * 10,
        scratch_shapes=[
            low(768, 1152), low(768, 768), low(768, 3072), low(3072, 768),
            low(512, 768), low(512, 768), low(512, 768), low(512, 768),
            low(1152, 512), low(768, 512), low(512, 512), low(6, 512, 512), low(6, 512, 512),
            full(384, 512), full(8, 512), full(8, 512), full(8, 512), full(8, 512),
            low(768, 512), full(256, 768), low(512, 768), low(512, 3072), low(256, 3072),
            low(256, 768), low(512, 384), low(256, 3072), low(512, 1536), full(256, 768),
            full(256, 768), low(512, 768), low(1152, 512), low(768, 512),
            full(2, 8, 128), full(4, 8, 128), full(4, 8, 768), full(6, 8, 768),
            low(3072, 384), low(768, 1536), low(768, 384), low(768, 1152),
        ]
        + per_block((4, 2)) + per_block((4,)) + per_block((4,)) + per_block((3,)) + per_block((3,))
        + [pltpu.VMEM(block, F32) for block in BLOCKS]
        + [
            pltpu.SemaphoreType.DMA((4, 15)),
            pltpu.SemaphoreType.DMA((4, 15)),
            pltpu.SemaphoreType.DMA((24,)),
            pltpu.SemaphoreType.DMA((24,)),
            pltpu.SemaphoreType.DMA((6,)),
        ],
        compiler_params=pltpu.CompilerParams(
            collective_id=0, has_side_effects=True, vmem_limit_bytes=60 * 1024 * 1024
        ),
    )(*args)


def general_body(
    tokens,
    attn_gain,
    attn_shift,
    w_qkv,
    w_proj,
    mlp_gain,
    mlp_shift,
    w_up,
    w_down,
    upstream,
    clip_length,
    dataset_group,
    sample_weight,
):
    tok_rows = tokens.shape[0]
    model_width = tokens.shape[1]
    head_count = model_width // HD
    ctx_count = lax.axis_size("ctx")
    seq_rows = tok_rows * ctx_count
    first_row = lax.axis_index("ctx") * tok_rows
    length = clip_length[0]
    key_span = min(seq_rows, max(tok_rows, 512))
    block_count = seq_rows // key_span
    query_pos = first_row + jnp.arange(tok_rows, dtype=jnp.int32)
    last_pos = first_row + tok_rows - 1
    onehot = (dataset_group[0, 0] == jnp.arange(NGROUPS, dtype=jnp.int32)).astype(jnp.float32)
    counts = lax.psum(onehot * length.astype(jnp.float32), "dp")
    total_all = jnp.sum(counts)
    clip_scale = (
        sample_weight[0].astype(jnp.float32) * total_all / (NGROUPS * jnp.sum(onehot * counts))
    )
    x_rows = tokens.astype(jnp.float32)
    normed, norm_one_back = jax.vjp(layer_norm, x_rows, attn_gain, attn_shift)
    normed_low = normed.astype(jnp.bfloat16)
    mixed_qkv = jnp.dot(normed_low, w_qkv, preferred_element_type=jnp.float32).astype(jnp.bfloat16)
    queries = mixed_qkv[:, :model_width]
    key_local = mixed_qkv[:, model_width : 2 * model_width]
    value_local = mixed_qkv[:, 2 * model_width :]
    key_all, value_all = (
        lax.all_gather(key_local, "ctx", axis=0, tiled=True),
        lax.all_gather(value_local, "ctx", axis=0, tiled=True),
    )
    queries3 = queries.reshape(tok_rows, head_count, HD)

    def scores_for(kstart, key_rows):
        piece = key_rows[kstart : kstart + key_span].reshape(key_span, head_count, HD)
        raw = (
            jnp.einsum("qhd,khd->hqk", queries3, piece, preferred_element_type=jnp.float32) * 0.125
        )
        key_pos = kstart + jnp.arange(key_span, dtype=jnp.int32)
        allowed = (key_pos[None, :] <= query_pos[:, None]) & (key_pos[None, :] < length)
        return (jnp.where(allowed[None], raw, NEG_FILL), allowed)

    def useful(kstart):
        return (kstart <= last_pos) & (kstart < length)

    peak = jnp.full((head_count, tok_rows), NEG_FILL, jnp.float32)
    exp_total = jnp.zeros((head_count, tok_rows), jnp.float32)
    for index in range(block_count):
        kstart = index * key_span

        def gather_stats(carry, kstart=kstart):
            old_peak, old_total = carry
            scores, allowed = scores_for(kstart, key_all)
            new_peak = jnp.maximum(old_peak, jnp.max(scores, axis=-1))
            expo_vals = jnp.where(allowed[None], jnp.exp(scores - new_peak[..., None]), 0.0)
            return (
                new_peak,
                old_total * jnp.exp(old_peak - new_peak) + jnp.sum(expo_vals, axis=-1),
            )

        peak, exp_total = lax.cond(
            useful(kstart), gather_stats, lambda carry: carry, (peak, exp_total)
        )

    def probs_for(kstart, key_rows):
        scores, allowed = scores_for(kstart, key_rows)
        return (
            jnp.where(allowed[None], jnp.exp(scores - peak[..., None]), 0.0) / exp_total[..., None]
        )

    out_high = jnp.zeros((tok_rows, head_count, HD), jnp.float32)
    out_rest = jnp.zeros((tok_rows, head_count, HD), jnp.float32)
    for index in range(block_count):
        kstart = index * key_span

        def add_values(carry, kstart=kstart):
            high_acc, rest_acc = carry
            probs = probs_for(kstart, key_all)
            probs_low = probs.astype(jnp.bfloat16)
            remainder = (probs - probs_low.astype(jnp.float32)).astype(jnp.bfloat16)
            piece = value_all[kstart : kstart + key_span].reshape(key_span, head_count, HD)
            high_acc = high_acc + jnp.einsum(
                "hqk,khd->qhd", probs_low, piece, preferred_element_type=jnp.float32
            )
            rest_acc = rest_acc + jnp.einsum(
                "hqk,khd->qhd", remainder, piece, preferred_element_type=jnp.float32
            )
            return (high_acc, rest_acc)

        out_high, out_rest = lax.cond(
            useful(kstart), add_values, lambda carry: carry, (out_high, out_rest)
        )
    attended_low = out_high.reshape(tok_rows, model_width).astype(jnp.bfloat16)
    out_full = out_high + out_rest
    hidden = x_rows + jnp.dot(attended_low, w_proj, preferred_element_type=jnp.float32)
    normed_two, norm_two_back = jax.vjp(layer_norm, hidden, mlp_gain, mlp_shift)
    normed_two_low = normed_two.astype(jnp.bfloat16)
    up_proj = jnp.dot(normed_two_low, w_up, preferred_element_type=jnp.float32)
    gelu_vals, gelu_back = jax.vjp(gelu, up_proj)
    gelu_low = gelu_vals.astype(jnp.bfloat16)
    block_out = (hidden + jnp.dot(gelu_low, w_down, preferred_element_type=jnp.float32)).astype(
        jnp.bfloat16
    )
    valid = query_pos < length
    out_cot = upstream.astype(jnp.float32) * jnp.where(valid, clip_scale, 0.0)[:, None]
    out_cot_low = out_cot.astype(jnp.bfloat16)
    down_grad = jnp.einsum("tf,td->fd", gelu_low, out_cot_low, preferred_element_type=jnp.float32)
    gelu_in = jnp.einsum("td,fd->tf", out_cot_low, w_down, preferred_element_type=jnp.float32)
    (up_cot,) = gelu_back(gelu_in)
    up_cot_low = up_cot.astype(jnp.bfloat16)
    up_grad = jnp.einsum(
        "td,tf->df", normed_two_low, up_cot_low, preferred_element_type=jnp.float32
    )
    normed_two_cot = jnp.einsum("tf,df->td", up_cot_low, w_up, preferred_element_type=jnp.float32)
    norm_two_rows, mlp_gain_grad, mlp_shift_grad = norm_two_back(normed_two_cot)
    hidden_cot = out_cot + norm_two_rows
    hidden_cot_low = hidden_cot.astype(jnp.bfloat16)
    proj_grad = jnp.einsum(
        "ti,to->io", attended_low, hidden_cot_low, preferred_element_type=jnp.float32
    )
    attended_cot = jnp.einsum(
        "to,io->ti", hidden_cot_low, w_proj, preferred_element_type=jnp.float32
    ).astype(jnp.bfloat16)
    attended_cot3 = attended_cot.reshape(tok_rows, head_count, HD)
    delta = jnp.einsum("qhd,qhd->hq", attended_cot3.astype(jnp.float32), out_full)
    key_back, value_back = (key_all, value_all)
    query_cot = jnp.zeros((tok_rows, head_count, HD), jnp.float32)
    key_pieces = []
    value_pieces = []
    empty_piece = jnp.zeros((key_span, head_count, HD), jnp.float32)
    for index in range(block_count):
        kstart = index * key_span

        def block_grads(q_acc, kstart=kstart):
            probs = probs_for(kstart, key_back)
            probs_low = probs.astype(jnp.bfloat16)
            key_piece = key_back[kstart : kstart + key_span].reshape(key_span, head_count, HD)
            value_piece = value_back[kstart : kstart + key_span].reshape(key_span, head_count, HD)
            prob_cot = jnp.einsum(
                "qhd,khd->hqk", attended_cot3, value_piece, preferred_element_type=jnp.float32
            )
            score_cot = (probs * (prob_cot - delta[..., None])).astype(jnp.bfloat16)
            q_acc = (
                q_acc
                + jnp.einsum(
                    "hqk,khd->qhd", score_cot, key_piece, preferred_element_type=jnp.float32
                )
                * 0.125
            )
            key_term = (
                jnp.einsum("hqk,qhd->khd", score_cot, queries3, preferred_element_type=jnp.float32)
                * 0.125
            )
            value_term = jnp.einsum(
                "hqk,qhd->khd", probs_low, attended_cot3, preferred_element_type=jnp.float32
            )
            return (q_acc, key_term, value_term)

        query_cot, key_term, value_term = lax.cond(
            useful(kstart), block_grads, lambda q_acc: (q_acc, empty_piece, empty_piece), query_cot
        )
        key_pieces.append(key_term.reshape(key_span, model_width))
        value_pieces.append(value_term.reshape(key_span, model_width))
    key_terms = jnp.concatenate(key_pieces, axis=0)
    value_terms = jnp.concatenate(value_pieces, axis=0)
    key_cot, value_cot = (
        lax.psum_scatter(
            key_terms.astype(jnp.bfloat16), "ctx", scatter_dimension=0, tiled=True
        ).astype(jnp.float32),
        lax.psum_scatter(
            value_terms.astype(jnp.bfloat16), "ctx", scatter_dimension=0, tiled=True
        ).astype(jnp.float32),
    )
    mixed_cot = jnp.concatenate(
        [query_cot.reshape(tok_rows, model_width), key_cot, value_cot], axis=1
    ).astype(jnp.bfloat16)
    qkv_grad = jnp.einsum("td,te->de", normed_low, mixed_cot, preferred_element_type=jnp.float32)
    normed_cot = jnp.einsum("te,de->td", mixed_cot, w_qkv, preferred_element_type=jnp.float32)
    norm_one_rows, attn_gain_grad, attn_shift_grad = norm_one_back(normed_cot)
    input_grad = (hidden_cot + norm_one_rows).astype(jnp.bfloat16)
    reduced = (
        lax.psum_scatter(attn_gain_grad, ("dp", "ctx"), scatter_dimension=0, tiled=True),
        lax.psum_scatter(attn_shift_grad, ("dp", "ctx"), scatter_dimension=0, tiled=True),
        lax.psum_scatter(qkv_grad, ("dp", "ctx"), scatter_dimension=0, tiled=True),
        lax.psum_scatter(proj_grad, ("dp", "ctx"), scatter_dimension=0, tiled=True),
        lax.psum_scatter(mlp_gain_grad, ("dp", "ctx"), scatter_dimension=0, tiled=True),
        lax.psum_scatter(mlp_shift_grad, ("dp", "ctx"), scatter_dimension=0, tiled=True),
        lax.psum_scatter(up_grad, ("dp", "ctx"), scatter_dimension=0, tiled=True),
        lax.psum_scatter(down_grad, ("dp", "ctx"), scatter_dimension=0, tiled=True),
    )
    return (
        block_out,
        input_grad,
        reduced[0],
        reduced[1],
        reduced[2],
        reduced[3],
        reduced[4],
        reduced[5],
        reduced[6],
        reduced[7],
    )


def fused_body(
    tokens, attn_gain, attn_shift, w_qkv, w_proj, mlp_gain, mlp_shift, w_up, w_down, upstream,
    clip_length, dataset_group, sample_weight,
):
    rows = [array.reshape(1, WIDTH) for array in (attn_gain, attn_shift, mlp_gain, mlp_shift)]
    outs = fused_layer(
        [clip_length, dataset_group.reshape(1), sample_weight, tokens, upstream]
        + rows
        + [w_qkv, w_proj, w_up, w_down]
    )
    return tuple(out[0, :24] if out.shape == (1, 128) else out for out in outs)


def solution(mesh):
    in_specs = (
        P(("dp", "ctx"), None),
        P(),
        P(),
        P(),
        P(),
        P(),
        P(),
        P(),
        P(),
        P(("dp", "ctx"), None),
        P("dp"),
        P("dp", None),
        P("dp"),
    )
    out_specs = (
        P(("dp", "ctx"), None),
        P(("dp", "ctx"), None),
        P(("dp", "ctx")),
        P(("dp", "ctx")),
        P(("dp", "ctx"), None),
        P(("dp", "ctx"), None),
        P(("dp", "ctx")),
        P(("dp", "ctx")),
        P(("dp", "ctx"), None),
        P(("dp", "ctx"), None),
    )
    fused = mesh.shape["dp"] == 8 and mesh.shape["ctx"] == 4
    body = fused_body if fused else general_body
    return jax.shard_map(body, mesh=mesh, in_specs=in_specs, out_specs=out_specs, check_vma=False)
```

```python
import jax
import jax.numpy as jnp
from jax import lax
from jax.experimental import pallas as pl
from jax.experimental.pallas import tpu as pltpu
from jax.sharding import PartitionSpec as P

HD = 64
NGROUPS = 4


EPSILON = 1e-05
NEG_FILL = -1e30
GELU_COEF = 0.7978845608028654


def layer_norm(values, gain_vec, shift_vec):
    average = jnp.mean(values, axis=-1, keepdims=True)
    centred = values - average
    spread = jnp.mean(centred * centred, axis=-1, keepdims=True)
    return centred * lax.rsqrt(spread + EPSILON) * gain_vec + shift_vec


def gelu(inputs):
    return (
        0.5 * inputs * (1.0 + jnp.tanh(GELU_COEF * (inputs + 0.044715 * inputs * inputs * inputs)))
    )


MESH = pl.DeviceIdType.MESH
BF16 = jnp.bfloat16
F32 = jnp.float32
ROWS = 256
WIDTH = 768
HIDDEN = 3072
HALF_HEADS = 6
HALF_WIDTH = 384
BLOCKS = ((192, 384), (48, 1536), (48, 384), (48, 1152))


def dot_nn(left, right):
    return lax.dot_general(left, right, (((1,), (0,)), ((), ())), preferred_element_type=F32)


def dot_nt(left, right):
    return lax.dot_general(left, right, (((1,), (1,)), ((), ())), preferred_element_type=F32)


def dot_tn(left, right):
    return lax.dot_general(left, right, (((0,), (0,)), ((), ())), preferred_element_type=F32)


def dot_tt(left, right):
    return lax.dot_general(left, right, (((0,), (1,)), ((), ())), preferred_element_type=F32)


def device_at(z, y, x, core):
    return (z * 2 + y, x * 2 + core)


def normalise(values):
    average = jnp.mean(values, axis=-1, keepdims=True)
    centred = values - average
    spread = jnp.mean(centred * centred, axis=-1, keepdims=True)
    inverse = lax.rsqrt(spread + EPSILON)
    return centred * inverse, inverse


def normalise_back(cot, gain, unit, inverse):
    scaled = cot * gain
    first = jnp.mean(scaled, axis=-1, keepdims=True)
    second = jnp.mean(scaled * unit, axis=-1, keepdims=True)
    return inverse * (scaled - first - unit * second)


def loop(count, step):
    def wrapped(index, carry):
        step(index)
        return carry

    lax.fori_loop(0, count, wrapped, 0)


def at(start, size, unit):
    return pl.ds(pl.multiple_of(start, unit), size)


def layer_kernel(
    length_ref, group_ref, weight_ref, tok, ups, gain1_ref, shift1_ref, gain2_ref, shift2_ref,
    w_qkv, w_proj, w_up, w_down,
    block_out, input_grad, o_qk, o_pr, o_up, o_dn, o_vec,
    wq, wp, wu, wd, tokc, tokf, nc, nf, qkvt, kvft, bias, ec, ef, o1, m1, l1, f1, f2,
    attt, hid, n2, gel, dg, outl, outh, upo, uph, ncot, hc, hl, mixc, mixf,
    cs, cr, vsend, vrecv,
    g_dn, g_up, g_pr, g_qk,
    r1_dn, r1_up, r1_pr, r1_qk, s2_dn, s2_up, s2_pr, s2_qk, r2_dn, r2_up, r2_pr, r2_qk,
    s3_dn, s3_up, s3_pr, s3_qk, r3_dn, r3_up, r3_pr, r3_qk, f_dn, f_up, f_pr, f_qk,
    send_sem, recv_sem, misc_send, misc_recv, local_sem,
):
    dp, ctx = lax.axis_index("dp"), lax.axis_index("ctx")
    z, y, x, core = dp // 2, dp % 2, ctx // 2, ctx % 2
    mate = device_at(z, y, x, 1 - core)
    x_peer = device_at(z, y, 1 - x, core)
    y_peer = device_at(z, 1 - y, x, core)
    z_peers = [device_at((z + d) % 4, y, x, core) for d in (1, 2, 3)]
    own, oth = core * ROWS, (1 - core) * ROWS
    own_rows, oth_rows = at(own, ROWS, ROWS), at(oth, ROWS, ROWS)
    own_half, oth_half = at(core * HALF_WIDTH, HALF_WIDTH, 128), at((1 - core) * HALF_WIDTH, HALF_WIDTH, 128)
    length, group = length_ref[0], group_ref[0]
    gain1, shift1, gain2, shift2 = (
        ref[...].reshape(1, WIDTH) for ref in (gain1_ref, shift1_ref, gain2_ref, shift2_ref)
    )
    left, right = x == 0, x == 1

    def fetch(slot, src, dst):
        return pltpu.make_async_copy(src, dst, local_sem.at[slot])

    def weight_copies(name):
        if name == "qkv":
            return [
                fetch(i, w_qkv.at[:, at(i * WIDTH + core * HALF_WIDTH, HALF_WIDTH, 128)],
                      wq.at[:, pl.ds(i * HALF_WIDTH, HALF_WIDTH)])
                for i in range(3)
            ]
        if name == "proj":
            return [fetch(3, w_proj, wp)]
        if name == "up":
            return [fetch(4, w_up, wu)]
        return [fetch(5, w_down, wd)]

    def ask(*names):
        for name in names:
            for copy in weight_copies(name):
                copy.start()

    ask("qkv")

    def arrive(name):
        for copy in weight_copies(name):
            copy.wait()

    diagonal = device_at(z, y, 1 - x, 1 - core)
    yz_peers = [device_at((z + d) % 4, 1 - y, x, core) for d in (1, 2, 3)]
    peers = [mate, x_peer, diagonal, y_peer] + z_peers + yz_peers
    barrier = pltpu.get_barrier_semaphore()
    for peer in peers:
        pl.semaphore_signal(barrier, inc=1, device_id=peer, device_id_type=MESH)
    pl.semaphore_wait(barrier, len(peers))

    def misc(slot, src, dst, target):
        return pltpu.make_async_remote_copy(
            src_ref=src, dst_ref=dst, send_sem=misc_send.at[slot], recv_sem=misc_recv.at[slot],
            device_id=target, device_id_type=MESH,
        )

    tok_far = misc(0, tok, tokf.at[own_rows], x_peer)
    tok_mate = misc(1, tok, tokc, mate)
    tok_on = misc(2, tokf.at[own_rows], tokf.at[own_rows], mate)
    ups_mate = misc(3, ups.at[:, oth_half], outh.at[own_rows], mate)
    count_y = misc(4, cs.at[0], cr.at[0], y_peer)
    count_z = [misc(4 + d, cs.at[1], cr.at[d], z_peers[d - 1]) for d in (1, 2, 3)]
    att_rows = at(core * HALF_WIDTH, HALF_WIDTH, 128)
    att_mate = misc(8, attt.at[att_rows], attt.at[att_rows], mate)
    n2_mate = misc(9, n2.at[own_rows], n2.at[own_rows], mate)
    gel_mate = [
        misc(10 + i, gel.at[own_rows, pl.ds(1024 * i, 1024)], gel.at[own_rows, pl.ds(1024 * i, 1024)], mate)
        for i in range(3)
    ]
    up_mate = misc(13, upo.at[:, at((1 - core) * 1536, 1536, 128)], uph.at[own_rows], mate)
    hl_mate = misc(14, hl.at[own_rows], hl.at[own_rows], mate)
    nc_mate = misc(15, upo.at[:, :WIDTH], tokc, mate)
    nf_mate = misc(16, tokf.at[own_rows], tokf.at[own_rows], mate)
    nf_far = misc(17, tokf.at[own_rows], tokf.at[own_rows], x_peer)

    @pl.when(left)
    def _():
        tok_far.start()

    tok_mate.start()
    ups_mate.start()
    lane = lax.broadcasted_iota(jnp.int32, (8, 128), 1)
    cs[0] = jnp.where(lane == group, length.astype(F32), 0.0)
    count_y.start()
    ask("proj", "up", "down")

    def first_norm(src, src_at, dst, dst_at):
        def step(i):
            unit, _ = normalise(src[at(src_at + i * 64, 64, 64), :].astype(F32))
            dst[at(dst_at + i * 64, 64, 64), :] = (unit * gain1 + shift1).astype(BF16)

        loop(ROWS // 64, step)

    first_norm(tok, 0, nc, own)
    tok_mate.wait()
    first_norm(tokc, 0, nc, oth)
    arrive("qkv")

    def project(i):
        part = dot_tt(wq[:, at(i * HALF_WIDTH, HALF_WIDTH, 128)], nc[...])
        qkvt[at(i * HALF_WIDTH, HALF_WIDTH, 128), :] = (part * jnp.where(i == 0, 0.125, 1.0)).astype(BF16)

    loop(3, project)

    key_at = lax.broadcasted_iota(jnp.int32, (512, 512), 0)
    query_at = lax.broadcasted_iota(jnp.int32, (512, 512), 1)
    bias[...] = jnp.where((key_at <= query_at) & (key_at + x * 512 < length), 0.0, NEG_FILL).astype(BF16)

    def attend_chip(h):
        r = h * 64
        keys, queries, values = qkvt[at(HALF_WIDTH + r, 64, 64), :], qkvt[at(r, 64, 64), :], qkvt[at(2 * HALF_WIDTH + r, 64, 64), :]
        for half in (0, 1):
            span, cols = 256 * (half + 1), slice(256 * half, 256 * half + 256)
            scores = dot_tn(keys[:, :span], queries[:, cols]) + bias[:span, cols].astype(F32)
            peak = jnp.max(scores, axis=0, keepdims=True)
            expo = jnp.exp(scores - peak)
            expo_low = expo.astype(BF16)
            m1[pl.ds(h, 1), cols] = peak
            l1[pl.ds(h, 1), cols] = jnp.sum(expo_low.astype(F32), axis=0, keepdims=True)
            ec[h, :span, cols] = expo_low
            o1[at(r, 64, 64), cols] = dot_nn(values[:, :span], expo_low)

    loop(HALF_HEADS, attend_chip)

    count_y.wait()
    cs[1] = cs[0] + cr[0]
    for copy in count_z:
        copy.start()
    for copy in count_z:
        copy.wait()
    counts = cs[1] + cr[1] + cr[2] + cr[3]
    total = jnp.sum(counts, axis=1, keepdims=True)
    mine = jnp.sum(jnp.where(lane == group, counts, 0.0), axis=1, keepdims=True)
    scale = (weight_ref[0].astype(F32) * total / (NGROUPS * mine))[0:1, 0:1]
    row_at = lax.broadcasted_iota(jnp.int32, (ROWS, 1), 0) + x * 512
    own_scale = jnp.where(row_at + own < length, scale, 0.0)
    oth_scale = jnp.where(row_at + oth < length, scale, 0.0)
    outl[...] = (ups[...].astype(F32) * own_scale).astype(BF16)
    outh[own_rows, :] = (ups[:, own_half].astype(F32) * own_scale).astype(BF16)
    ups_mate.wait()
    outh[oth_rows, :] = (outh[oth_rows, :].astype(F32) * oth_scale).astype(BF16)

    @pl.when(right)
    def _():
        def far_block(start):
            first_norm(tokf, start, nf, start)
            columns = at(start, ROWS, ROWS)

            def project_far(i):
                part = dot_tt(wq[:, at((i + 1) * HALF_WIDTH, HALF_WIDTH, 128)], nf[columns, :])
                kvft[at(i * HALF_WIDTH, HALF_WIDTH, 128), columns] = part.astype(BF16)

            loop(2, project_far)

        tok_far.wait_recv()
        tok_on.start()
        far_block(own)
        tok_on.wait()
        far_block(oth)

        def attend_far(h):
            r = h * 64
            keys, queries, values = kvft[at(r, 64, 64), :], qkvt[at(r, 64, 64), :], kvft[at(HALF_WIDTH + r, 64, 64), :]
            for half in (0, 1):
                cols = slice(256 * half, 256 * half + 256)
                scores = dot_tn(keys, queries[:, cols])
                peak = jnp.max(scores, axis=0, keepdims=True)
                expo = jnp.exp(scores - peak)
                expo_low = expo.astype(BF16)
                expo_sum = jnp.sum(expo_low.astype(F32), axis=0, keepdims=True)
                ef[h, :, cols] = expo_low
                out = dot_nn(values, expo_low)
                old = m1[pl.ds(h, 1), cols]
                top = jnp.maximum(old, peak)
                old_part, new_part = jnp.exp(old - top), jnp.exp(peak - top)
                share = 1.0 / (l1[pl.ds(h, 1), cols] * old_part + expo_sum * new_part)
                f1[pl.ds(h, 1), cols] = old_part * share
                f2[pl.ds(h, 1), cols] = new_part * share
                o1[at(r, 64, 64), cols] = o1[at(r, 64, 64), cols] * (old_part * share) + out * (new_part * share)

        loop(HALF_HEADS, attend_far)

    @pl.when(left)
    def _():
        nf[...] = jnp.zeros_like(nf)
        mixf[...] = jnp.zeros_like(mixf)

        def share_out(h):
            share = 1.0 / l1[pl.ds(h, 1), :]
            f1[pl.ds(h, 1), :] = share
            f2[pl.ds(h, 1), :] = jnp.zeros_like(share)
            o1[at(h * 64, 64, 64), :] = o1[at(h * 64, 64, 64), :] * share

        loop(HALF_HEADS, share_out)

    attt[att_rows, :] = o1[...].astype(BF16)
    att_mate.start()
    arrive("proj")
    att_mate.wait()

    for i in range(3):
        cols = slice(256 * i, 256 * i + 256)
        hid[:, cols] = tok[:, cols].astype(F32) + dot_tn(attt[:, own_rows], wp[:, cols])

    def second_norm(i):
        unit, _ = normalise(hid[at(i * 64, 64, 64), :])
        n2[at(own + i * 64, 64, 64), :] = (unit * gain2 + shift2).astype(BF16)

    loop(ROWS // 64, second_norm)
    n2_mate.start()
    arrive("up")
    for part in range(3):

        def feed(i, part=part):
            cols = at(part * 1024 + i * 256, 256, 256)
            u = dot_nn(n2[own_rows, :], wu[:, cols])
            square = u * u
            bend = jnp.tanh(GELU_COEF * (u + 0.044715 * square * u))
            lift = 0.5 * (1.0 + bend)
            gel[own_rows, cols] = (u * lift).astype(BF16)
            slope = lift + 0.5 * u * (1.0 - bend * bend) * (GELU_COEF * (1.0 + 3 * 0.044715 * square))
            dg[:, cols] = slope.astype(BF16)

        loop(4, feed)
        gel_mate[part].start()

    first = device_at(z, (y + core) % 2, (x + 1 - core) % 2, core)
    second = device_at(z, (y + 1 - core) % 2, (x + core) % 2, core)
    kept = jnp.where(core == 0, y, x)
    grads = (g_dn, g_up, g_pr, g_qk)
    outs = (o_dn, o_up, o_pr, o_qk)
    r1s, s2s, r2s = (r1_dn, r1_up, r1_pr, r1_qk), (s2_dn, s2_up, s2_pr, s2_qk), (r2_dn, r2_up, r2_pr, r2_qk)
    s3s, r3s = (s3_dn, s3_up, s3_pr, s3_qk), (r3_dn, r3_up, r3_pr, r3_qk)
    fs = (f_dn, f_up, f_pr, f_qk)

    def remote(src, dst, w, slot, target):
        return pltpu.make_async_remote_copy(
            src_ref=src, dst_ref=dst, send_sem=send_sem.at[w, slot], recv_sem=recv_sem.at[w, slot],
            device_id=target, device_id_type=MESH,
        )

    def block(w, index):
        rows = BLOCKS[w][0]
        return at(index * rows, rows, 16)

    def kept_block(w, zz, j):
        return grads[w][block(w, zz * 4 + jnp.where(core == 0, j * 2 + x, y * 2 + j)), :].astype(F32)

    def first_copy(w, zz, j):
        index = zz * 4 + jnp.where(core == 0, j * 2 + 1 - x, (1 - y) * 2 + j)
        return remote(grads[w].at[block(w, index)], r1s[w].at[zz, j], w, zz * 2 + j, first)

    def start_first(w, places):
        for zz in places:
            for j in range(2):
                first_copy(w, zz, j).start()

    def second_copy(w):
        return remote(s2s[w], r2s[w], w, 8, second)

    def third_copy(w, d):
        return remote(s3s[w].at[d - 1], r3s[w].at[d - 1], w, 8 + d, z_peers[d - 1])

    def places(w):
        parts = 3 if w == 3 else 1
        width = BLOCKS[w][1] // parts
        return [(pl.ds(i * width, width), at((2 * i + core) * width, width, 128)) for i in range(parts)]

    def last_copies(w):
        rows = BLOCKS[w][0] // 2
        far_rows = at((1 - core) * rows, rows, 8)
        return [
            remote(fs[w].at[far_rows, src], outs[w].at[:, dst], w, 12 + i, mate)
            for i, (src, dst) in enumerate(places(w))
        ]

    def start_second(w):
        for zz in range(4):
            for j in range(2):
                first_copy(w, zz, j).wait()
        j = 1 - kept
        for zz in range(4):
            s2s[w][zz] = (kept_block(w, zz, j) + r1s[w][zz, j].astype(F32)).astype(BF16)
        second_copy(w).start()

    def summed(w, zz):
        return kept_block(w, zz, kept) + r1s[w][zz, kept].astype(F32) + r2s[w][zz].astype(F32)

    def start_third(w):
        second_copy(w).wait()
        for d in (1, 2, 3):
            s3s[w][d - 1] = summed(w, (z + d) % 4).astype(BF16)
            third_copy(w, d).start()
        fs[w][...] = summed(w, z)

    def start_last(w):
        for d in (1, 2, 3):
            third_copy(w, d).wait()
        rows = BLOCKS[w][0] // 2
        fs[w][...] = fs[w][...] + r3s[w][0].astype(F32) + r3s[w][1].astype(F32) + r3s[w][2].astype(F32)
        for copy in last_copies(w):
            copy.start()
        for src, dst in places(w):
            outs[w][:, dst] = fs[w][at(core * rows, rows, 8), src]

    def finish(w):
        for copy in last_copies(w):
            copy.wait()

    for copy in gel_mate:
        copy.wait()
    for zz in range(4):

        def down_rows(i, zz=zz):
            start = zz * WIDTH + i * 256
            g_dn[at(start, 256, 256), :] = dot_tn(gel[:, at(start, 256, 256)], outh[...]).astype(BF16)

        loop(3, down_rows)
        start_first(0, (zz,))

    arrive("down")

    def gelu_back(cols):
        up_cot = dot_nt(outl[...], wd[cols, :]) * dg[:, cols].astype(F32)
        up_cot = up_cot.astype(BF16)
        upo[:, cols] = up_cot
        return up_cot

    def back_other(i):
        gelu_back(at((1 - core) * 1536 + i * 256, 256, 256))

    def back_own(i):
        uph[own_rows, at(i * 256, 256, 256)] = gelu_back(at(core * 1536 + i * 256, 256, 256))

    loop(6, back_other)
    up_mate.start()
    loop(6, back_own)

    def n2_back(i):
        cols = at(i * 256, 256, 256)
        ncot[:, cols] = dot_nt(upo[...], wu[cols, :])

    loop(3, n2_back)
    vsend[...] = jnp.zeros_like(vsend)

    def second_back(i):
        rows = at(i * 64, 64, 64)
        unit, inverse = normalise(hid[rows, :])
        cot = ncot[rows, :]
        position = lax.broadcasted_iota(jnp.int32, (64, 1), 0) + i * 64 + x * 512 + own
        out_cot = ups[rows, :].astype(F32) * jnp.where(position < length, scale, 0.0)
        hidden_cot = out_cot + normalise_back(cot, gain2, unit, inverse)
        hc[rows, :] = hidden_cot
        hl[at(own + i * 64, 64, 64), :] = hidden_cot.astype(BF16)
        vsend[0, 2:3, :] += jnp.sum(cot * unit, axis=0, keepdims=True)
        vsend[0, 3:4, :] += jnp.sum(cot, axis=0, keepdims=True)

    loop(ROWS // 64, second_back)
    hl_mate.start()

    n2_mate.wait()
    up_mate.wait()
    for part in range(2):

        def up_columns(i, part=part):
            cols = at(i * 512, 512, 512)
            g_up[384 * part : 384 * part + 384, cols] = dot_tn(n2[:, 384 * part : 384 * part + 384], uph[:, cols]).astype(BF16)

        loop(3, up_columns)
        start_first(1, (2 * part, 2 * part + 1))

    hl_mate.wait()

    def proj_rows(i):
        rows = at(i * 256, 256, 256)
        g_pr[rows, :] = dot_nn(attt[rows, :], hl[:, own_half]).astype(BF16)

    loop(3, proj_rows)
    start_first(2, range(4))
    attt[att_rows, :] = dot_nt(wp[att_rows, :], hl[...]).astype(BF16)

    def attend_back(h):
        r = h * 64
        rows = at(r, 64, 64)
        keys, queries, values = qkvt[at(HALF_WIDTH + r, 64, 64), :], qkvt[rows, :], qkvt[at(2 * HALF_WIDTH + r, 64, 64), :]
        cot = attt[at(core * HALF_WIDTH + r, 64, 64), :].astype(F32)
        near = (cot * f1[pl.ds(h, 1), :]).astype(BF16)
        delta = jnp.sum(near.astype(F32) * o1[rows, :], axis=0, keepdims=True)
        far = (cot * f2[pl.ds(h, 1), :]).astype(BF16)
        far_delta = jnp.sum(far.astype(F32) * o1[rows, :], axis=0, keepdims=True)
        key_terms, value_terms = [], []
        for half in (0, 1):
            span, cols = 256 * (half + 1), slice(256 * half, 256 * half + 256)
            expo = ec[h, :span, cols]
            prob_cot = dot_tn(values[:, :span], near[:, cols])
            score_cot = (expo.astype(F32) * (prob_cot - delta[:, cols])).astype(BF16)
            o1[rows, cols] = dot_nn(keys[:, :span], score_cot)
            key_terms.append(dot_nt(queries[:, cols], score_cot))
            value_terms.append(dot_nt(near[:, cols], expo))
        for start, terms in ((HALF_WIDTH, key_terms), (2 * HALF_WIDTH, value_terms)):
            mixc[at(start + r, 64, 64), :256] = (terms[0] + terms[1][:, :256]).astype(BF16)
            mixc[at(start + r, 64, 64), 256:] = terms[1][:, 256:].astype(BF16)

        @pl.when(right)
        def _():
            far_keys, far_values = kvft[rows, :], kvft[at(HALF_WIDTH + r, 64, 64), :]
            expo = ef[h]
            prob_cot = dot_tn(far_values, far)
            score_cot = (expo.astype(F32) * (prob_cot - far_delta)).astype(BF16)
            o1[rows, :] += dot_nn(far_keys, score_cot)
            mixf[rows, :] = dot_nt(queries, score_cot).astype(BF16)
            mixf[at(HALF_WIDTH + r, 64, 64), :] = dot_nt(far, expo).astype(BF16)

        mixc[rows, :] = (o1[rows, :] * 0.125).astype(BF16)

    def attend_back_late(h):
        attend_back(h + 3)

    loop(3, attend_back)
    start_second(0)
    loop(3, attend_back_late)
    start_second(1)

    def normed_cot(mixed, first_column, columns, store):
        def step(i):
            rows = at(i * 256, 256, 256)
            store(rows, dot_tt(mixed[:, columns], wq[rows, first_column:]))

        loop(3, step)

    def store_to(ref, rows):
        def store(cols, value):
            ref[rows, cols] = value.astype(ref.dtype)

        return store

    @pl.when(right)
    def _():
        normed_cot(mixf, HALF_WIDTH, oth_rows, store_to(tokf, own_rows))
        nf_mate.start()

    normed_cot(mixc, 0, oth_rows, store_to(upo, at(0, ROWS, ROWS)))
    nc_mate.start()

    @pl.when(right)
    def _():
        normed_cot(mixf, HALF_WIDTH, own_rows, store_to(ncot, at(0, ROWS, ROWS)))
        nf_mate.wait()
        tokf[own_rows, :] = (ncot[...] + tokf[oth_rows, :].astype(F32)).astype(BF16)
        nf_far.start()

    for part in range(2):
        cols = slice(384 * part, 384 * part + 384)
        g_qk[cols, :384] = dot_tt(nc[:, cols], mixc[:384, :]).astype(BF16)
        for i in range(2):
            g_qk[cols, 384 * (i + 1) : 384 * (i + 2)] = (
                dot_tt(nc[:, cols], mixc[384 * (i + 1) : 384 * (i + 2), :])
                + dot_tt(nf[:, cols], mixf[384 * i : 384 * (i + 1), :])
            ).astype(BF16)
        start_first(3, (2 * part, 2 * part + 1))

    normed_cot(mixc, 0, own_rows, store_to(ncot, at(0, ROWS, ROWS)))
    start_third(0)
    start_second(2)

    def block_rows(i):
        cols = at(i * 256, 256, 256)
        block_out[:, cols] = (hid[:, cols] + dot_nn(gel[own_rows, :], wd[:, cols])).astype(BF16)

    loop(3, block_rows)
    nc_mate.wait()

    @pl.when(left)
    def _():
        nf_far.wait_recv()
        tok_far.wait_send()

    @pl.when(right)
    def _():
        nf_far.wait_send()

    def first_back(i):
        rows = at(i * 64, 64, 64)
        unit, inverse = normalise(tok[rows, :].astype(F32))
        near = tokc[rows, :].astype(F32)
        far = tokf[at(own + i * 64, 64, 64), :].astype(F32)
        cot = ncot[rows, :] + near + jnp.where(left, far, 0.0)
        input_grad[rows, :] = (hc[rows, :] + normalise_back(cot, gain1, unit, inverse)).astype(BF16)
        vsend[0, 0:1, :] += jnp.sum(cot * unit, axis=0, keepdims=True)
        vsend[0, 1:2, :] += jnp.sum(cot, axis=0, keepdims=True)

    loop(ROWS // 64, first_back)

    clip_peers = [mate, x_peer, diagonal]
    other_clips = [y_peer] + z_peers + yz_peers

    def clip_sum(i):
        return misc(18 + i, vsend.at[0], vrecv.at[i], clip_peers[i])

    def all_sum(i):
        return misc(21 + i, vsend.at[1], vrecv.at[3 + i], other_clips[i])

    for i in range(3):
        clip_sum(i).start()
    start_third(1)
    for i in range(3):
        clip_sum(i).wait()
    vsend[1] = vsend[0] + vrecv[0] + vrecv[1] + vrecv[2]
    for i in range(7):
        all_sum(i).start()
    start_second(3)
    start_last(0)
    start_third(2)
    for i in range(7):
        all_sum(i).wait()
    sums = vsend[1]
    for i in range(7):
        sums = sums + vrecv[3 + i]
    rank = dp * 4 + ctx
    o_vec[...] = pltpu.roll(sums, lax.rem(WIDTH - rank * 24, WIDTH), 1)[:, :128]
    start_last(1)
    start_third(3)
    start_last(2)
    start_last(3)
    for w in range(4):
        finish(w)


def hand_out_kernel(
    block_out, input_grad, qk, pr, up, dn, vec,
    o_block, o_input, o_v0, o_v1, o_qk, o_pr, o_v2, o_v3, o_up, o_dn, sem,
):
    pairs = ((block_out, o_block), (input_grad, o_input), (qk, o_qk), (pr, o_pr), (up, o_up), (dn, o_dn))
    copies = [pltpu.make_async_copy(src, dst, sem.at[i]) for i, (src, dst) in enumerate(pairs)]
    for copy in copies:
        copy.start()
    for i, ref in enumerate((o_v0, o_v1, o_v2, o_v3)):
        ref[...] = vec[i, :24]
    for copy in copies:
        copy.wait()


def fused_layer(args):
    vmem, smem, anywhere = (
        pl.BlockSpec(memory_space=pltpu.VMEM),
        pl.BlockSpec(memory_space=pltpu.SMEM),
        pl.BlockSpec(memory_space=pl.ANY),
    )

    def low(*shape):
        return pltpu.VMEM(shape, BF16)

    def full(*shape):
        return pltpu.VMEM(shape, F32)

    def per_block(lead):
        return [pltpu.VMEM(lead + block, BF16) for block in BLOCKS]

    vector = jax.ShapeDtypeStruct((24,), F32)

    def grad_shape(w):
        return jax.ShapeDtypeStruct((BLOCKS[w][0] // 2, BLOCKS[w][1] * 2), F32)

    rows_out = jax.ShapeDtypeStruct((ROWS, WIDTH), BF16)
    made = pl.pallas_call(
        layer_kernel,
        out_shape=[
            rows_out, rows_out, grad_shape(3), grad_shape(2), grad_shape(1), grad_shape(0),
            jax.ShapeDtypeStruct((8, 128), F32),
        ],
        in_specs=[smem] * 3 + [vmem] * 6 + [anywhere] * 4,
        out_specs=[vmem] * 7,
        scratch_shapes=[
            low(768, 1152), low(768, 768), low(768, 3072), low(3072, 768),
            low(256, 768), low(512, 768), low(512, 768), low(512, 768),
            low(1152, 512), low(768, 512), low(512, 512), low(6, 512, 512), low(6, 512, 512),
            full(384, 512), full(8, 512), full(8, 512), full(8, 512), full(8, 512),
            low(768, 512), full(256, 768), low(512, 768), low(512, 3072), low(256, 3072),
            low(256, 768), low(512, 384), low(256, 3072), low(512, 1536), full(256, 768),
            full(256, 768), low(512, 768), low(1152, 512), low(768, 512),
            full(2, 8, 128), full(4, 8, 128), full(2, 8, 768), full(10, 8, 768),
            low(3072, 384), low(768, 1536), low(768, 384), low(768, 1152),
        ]
        + per_block((4, 2)) + per_block((4,)) + per_block((4,)) + per_block((3,)) + per_block((3,))
        + [pltpu.VMEM(block, F32) for block in BLOCKS]
        + [
            pltpu.SemaphoreType.DMA((4, 15)),
            pltpu.SemaphoreType.DMA((4, 15)),
            pltpu.SemaphoreType.DMA((28,)),
            pltpu.SemaphoreType.DMA((28,)),
            pltpu.SemaphoreType.DMA((6,)),
        ],
        compiler_params=pltpu.CompilerParams(
            collective_id=0, has_side_effects=True, vmem_limit_bytes=60 * 1024 * 1024
        ),
    )(*args)
    return pl.pallas_call(
        hand_out_kernel,
        out_shape=[
            rows_out, rows_out, vector, vector, grad_shape(3), grad_shape(2), vector, vector,
            grad_shape(1), grad_shape(0),
        ],
        in_specs=[vmem] * 7,
        out_specs=[anywhere] * 2 + [vmem] * 2 + [anywhere] * 2 + [vmem] * 2 + [anywhere] * 2,
        scratch_shapes=[pltpu.SemaphoreType.DMA((6,))],
        compiler_params=pltpu.CompilerParams(vmem_limit_bytes=60 * 1024 * 1024),
    )(*made)


def general_body(
    tokens,
    attn_gain,
    attn_shift,
    w_qkv,
    w_proj,
    mlp_gain,
    mlp_shift,
    w_up,
    w_down,
    upstream,
    clip_length,
    dataset_group,
    sample_weight,
):
    tok_rows = tokens.shape[0]
    model_width = tokens.shape[1]
    head_count = model_width // HD
    ctx_count = lax.axis_size("ctx")
    seq_rows = tok_rows * ctx_count
    first_row = lax.axis_index("ctx") * tok_rows
    length = clip_length[0]
    key_span = min(seq_rows, max(tok_rows, 512))
    block_count = seq_rows // key_span
    query_pos = first_row + jnp.arange(tok_rows, dtype=jnp.int32)
    last_pos = first_row + tok_rows - 1
    onehot = (dataset_group[0, 0] == jnp.arange(NGROUPS, dtype=jnp.int32)).astype(jnp.float32)
    counts = lax.psum(onehot * length.astype(jnp.float32), "dp")
    total_all = jnp.sum(counts)
    clip_scale = (
        sample_weight[0].astype(jnp.float32) * total_all / (NGROUPS * jnp.sum(onehot * counts))
    )
    x_rows = tokens.astype(jnp.float32)
    normed, norm_one_back = jax.vjp(layer_norm, x_rows, attn_gain, attn_shift)
    normed_low = normed.astype(jnp.bfloat16)
    mixed_qkv = jnp.dot(normed_low, w_qkv, preferred_element_type=jnp.float32).astype(jnp.bfloat16)
    queries = mixed_qkv[:, :model_width]
    key_local = mixed_qkv[:, model_width : 2 * model_width]
    value_local = mixed_qkv[:, 2 * model_width :]
    key_all, value_all = (
        lax.all_gather(key_local, "ctx", axis=0, tiled=True),
        lax.all_gather(value_local, "ctx", axis=0, tiled=True),
    )
    queries3 = queries.reshape(tok_rows, head_count, HD)

    def scores_for(kstart, key_rows):
        piece = key_rows[kstart : kstart + key_span].reshape(key_span, head_count, HD)
        raw = (
            jnp.einsum("qhd,khd->hqk", queries3, piece, preferred_element_type=jnp.float32) * 0.125
        )
        key_pos = kstart + jnp.arange(key_span, dtype=jnp.int32)
        allowed = (key_pos[None, :] <= query_pos[:, None]) & (key_pos[None, :] < length)
        return (jnp.where(allowed[None], raw, NEG_FILL), allowed)

    def useful(kstart):
        return (kstart <= last_pos) & (kstart < length)

    peak = jnp.full((head_count, tok_rows), NEG_FILL, jnp.float32)
    exp_total = jnp.zeros((head_count, tok_rows), jnp.float32)
    for index in range(block_count):
        kstart = index * key_span

        def gather_stats(carry, kstart=kstart):
            old_peak, old_total = carry
            scores, allowed = scores_for(kstart, key_all)
            new_peak = jnp.maximum(old_peak, jnp.max(scores, axis=-1))
            expo_vals = jnp.where(allowed[None], jnp.exp(scores - new_peak[..., None]), 0.0)
            return (
                new_peak,
                old_total * jnp.exp(old_peak - new_peak) + jnp.sum(expo_vals, axis=-1),
            )

        peak, exp_total = lax.cond(
            useful(kstart), gather_stats, lambda carry: carry, (peak, exp_total)
        )

    def probs_for(kstart, key_rows):
        scores, allowed = scores_for(kstart, key_rows)
        return (
            jnp.where(allowed[None], jnp.exp(scores - peak[..., None]), 0.0) / exp_total[..., None]
        )

    out_high = jnp.zeros((tok_rows, head_count, HD), jnp.float32)
    out_rest = jnp.zeros((tok_rows, head_count, HD), jnp.float32)
    for index in range(block_count):
        kstart = index * key_span

        def add_values(carry, kstart=kstart):
            high_acc, rest_acc = carry
            probs = probs_for(kstart, key_all)
            probs_low = probs.astype(jnp.bfloat16)
            remainder = (probs - probs_low.astype(jnp.float32)).astype(jnp.bfloat16)
            piece = value_all[kstart : kstart + key_span].reshape(key_span, head_count, HD)
            high_acc = high_acc + jnp.einsum(
                "hqk,khd->qhd", probs_low, piece, preferred_element_type=jnp.float32
            )
            rest_acc = rest_acc + jnp.einsum(
                "hqk,khd->qhd", remainder, piece, preferred_element_type=jnp.float32
            )
            return (high_acc, rest_acc)

        out_high, out_rest = lax.cond(
            useful(kstart), add_values, lambda carry: carry, (out_high, out_rest)
        )
    attended_low = out_high.reshape(tok_rows, model_width).astype(jnp.bfloat16)
    out_full = out_high + out_rest
    hidden = x_rows + jnp.dot(attended_low, w_proj, preferred_element_type=jnp.float32)
    normed_two, norm_two_back = jax.vjp(layer_norm, hidden, mlp_gain, mlp_shift)
    normed_two_low = normed_two.astype(jnp.bfloat16)
    up_proj = jnp.dot(normed_two_low, w_up, preferred_element_type=jnp.float32)
    gelu_vals, gelu_back = jax.vjp(gelu, up_proj)
    gelu_low = gelu_vals.astype(jnp.bfloat16)
    block_out = (hidden + jnp.dot(gelu_low, w_down, preferred_element_type=jnp.float32)).astype(
        jnp.bfloat16
    )
    valid = query_pos < length
    out_cot = upstream.astype(jnp.float32) * jnp.where(valid, clip_scale, 0.0)[:, None]
    out_cot_low = out_cot.astype(jnp.bfloat16)
    down_grad = jnp.einsum("tf,td->fd", gelu_low, out_cot_low, preferred_element_type=jnp.float32)
    gelu_in = jnp.einsum("td,fd->tf", out_cot_low, w_down, preferred_element_type=jnp.float32)
    (up_cot,) = gelu_back(gelu_in)
    up_cot_low = up_cot.astype(jnp.bfloat16)
    up_grad = jnp.einsum(
        "td,tf->df", normed_two_low, up_cot_low, preferred_element_type=jnp.float32
    )
    normed_two_cot = jnp.einsum("tf,df->td", up_cot_low, w_up, preferred_element_type=jnp.float32)
    norm_two_rows, mlp_gain_grad, mlp_shift_grad = norm_two_back(normed_two_cot)
    hidden_cot = out_cot + norm_two_rows
    hidden_cot_low = hidden_cot.astype(jnp.bfloat16)
    proj_grad = jnp.einsum(
        "ti,to->io", attended_low, hidden_cot_low, preferred_element_type=jnp.float32
    )
    attended_cot = jnp.einsum(
        "to,io->ti", hidden_cot_low, w_proj, preferred_element_type=jnp.float32
    ).astype(jnp.bfloat16)
    attended_cot3 = attended_cot.reshape(tok_rows, head_count, HD)
    delta = jnp.einsum("qhd,qhd->hq", attended_cot3.astype(jnp.float32), out_full)
    key_back, value_back = (key_all, value_all)
    query_cot = jnp.zeros((tok_rows, head_count, HD), jnp.float32)
    key_pieces = []
    value_pieces = []
    empty_piece = jnp.zeros((key_span, head_count, HD), jnp.float32)
    for index in range(block_count):
        kstart = index * key_span

        def block_grads(q_acc, kstart=kstart):
            probs = probs_for(kstart, key_back)
            probs_low = probs.astype(jnp.bfloat16)
            key_piece = key_back[kstart : kstart + key_span].reshape(key_span, head_count, HD)
            value_piece = value_back[kstart : kstart + key_span].reshape(key_span, head_count, HD)
            prob_cot = jnp.einsum(
                "qhd,khd->hqk", attended_cot3, value_piece, preferred_element_type=jnp.float32
            )
            score_cot = (probs * (prob_cot - delta[..., None])).astype(jnp.bfloat16)
            q_acc = (
                q_acc
                + jnp.einsum(
                    "hqk,khd->qhd", score_cot, key_piece, preferred_element_type=jnp.float32
                )
                * 0.125
            )
            key_term = (
                jnp.einsum("hqk,qhd->khd", score_cot, queries3, preferred_element_type=jnp.float32)
                * 0.125
            )
            value_term = jnp.einsum(
                "hqk,qhd->khd", probs_low, attended_cot3, preferred_element_type=jnp.float32
            )
            return (q_acc, key_term, value_term)

        query_cot, key_term, value_term = lax.cond(
            useful(kstart), block_grads, lambda q_acc: (q_acc, empty_piece, empty_piece), query_cot
        )
        key_pieces.append(key_term.reshape(key_span, model_width))
        value_pieces.append(value_term.reshape(key_span, model_width))
    key_terms = jnp.concatenate(key_pieces, axis=0)
    value_terms = jnp.concatenate(value_pieces, axis=0)
    key_cot, value_cot = (
        lax.psum_scatter(
            key_terms.astype(jnp.bfloat16), "ctx", scatter_dimension=0, tiled=True
        ).astype(jnp.float32),
        lax.psum_scatter(
            value_terms.astype(jnp.bfloat16), "ctx", scatter_dimension=0, tiled=True
        ).astype(jnp.float32),
    )
    mixed_cot = jnp.concatenate(
        [query_cot.reshape(tok_rows, model_width), key_cot, value_cot], axis=1
    ).astype(jnp.bfloat16)
    qkv_grad = jnp.einsum("td,te->de", normed_low, mixed_cot, preferred_element_type=jnp.float32)
    normed_cot = jnp.einsum("te,de->td", mixed_cot, w_qkv, preferred_element_type=jnp.float32)
    norm_one_rows, attn_gain_grad, attn_shift_grad = norm_one_back(normed_cot)
    input_grad = (hidden_cot + norm_one_rows).astype(jnp.bfloat16)
    reduced = (
        lax.psum_scatter(attn_gain_grad, ("dp", "ctx"), scatter_dimension=0, tiled=True),
        lax.psum_scatter(attn_shift_grad, ("dp", "ctx"), scatter_dimension=0, tiled=True),
        lax.psum_scatter(qkv_grad, ("dp", "ctx"), scatter_dimension=0, tiled=True),
        lax.psum_scatter(proj_grad, ("dp", "ctx"), scatter_dimension=0, tiled=True),
        lax.psum_scatter(mlp_gain_grad, ("dp", "ctx"), scatter_dimension=0, tiled=True),
        lax.psum_scatter(mlp_shift_grad, ("dp", "ctx"), scatter_dimension=0, tiled=True),
        lax.psum_scatter(up_grad, ("dp", "ctx"), scatter_dimension=0, tiled=True),
        lax.psum_scatter(down_grad, ("dp", "ctx"), scatter_dimension=0, tiled=True),
    )
    return (
        block_out,
        input_grad,
        reduced[0],
        reduced[1],
        reduced[2],
        reduced[3],
        reduced[4],
        reduced[5],
        reduced[6],
        reduced[7],
    )


def fused_body(
    tokens, attn_gain, attn_shift, w_qkv, w_proj, mlp_gain, mlp_shift, w_up, w_down, upstream,
    clip_length, dataset_group, sample_weight,
):
    outs = fused_layer(
        [clip_length, dataset_group.reshape(1), sample_weight, tokens, upstream]
        + [attn_gain, attn_shift, mlp_gain, mlp_shift, w_qkv, w_proj, w_up, w_down]
    )
    return tuple(outs)


def solution(mesh):
    in_specs = (
        P(("dp", "ctx"), None),
        P(),
        P(),
        P(),
        P(),
        P(),
        P(),
        P(),
        P(),
        P(("dp", "ctx"), None),
        P("dp"),
        P("dp", None),
        P("dp"),
    )
    out_specs = (
        P(("dp", "ctx"), None),
        P(("dp", "ctx"), None),
        P(("dp", "ctx")),
        P(("dp", "ctx")),
        P(("dp", "ctx"), None),
        P(("dp", "ctx"), None),
        P(("dp", "ctx")),
        P(("dp", "ctx")),
        P(("dp", "ctx"), None),
        P(("dp", "ctx"), None),
    )
    fused = mesh.shape["dp"] == 8 and mesh.shape["ctx"] == 4
    body = fused_body if fused else general_body
    return jax.shard_map(body, mesh=mesh, in_specs=in_specs, out_specs=out_specs, check_vma=False)
```

```python
import jax
import jax.numpy as jnp
from jax import lax
from jax.experimental import pallas as pl
from jax.experimental.pallas import tpu as pltpu
from jax.sharding import PartitionSpec as P

HD = 64
NGROUPS = 4


EPSILON = 1e-05
NEG_FILL = -1e30
GELU_COEF = 0.7978845608028654


def layer_norm(values, gain_vec, shift_vec):
    average = jnp.mean(values, axis=-1, keepdims=True)
    centred = values - average
    spread = jnp.mean(centred * centred, axis=-1, keepdims=True)
    return centred * lax.rsqrt(spread + EPSILON) * gain_vec + shift_vec


def gelu(inputs):
    return (
        0.5 * inputs * (1.0 + jnp.tanh(GELU_COEF * (inputs + 0.044715 * inputs * inputs * inputs)))
    )


MESH = pl.DeviceIdType.MESH
BF16 = jnp.bfloat16
F32 = jnp.float32
ROWS = 256
WIDTH = 768
HIDDEN = 3072
HALF_HEADS = 6
HALF_WIDTH = 384
BLOCKS = ((192, 384), (48, 1536), (48, 384), (48, 1152))
ORDERS = (('zyx', 'yxz'), ('xyz', 'yxz'), ('zyx', 'zxy'), ('xyz', 'yxz'))


def dot_nn(left, right):
    return lax.dot_general(left, right, (((1,), (0,)), ((), ())), preferred_element_type=F32)


def dot_nt(left, right):
    return lax.dot_general(left, right, (((1,), (1,)), ((), ())), preferred_element_type=F32)


def dot_tn(left, right):
    return lax.dot_general(left, right, (((0,), (0,)), ((), ())), preferred_element_type=F32)


def dot_tt(left, right):
    return lax.dot_general(left, right, (((0,), (1,)), ((), ())), preferred_element_type=F32)


def device_at(z, y, x, core):
    return (z * 2 + y, x * 2 + core)


def normalise(values):
    average = jnp.mean(values, axis=-1, keepdims=True)
    centred = values - average
    spread = jnp.mean(centred * centred, axis=-1, keepdims=True)
    inverse = lax.rsqrt(spread + EPSILON)
    return centred * inverse, inverse


def normalise_back(cot, gain, unit, inverse):
    scaled = cot * gain
    first = jnp.mean(scaled, axis=-1, keepdims=True)
    second = jnp.mean(scaled * unit, axis=-1, keepdims=True)
    return inverse * (scaled - first - unit * second)


def loop(count, step, unroll=1):
    if unroll == 0:
        for i in range(count):
            step(i)
        return

    def wrapped(index, carry):
        step(index)
        return carry

    lax.fori_loop(0, count, wrapped, 0, unroll=unroll)


def at(start, size, unit):
    return pl.ds(pl.multiple_of(start, unit), size)


def layer_kernel(
    length_ref, group_ref, weight_ref, tok, ups, gain1_ref, shift1_ref, gain2_ref, shift2_ref,
    w_qkv, w_proj, w_up, w_down,
    block_out, input_grad, o_qk, o_pr, o_up, o_dn, o_vec,
    wq, wp, wu, wd, tokc, tokf, nc, nf, qkvt, kvft, bias, ec, ef, o1, m1, l1, f1, f2,
    attt, hid, n2, gel, dg, outh, upo, uph, ncot, hc, hl, mixc, mixf,
    cs, cr, vsend, vrecv,
    g_dn, g_up, g_pr, g_qk,
    c_dn, c_up, c_pr, c_qk, s_dn, s_up, s_pr, s_qk, h_dn, h_up, h_pr, h_qk,
    send_sem, recv_sem, misc_send, misc_recv, local_sem,
):
    dp, ctx = lax.axis_index("dp"), lax.axis_index("ctx")
    z, y, x, core = dp // 2, dp % 2, ctx // 2, ctx % 2
    mate = device_at(z, y, x, 1 - core)
    x_peer = device_at(z, y, 1 - x, core)
    y_peer = device_at(z, 1 - y, x, core)
    z_peers = [device_at((z + d) % 4, y, x, core) for d in (1, 2, 3)]
    own, oth = core * ROWS, (1 - core) * ROWS
    own_rows, oth_rows = at(own, ROWS, ROWS), at(oth, ROWS, ROWS)
    own_half, oth_half = at(core * HALF_WIDTH, HALF_WIDTH, 128), at((1 - core) * HALF_WIDTH, HALF_WIDTH, 128)
    length, group = length_ref[0], group_ref[0]
    gain1, shift1, gain2, shift2 = (
        ref[...].reshape(1, WIDTH) for ref in (gain1_ref, shift1_ref, gain2_ref, shift2_ref)
    )
    left, right = x == 0, x == 1

    def fetch(slot, src, dst):
        return pltpu.make_async_copy(src, dst, local_sem.at[slot])

    def weight_copies(name):
        if name == "qkv":
            return [
                fetch(i, w_qkv.at[:, at(i * WIDTH + core * HALF_WIDTH, HALF_WIDTH, 128)],
                      wq.at[:, pl.ds(i * HALF_WIDTH, HALF_WIDTH)])
                for i in range(3)
            ]
        if name == "proj":
            return [fetch(3, w_proj, wp)]
        if name == "up":
            return [fetch(4, w_up, wu)]
        return [fetch(5, w_down, wd)]

    def ask(*names):
        for name in names:
            for copy in weight_copies(name):
                copy.start()

    ask("qkv")

    def arrive(name):
        for copy in weight_copies(name):
            copy.wait()

    diagonal = device_at(z, y, 1 - x, 1 - core)
    yz_peers = [device_at((z + d) % 4, 1 - y, x, core) for d in (1, 2, 3)]
    peers = [mate, x_peer, diagonal, y_peer] + z_peers + yz_peers
    barrier = pltpu.get_barrier_semaphore()
    for peer in peers:
        pl.semaphore_signal(barrier, inc=1, device_id=peer, device_id_type=MESH)
    pl.semaphore_wait(barrier, len(peers))

    def misc(slot, src, dst, target):
        return pltpu.make_async_remote_copy(
            src_ref=src, dst_ref=dst, send_sem=misc_send.at[slot], recv_sem=misc_recv.at[slot],
            device_id=target, device_id_type=MESH,
        )

    tok_far = misc(0, tok, tokf.at[own_rows], x_peer)
    tok_mate = misc(1, tok, tokc, mate)
    tok_on = misc(2, tokf.at[own_rows], tokf.at[own_rows], mate)
    ups_mate = misc(3, ups.at[:, oth_half], outh.at[own_rows], mate)
    count_y = misc(4, cs.at[0], cr.at[0], y_peer)
    count_z = [misc(4 + d, cs.at[1], cr.at[d], z_peers[d - 1]) for d in (1, 2, 3)]
    att_rows = at(core * HALF_WIDTH, HALF_WIDTH, 128)
    att_mate = misc(8, attt.at[att_rows], attt.at[att_rows], mate)
    n2_mate = misc(9, n2.at[own_rows], n2.at[own_rows], mate)
    gel_mate = [
        misc(10 + i, gel.at[own_rows, pl.ds(1024 * i, 1024)], gel.at[own_rows, pl.ds(1024 * i, 1024)], mate)
        for i in range(3)
    ]
    up_mate = misc(13, upo.at[:, at((1 - core) * 1536, 1536, 128)], uph.at[own_rows], mate)
    hl_mate = misc(14, hl.at[own_rows], hl.at[own_rows], mate)
    nc_mate = misc(15, upo.at[:, :WIDTH], tokc, mate)
    nf_mate = misc(16, tokf.at[own_rows], tokf.at[own_rows], mate)
    nf_far = misc(17, tokf.at[own_rows], tokf.at[own_rows], x_peer)

    @pl.when(left)
    def _():
        tok_far.start()

    tok_mate.start()
    ups_mate.start()
    lane = lax.broadcasted_iota(jnp.int32, (8, 128), 1)
    cs[0] = jnp.where(lane == group, length.astype(F32), 0.0)
    count_y.start()
    ask("proj", "up", "down")

    def first_norm(src, src_at, dst, dst_at):
        def step(i):
            unit, _ = normalise(src[at(src_at + i * 64, 64, 64), :].astype(F32))
            dst[at(dst_at + i * 64, 64, 64), :] = (unit * gain1 + shift1).astype(BF16)

        loop(ROWS // 64, step, 0)

    first_norm(tok, 0, nc, own)
    tok_mate.wait()
    first_norm(tokc, 0, nc, oth)
    arrive("qkv")

    def project(i):
        part = dot_tt(wq[:, at(i * HALF_WIDTH, HALF_WIDTH, 128)], nc[...])
        qkvt[at(i * HALF_WIDTH, HALF_WIDTH, 128), :] = (part * jnp.where(i == 0, 0.125, 1.0)).astype(BF16)

    loop(3, project, 0)

    key_at = lax.broadcasted_iota(jnp.int32, (512, 512), 0)
    query_at = lax.broadcasted_iota(jnp.int32, (512, 512), 1)
    bias[...] = jnp.where((key_at <= query_at) & (key_at + x * 512 < length), 0.0, NEG_FILL).astype(BF16)

    def attend_chip(h):
        r = h * 64
        keys, queries, values = qkvt[at(HALF_WIDTH + r, 64, 64), :], qkvt[at(r, 64, 64), :], qkvt[at(2 * HALF_WIDTH + r, 64, 64), :]
        for half in (0, 1):
            span, cols = 256 * (half + 1), slice(256 * half, 256 * half + 256)
            scores = dot_tn(keys[:, :span], queries[:, cols]) + bias[:span, cols].astype(F32)
            peak = jnp.max(scores, axis=0, keepdims=True)
            expo = jnp.exp(scores - peak)
            expo_low = expo.astype(BF16)
            m1[pl.ds(h, 1), cols] = peak
            l1[pl.ds(h, 1), cols] = jnp.sum(expo_low.astype(F32), axis=0, keepdims=True)
            ec[h, :span, cols] = expo_low
            o1[at(r, 64, 64), cols] = dot_nn(values[:, :span], expo_low)

    loop(HALF_HEADS, attend_chip, 0)

    count_y.wait()
    cs[1] = cs[0] + cr[0]
    for copy in count_z:
        copy.start()
    for copy in count_z:
        copy.wait()
    counts = cs[1] + cr[1] + cr[2] + cr[3]
    total = jnp.sum(counts, axis=1, keepdims=True)
    mine = jnp.sum(jnp.where(lane == group, counts, 0.0), axis=1, keepdims=True)
    scale = (weight_ref[0].astype(F32) * total / (NGROUPS * mine))[0:1, 0:1]
    row_at = lax.broadcasted_iota(jnp.int32, (ROWS, 1), 0) + x * 512
    own_scale = jnp.where(row_at + own < length, scale, 0.0)
    oth_scale = jnp.where(row_at + oth < length, scale, 0.0)
    hl[own_rows, :] = (ups[...].astype(F32) * own_scale).astype(BF16)
    outh[own_rows, :] = (ups[:, own_half].astype(F32) * own_scale).astype(BF16)
    ups_mate.wait()
    outh[oth_rows, :] = (outh[oth_rows, :].astype(F32) * oth_scale).astype(BF16)

    @pl.when(right)
    def _():
        def far_block(start):
            first_norm(tokf, start, nf, start)
            columns = at(start, ROWS, ROWS)

            def project_far(i):
                part = dot_tt(wq[:, at((i + 1) * HALF_WIDTH, HALF_WIDTH, 128)], nf[columns, :])
                kvft[at(i * HALF_WIDTH, HALF_WIDTH, 128), columns] = part.astype(BF16)

            loop(2, project_far, 0)

        tok_far.wait_recv()
        tok_on.start()
        far_block(own)
        tok_on.wait()
        far_block(oth)

        def attend_far(h):
            r = h * 64
            keys, queries, values = kvft[at(r, 64, 64), :], qkvt[at(r, 64, 64), :], kvft[at(HALF_WIDTH + r, 64, 64), :]
            for half in (0, 1):
                cols = slice(256 * half, 256 * half + 256)
                scores = dot_tn(keys, queries[:, cols])
                peak = jnp.max(scores, axis=0, keepdims=True)
                expo = jnp.exp(scores - peak)
                expo_low = expo.astype(BF16)
                expo_sum = jnp.sum(expo_low.astype(F32), axis=0, keepdims=True)
                ef[h, :, cols] = expo_low
                out = dot_nn(values, expo_low)
                old = m1[pl.ds(h, 1), cols]
                top = jnp.maximum(old, peak)
                old_part, new_part = jnp.exp(old - top), jnp.exp(peak - top)
                share = 1.0 / (l1[pl.ds(h, 1), cols] * old_part + expo_sum * new_part)
                f1[pl.ds(h, 1), cols] = old_part * share
                f2[pl.ds(h, 1), cols] = new_part * share
                o1[at(r, 64, 64), cols] = o1[at(r, 64, 64), cols] * (old_part * share) + out * (new_part * share)

        loop(HALF_HEADS, attend_far, 0)

    @pl.when(left)
    def _():
        nf[...] = jnp.zeros_like(nf)
        mixf[...] = jnp.zeros_like(mixf)

        def share_out(h):
            share = 1.0 / l1[pl.ds(h, 1), :]
            f1[pl.ds(h, 1), :] = share
            f2[pl.ds(h, 1), :] = jnp.zeros_like(share)
            o1[at(h * 64, 64, 64), :] = o1[at(h * 64, 64, 64), :] * share

        loop(HALF_HEADS, share_out)

    attt[att_rows, :] = o1[...].astype(BF16)
    att_mate.start()
    arrive("proj")
    att_mate.wait()

    for i in range(3):
        cols = slice(256 * i, 256 * i + 256)
        hid[:, cols] = tok[:, cols].astype(F32) + dot_tn(attt[:, own_rows], wp[:, cols])

    def second_norm(i):
        unit, _ = normalise(hid[at(i * 64, 64, 64), :])
        n2[at(own + i * 64, 64, 64), :] = (unit * gain2 + shift2).astype(BF16)

    loop(ROWS // 64, second_norm, 0)
    n2_mate.start()
    arrive("up")
    for third in range(3):

        def feed(i, third=third):
            cols = at(third * 1024 + i * 256, 256, 256)
            u = dot_nn(n2[own_rows, :], wu[:, cols])
            square = u * u
            bend = jnp.tanh(GELU_COEF * (u + 0.044715 * square * u))
            lift = 0.5 * (1.0 + bend)
            gel[own_rows, cols] = (u * lift).astype(BF16)
            slope = lift + 0.5 * u * (1.0 - bend * bend) * (GELU_COEF * (1.0 + 3 * 0.044715 * square))
            dg[:, cols] = slope.astype(BF16)

        loop(4, feed, 0)
        gel_mate[third].start()

    grads = (g_dn, g_up, g_pr, g_qk)
    outs = (o_dn, o_up, o_pr, o_qk)
    came, sent = (c_dn, c_up, c_pr, c_qk), (s_dn, s_up, s_pr, s_qk)
    hs = (h_dn, h_up, h_pr, h_qk)

    def remote(src, dst, w, slot, target):
        return pltpu.make_async_remote_copy(
            src_ref=src, dst_ref=dst, send_sem=send_sem.at[w, slot], recv_sem=recv_sem.at[w, slot],
            device_id=target, device_id_type=MESH,
        )

    def part(ref, w, index, count=1):
        rows = BLOCKS[w][0]
        return ref.at[at(index * rows, count * rows, 16)]

    def value(ref, w, index):
        rows = BLOCKS[w][0]
        return ref[at(index * rows, rows, 16), :].astype(F32)

    def keep(ref, w, index, result):
        rows = BLOCKS[w][0]
        ref[at(index * rows, rows, 16), :] = result.astype(BF16)

    class PlaneFirst:
        def __init__(self, w, x_first):
            self.w, self.x_first = w, x_first
            self.first, self.second = (x_peer, y_peer) if x_first else (y_peer, x_peer)
            self.kept = y if x_first else x

        def block(self, zz, j, mine):
            side = (x if mine else 1 - x) if self.x_first else (y if mine else 1 - y)
            return zz * 4 + (j * 2 + side if self.x_first else side * 2 + j)

        def first_copies(self, places):
            w = self.w
            return [
                remote(part(grads[w], w, self.block(zz, j, False)), part(came[w], w, zz * 2 + j), w, zz * 2 + j, self.first)
                for zz in places
                for j in range(2)
            ]

        def second_copy(self):
            w = self.w
            return remote(part(sent[w], w, 0, 4), part(came[w], w, 8, 4), w, 8, self.second)

        def third_copies(self):
            w = self.w
            return [
                remote(part(sent[w], w, 3 + d), part(came[w], w, 11 + d), w, 8 + d, z_peers[d - 1])
                for d in (1, 2, 3)
            ]

        def after_first(self, zz, j):
            w = self.w
            return value(grads[w], w, self.block(zz, j, True)) + value(came[w], w, zz * 2 + j)

        def after_second(self, zz):
            return self.after_first(zz, self.kept) + value(came[self.w], self.w, 8 + zz)

        def start_second(self):
            for copy in self.first_copies(range(4)):
                copy.wait()
            for zz in range(4):
                keep(sent[self.w], self.w, zz, self.after_first(zz, 1 - self.kept))
            self.second_copy().start()

        def start_third(self):
            self.second_copy().wait()
            for d, copy in zip((1, 2, 3), self.third_copies()):
                keep(sent[self.w], self.w, 3 + d, self.after_second((z + d) % 4))
                copy.start()

        def total(self):
            w = self.w
            for copy in self.third_copies():
                copy.wait()
            return self.after_second(z) + value(came[w], w, 12) + value(came[w], w, 13) + value(came[w], w, 14)

    class LineFirst:
        def __init__(self, w, x_second):
            self.w, self.x_second = w, x_second
            self.second, self.third = (x_peer, y_peer) if x_second else (y_peer, x_peer)
            self.kept = y if x_second else x

        def place(self, i, mine):
            side = (x if mine else 1 - x) if self.x_second else (y if mine else 1 - y)
            return i * 2 + side if self.x_second else side * 2 + i

        def first_copy(self, d):
            w = self.w
            return remote(part(grads[w], w, (z + d) % 4 * 4, 4), part(came[w], w, 4 * d - 4, 4), w, d - 1, z_peers[d - 1])

        def second_copy(self):
            w = self.w
            return remote(part(sent[w], w, 0, 2), part(came[w], w, 12, 2), w, 8, self.second)

        def third_copy(self):
            w = self.w
            return remote(part(sent[w], w, 2), part(came[w], w, 14), w, 9, self.third)

        def after_first(self, i, mine):
            w, b = self.w, self.place(i, mine)
            whole = value(grads[w], w, z * 4 + b)
            for d in range(3):
                whole = whole + value(came[w], w, 4 * d + b)
            return whole

        def start_second(self):
            for d in (1, 2, 3):
                self.first_copy(d).wait()
            for i in range(2):
                keep(sent[self.w], self.w, i, self.after_first(i, False))
            self.second_copy().start()

        def start_third(self):
            self.second_copy().wait()
            i = 1 - self.kept
            keep(sent[self.w], self.w, 2, self.after_first(i, True) + value(came[self.w], self.w, 12 + i))
            self.third_copy().start()

        def total(self):
            w = self.w
            self.third_copy().wait()
            return self.after_first(self.kept, True) + value(came[w], w, 12 + self.kept) + value(came[w], w, 14)

    def plan(w, order):
        return LineFirst(w, order == "zxy") if order[0] == "z" else PlaneFirst(w, order[0] == "x")

    plans = [[plan(w, order) for order in ORDERS[w]] for w in range(4)]

    def each_core(w, step):
        if ORDERS[w][0] == ORDERS[w][1]:
            step(plans[w][0])
            return
        for which in (0, 1):
            pl.when(core == which)(lambda which=which: step(plans[w][which]))

    def start_first(w, places):
        def step(plan):
            if isinstance(plan, PlaneFirst):
                for copy in plan.first_copies(places):
                    copy.start()
            elif 3 in places:
                for d in (1, 2, 3):
                    plan.first_copy(d).start()

        each_core(w, step)

    def start_second(w):
        each_core(w, lambda plan: plan.start_second())

    def start_third(w):
        each_core(w, lambda plan: plan.start_third())

    def places(w):
        parts = 3 if w == 3 else 1
        width = BLOCKS[w][1] // parts
        return [(pl.ds(i * width, width), at((2 * i + core) * width, width, 128)) for i in range(parts)]

    def last_copies(w):
        return [
            remote(hs[w].at[:, src], outs[w].at[:, dst], w, 12 + i, mate)
            for i, (src, dst) in enumerate(places(w))
        ]

    def start_last(w):
        rows = BLOCKS[w][0] // 2

        def step(plan):
            whole = plan.total()
            low_core = core == 0
            hs[w][...] = jnp.where(low_core, whole[rows:], whole[:rows])
            mine = jnp.where(low_core, whole[:rows], whole[rows:])
            parts = 3 if w == 3 else 1
            width = BLOCKS[w][1] // parts
            for i, (_, dst) in enumerate(places(w)):
                outs[w][:, dst] = mine[:, i * width : (i + 1) * width]

        each_core(w, step)
        for copy in last_copies(w):
            copy.start()

    def finish(w):
        for copy in last_copies(w):
            copy.wait()

    for copy in gel_mate:
        copy.wait()
    for zz in range(4):

        def down_rows(i, zz=zz):
            start = zz * WIDTH + i * 256
            g_dn[at(start, 256, 256), :] = dot_tn(gel[:, at(start, 256, 256)], outh[...]).astype(BF16)

        loop(3, down_rows, 0)
        start_first(0, (zz,))

    arrive("down")

    def gelu_back(cols):
        up_cot = dot_nt(hl[own_rows, :], wd[cols, :]) * dg[:, cols].astype(F32)
        up_cot = up_cot.astype(BF16)
        upo[:, cols] = up_cot
        return up_cot

    def back_other(i):
        gelu_back(at((1 - core) * 1536 + i * 256, 256, 256))

    def back_own(i):
        uph[own_rows, at(i * 256, 256, 256)] = gelu_back(at(core * 1536 + i * 256, 256, 256))

    loop(6, back_other, 0)
    up_mate.start()
    loop(6, back_own, 0)

    def n2_back(i):
        cols = at(i * 256, 256, 256)
        ncot[:, cols] = dot_nt(upo[...], wu[cols, :])

    loop(3, n2_back, 0)
    vsend[...] = jnp.zeros_like(vsend)

    def second_back(i):
        rows = at(i * 64, 64, 64)
        unit, inverse = normalise(hid[rows, :])
        cot = ncot[rows, :]
        position = lax.broadcasted_iota(jnp.int32, (64, 1), 0) + i * 64 + x * 512 + own
        out_cot = ups[rows, :].astype(F32) * jnp.where(position < length, scale, 0.0)
        hidden_cot = out_cot + normalise_back(cot, gain2, unit, inverse)
        hc[rows, :] = hidden_cot
        hl[at(own + i * 64, 64, 64), :] = hidden_cot.astype(BF16)
        vsend[0, 2:3, :] += jnp.sum(cot * unit, axis=0, keepdims=True)
        vsend[0, 3:4, :] += jnp.sum(cot, axis=0, keepdims=True)

    loop(ROWS // 64, second_back, 0)
    hl_mate.start()

    n2_mate.wait()
    up_mate.wait()
    for half in range(2):

        def up_columns(i, half=half):
            cols = at(i * 512, 512, 512)
            rows = slice(384 * half, 384 * half + 384)
            g_up[rows, cols] = dot_tn(n2[:, rows], uph[:, cols]).astype(BF16)

        loop(3, up_columns, 0)
        start_first(1, (2 * half, 2 * half + 1))

    hl_mate.wait()

    def proj_rows(i):
        rows = at(i * 256, 256, 256)
        g_pr[rows, :] = dot_nn(attt[rows, :], hl[:, own_half]).astype(BF16)

    loop(3, proj_rows, 0)
    start_first(2, range(4))
    attt[att_rows, :] = dot_nt(wp[att_rows, :], hl[...]).astype(BF16)

    def attend_back(h):
        r = h * 64
        rows = at(r, 64, 64)
        keys, queries, values = qkvt[at(HALF_WIDTH + r, 64, 64), :], qkvt[rows, :], qkvt[at(2 * HALF_WIDTH + r, 64, 64), :]
        cot = attt[at(core * HALF_WIDTH + r, 64, 64), :].astype(F32)
        near = (cot * f1[pl.ds(h, 1), :]).astype(BF16)
        delta = jnp.sum(near.astype(F32) * o1[rows, :], axis=0, keepdims=True)
        far = (cot * f2[pl.ds(h, 1), :]).astype(BF16)
        far_delta = jnp.sum(far.astype(F32) * o1[rows, :], axis=0, keepdims=True)
        key_terms, value_terms = [], []
        for half in (0, 1):
            span, cols = 256 * (half + 1), slice(256 * half, 256 * half + 256)
            expo = ec[h, :span, cols]
            prob_cot = dot_tn(values[:, :span], near[:, cols])
            score_cot = (expo.astype(F32) * (prob_cot - delta[:, cols])).astype(BF16)
            o1[rows, cols] = dot_nn(keys[:, :span], score_cot)
            key_terms.append(dot_nt(queries[:, cols], score_cot))
            value_terms.append(dot_nt(near[:, cols], expo))
        for start, terms in ((HALF_WIDTH, key_terms), (2 * HALF_WIDTH, value_terms)):
            mixc[at(start + r, 64, 64), :256] = (terms[0] + terms[1][:, :256]).astype(BF16)
            mixc[at(start + r, 64, 64), 256:] = terms[1][:, 256:].astype(BF16)

        @pl.when(right)
        def _():
            far_keys, far_values = kvft[rows, :], kvft[at(HALF_WIDTH + r, 64, 64), :]
            expo = ef[h]
            prob_cot = dot_tn(far_values, far)
            score_cot = (expo.astype(F32) * (prob_cot - far_delta)).astype(BF16)
            o1[rows, :] += dot_nn(far_keys, score_cot)
            mixf[rows, :] = dot_nt(queries, score_cot).astype(BF16)
            mixf[at(HALF_WIDTH + r, 64, 64), :] = dot_nt(far, expo).astype(BF16)

        mixc[rows, :] = (o1[rows, :] * 0.125).astype(BF16)

    def attend_back_late(h):
        attend_back(h + 3)

    loop(3, attend_back, 0)
    loop(3, attend_back_late, 0)

    def normed_cot(mixed, first_column, columns, store):
        def step(i):
            rows = at(i * 256, 256, 256)
            store(rows, dot_tt(mixed[:, columns], wq[rows, first_column:]))

        loop(3, step, 0)

    def store_to(ref, rows):
        def store(cols, value):
            ref[rows, cols] = value.astype(ref.dtype)

        return store

    @pl.when(right)
    def _():
        normed_cot(mixf, HALF_WIDTH, oth_rows, store_to(tokf, own_rows))
        nf_mate.start()

    for half in range(2):
        cols = slice(384 * half, 384 * half + 384)
        g_qk[cols, :384] = dot_tt(nc[:, cols], mixc[:384, :]).astype(BF16)
        for i in range(2):
            g_qk[cols, 384 * (i + 1) : 384 * (i + 2)] = (
                dot_tt(nc[:, cols], mixc[384 * (i + 1) : 384 * (i + 2), :])
                + dot_tt(nf[:, cols], mixf[384 * i : 384 * (i + 1), :])
            ).astype(BF16)
        start_first(3, (2 * half, 2 * half + 1))

    normed_cot(mixc, 0, oth_rows, store_to(upo, at(0, ROWS, ROWS)))
    nc_mate.start()

    @pl.when(right)
    def _():
        normed_cot(mixf, HALF_WIDTH, own_rows, store_to(ncot, at(0, ROWS, ROWS)))
        nf_mate.wait()
        tokf[own_rows, :] = (ncot[...] + tokf[oth_rows, :].astype(F32)).astype(BF16)
        nf_far.start()

    normed_cot(mixc, 0, own_rows, store_to(ncot, at(0, ROWS, ROWS)))

    def block_rows(i):
        cols = at(i * 256, 256, 256)
        block_out[:, cols] = (hid[:, cols] + dot_nn(gel[own_rows, :], wd[:, cols])).astype(BF16)

    loop(3, block_rows, 0)
    start_second(0)
    start_second(1)
    start_second(2)
    start_third(0)
    nc_mate.wait()
    start_third(1)

    @pl.when(left)
    def _():
        nf_far.wait_recv()
        tok_far.wait_send()

    @pl.when(right)
    def _():
        nf_far.wait_send()

    def first_back(i):
        rows = at(i * 64, 64, 64)
        unit, inverse = normalise(tok[rows, :].astype(F32))
        near = tokc[rows, :].astype(F32)
        far = tokf[at(own + i * 64, 64, 64), :].astype(F32)
        cot = ncot[rows, :] + near + jnp.where(left, far, 0.0)
        input_grad[rows, :] = (hc[rows, :] + normalise_back(cot, gain1, unit, inverse)).astype(BF16)
        vsend[0, 0:1, :] += jnp.sum(cot * unit, axis=0, keepdims=True)
        vsend[0, 1:2, :] += jnp.sum(cot, axis=0, keepdims=True)

    loop(ROWS // 64, first_back, 0)

    clip_peers = [mate, x_peer, diagonal]
    other_clips = [y_peer] + z_peers + yz_peers

    def clip_sum(i):
        return misc(18 + i, vsend.at[0], vrecv.at[i], clip_peers[i])

    def all_sum(i):
        return misc(21 + i, vsend.at[1], vrecv.at[3 + i], other_clips[i])

    for i in range(3):
        clip_sum(i).start()
    start_second(3)
    start_third(2)
    for i in range(3):
        clip_sum(i).wait()
    vsend[1] = vsend[0] + vrecv[0] + vrecv[1] + vrecv[2]
    for i in range(7):
        all_sum(i).start()
    start_last(0)
    start_third(3)
    for i in range(7):
        all_sum(i).wait()
    sums = vsend[1]
    for i in range(7):
        sums = sums + vrecv[3 + i]
    rank = dp * 4 + ctx
    o_vec[...] = pltpu.roll(sums, lax.rem(WIDTH - rank * 24, WIDTH), 1)[:, :128]
    start_last(1)
    start_last(2)
    start_last(3)
    for w in range(4):
        finish(w)


def hand_out_kernel(
    block_out, input_grad, qk, pr, up, dn, vec,
    o_block, o_input, o_v0, o_v1, o_qk, o_pr, o_v2, o_v3, o_up, o_dn, sem,
):
    pairs = ((block_out, o_block), (input_grad, o_input), (qk, o_qk), (pr, o_pr), (up, o_up), (dn, o_dn))
    copies = [pltpu.make_async_copy(src, dst, sem.at[i]) for i, (src, dst) in enumerate(pairs)]
    for copy in copies:
        copy.start()
    for i, ref in enumerate((o_v0, o_v1, o_v2, o_v3)):
        ref[...] = vec[i, :24]
    for copy in copies:
        copy.wait()


def fused_layer(args):
    vmem, smem, anywhere = (
        pl.BlockSpec(memory_space=pltpu.VMEM),
        pl.BlockSpec(memory_space=pltpu.SMEM),
        pl.BlockSpec(memory_space=pl.ANY),
    )

    def low(*shape):
        return pltpu.VMEM(shape, BF16)

    def full(*shape):
        return pltpu.VMEM(shape, F32)

    def per_block(count):
        return [low(count * rows, width) for rows, width in BLOCKS]

    vector = jax.ShapeDtypeStruct((24,), F32)

    def grad_shape(w):
        return jax.ShapeDtypeStruct((BLOCKS[w][0] // 2, BLOCKS[w][1] * 2), F32)

    rows_out = jax.ShapeDtypeStruct((ROWS, WIDTH), BF16)
    made = pl.pallas_call(
        layer_kernel,
        out_shape=[
            rows_out, rows_out, grad_shape(3), grad_shape(2), grad_shape(1), grad_shape(0),
            jax.ShapeDtypeStruct((8, 128), F32),
        ],
        in_specs=[smem] * 3 + [vmem] * 6 + [anywhere] * 4,
        out_specs=[vmem] * 7,
        scratch_shapes=[
            low(768, 1152), low(768, 768), low(768, 3072), low(3072, 768),
            low(256, 768), low(512, 768), low(512, 768), low(512, 768),
            low(1152, 512), low(768, 512), low(512, 512), low(6, 512, 512), low(6, 512, 512),
            full(384, 512), full(8, 512), full(8, 512), full(8, 512), full(8, 512),
            low(768, 512), full(256, 768), low(512, 768), low(512, 3072), low(256, 3072),
            low(512, 384), low(256, 3072), low(512, 1536), full(256, 768),
            full(256, 768), low(512, 768), low(1152, 512), low(768, 512),
            full(2, 8, 128), full(4, 8, 128), full(2, 8, 768), full(10, 8, 768),
            low(3072, 384), low(768, 1536), low(768, 384), low(768, 1152),
        ]
        + per_block(15) + per_block(7)
        + [pltpu.VMEM((block[0] // 2, block[1]), F32) for block in BLOCKS]
        + [
            pltpu.SemaphoreType.DMA((4, 15)),
            pltpu.SemaphoreType.DMA((4, 15)),
            pltpu.SemaphoreType.DMA((28,)),
            pltpu.SemaphoreType.DMA((28,)),
            pltpu.SemaphoreType.DMA((6,)),
        ],
        compiler_params=pltpu.CompilerParams(
            collective_id=0, has_side_effects=True, vmem_limit_bytes=60 * 1024 * 1024
        ),
    )(*args)
    return pl.pallas_call(
        hand_out_kernel,
        out_shape=[
            rows_out, rows_out, vector, vector, grad_shape(3), grad_shape(2), vector, vector,
            grad_shape(1), grad_shape(0),
        ],
        in_specs=[vmem] * 7,
        out_specs=[anywhere] * 2 + [vmem] * 2 + [anywhere] * 2 + [vmem] * 2 + [anywhere] * 2,
        scratch_shapes=[pltpu.SemaphoreType.DMA((6,))],
        compiler_params=pltpu.CompilerParams(vmem_limit_bytes=60 * 1024 * 1024),
    )(*made)


def general_body(
    tokens,
    attn_gain,
    attn_shift,
    w_qkv,
    w_proj,
    mlp_gain,
    mlp_shift,
    w_up,
    w_down,
    upstream,
    clip_length,
    dataset_group,
    sample_weight,
):
    tok_rows = tokens.shape[0]
    model_width = tokens.shape[1]
    head_count = model_width // HD
    ctx_count = lax.axis_size("ctx")
    seq_rows = tok_rows * ctx_count
    first_row = lax.axis_index("ctx") * tok_rows
    length = clip_length[0]
    key_span = min(seq_rows, max(tok_rows, 512))
    block_count = seq_rows // key_span
    query_pos = first_row + jnp.arange(tok_rows, dtype=jnp.int32)
    last_pos = first_row + tok_rows - 1
    onehot = (dataset_group[0, 0] == jnp.arange(NGROUPS, dtype=jnp.int32)).astype(jnp.float32)
    counts = lax.psum(onehot * length.astype(jnp.float32), "dp")
    total_all = jnp.sum(counts)
    clip_scale = (
        sample_weight[0].astype(jnp.float32) * total_all / (NGROUPS * jnp.sum(onehot * counts))
    )
    x_rows = tokens.astype(jnp.float32)
    normed, norm_one_back = jax.vjp(layer_norm, x_rows, attn_gain, attn_shift)
    normed_low = normed.astype(jnp.bfloat16)
    mixed_qkv = jnp.dot(normed_low, w_qkv, preferred_element_type=jnp.float32).astype(jnp.bfloat16)
    queries = mixed_qkv[:, :model_width]
    key_local = mixed_qkv[:, model_width : 2 * model_width]
    value_local = mixed_qkv[:, 2 * model_width :]
    key_all, value_all = (
        lax.all_gather(key_local, "ctx", axis=0, tiled=True),
        lax.all_gather(value_local, "ctx", axis=0, tiled=True),
    )
    queries3 = queries.reshape(tok_rows, head_count, HD)

    def scores_for(kstart, key_rows):
        piece = key_rows[kstart : kstart + key_span].reshape(key_span, head_count, HD)
        raw = (
            jnp.einsum("qhd,khd->hqk", queries3, piece, preferred_element_type=jnp.float32) * 0.125
        )
        key_pos = kstart + jnp.arange(key_span, dtype=jnp.int32)
        allowed = (key_pos[None, :] <= query_pos[:, None]) & (key_pos[None, :] < length)
        return (jnp.where(allowed[None], raw, NEG_FILL), allowed)

    def useful(kstart):
        return (kstart <= last_pos) & (kstart < length)

    peak = jnp.full((head_count, tok_rows), NEG_FILL, jnp.float32)
    exp_total = jnp.zeros((head_count, tok_rows), jnp.float32)
    for index in range(block_count):
        kstart = index * key_span

        def gather_stats(carry, kstart=kstart):
            old_peak, old_total = carry
            scores, allowed = scores_for(kstart, key_all)
            new_peak = jnp.maximum(old_peak, jnp.max(scores, axis=-1))
            expo_vals = jnp.where(allowed[None], jnp.exp(scores - new_peak[..., None]), 0.0)
            return (
                new_peak,
                old_total * jnp.exp(old_peak - new_peak) + jnp.sum(expo_vals, axis=-1),
            )

        peak, exp_total = lax.cond(
            useful(kstart), gather_stats, lambda carry: carry, (peak, exp_total)
        )

    def probs_for(kstart, key_rows):
        scores, allowed = scores_for(kstart, key_rows)
        return (
            jnp.where(allowed[None], jnp.exp(scores - peak[..., None]), 0.0) / exp_total[..., None]
        )

    out_high = jnp.zeros((tok_rows, head_count, HD), jnp.float32)
    out_rest = jnp.zeros((tok_rows, head_count, HD), jnp.float32)
    for index in range(block_count):
        kstart = index * key_span

        def add_values(carry, kstart=kstart):
            high_acc, rest_acc = carry
            probs = probs_for(kstart, key_all)
            probs_low = probs.astype(jnp.bfloat16)
            remainder = (probs - probs_low.astype(jnp.float32)).astype(jnp.bfloat16)
            piece = value_all[kstart : kstart + key_span].reshape(key_span, head_count, HD)
            high_acc = high_acc + jnp.einsum(
                "hqk,khd->qhd", probs_low, piece, preferred_element_type=jnp.float32
            )
            rest_acc = rest_acc + jnp.einsum(
                "hqk,khd->qhd", remainder, piece, preferred_element_type=jnp.float32
            )
            return (high_acc, rest_acc)

        out_high, out_rest = lax.cond(
            useful(kstart), add_values, lambda carry: carry, (out_high, out_rest)
        )
    attended_low = out_high.reshape(tok_rows, model_width).astype(jnp.bfloat16)
    out_full = out_high + out_rest
    hidden = x_rows + jnp.dot(attended_low, w_proj, preferred_element_type=jnp.float32)
    normed_two, norm_two_back = jax.vjp(layer_norm, hidden, mlp_gain, mlp_shift)
    normed_two_low = normed_two.astype(jnp.bfloat16)
    up_proj = jnp.dot(normed_two_low, w_up, preferred_element_type=jnp.float32)
    gelu_vals, gelu_back = jax.vjp(gelu, up_proj)
    gelu_low = gelu_vals.astype(jnp.bfloat16)
    block_out = (hidden + jnp.dot(gelu_low, w_down, preferred_element_type=jnp.float32)).astype(
        jnp.bfloat16
    )
    valid = query_pos < length
    out_cot = upstream.astype(jnp.float32) * jnp.where(valid, clip_scale, 0.0)[:, None]
    out_cot_low = out_cot.astype(jnp.bfloat16)
    down_grad = jnp.einsum("tf,td->fd", gelu_low, out_cot_low, preferred_element_type=jnp.float32)
    gelu_in = jnp.einsum("td,fd->tf", out_cot_low, w_down, preferred_element_type=jnp.float32)
    (up_cot,) = gelu_back(gelu_in)
    up_cot_low = up_cot.astype(jnp.bfloat16)
    up_grad = jnp.einsum(
        "td,tf->df", normed_two_low, up_cot_low, preferred_element_type=jnp.float32
    )
    normed_two_cot = jnp.einsum("tf,df->td", up_cot_low, w_up, preferred_element_type=jnp.float32)
    norm_two_rows, mlp_gain_grad, mlp_shift_grad = norm_two_back(normed_two_cot)
    hidden_cot = out_cot + norm_two_rows
    hidden_cot_low = hidden_cot.astype(jnp.bfloat16)
    proj_grad = jnp.einsum(
        "ti,to->io", attended_low, hidden_cot_low, preferred_element_type=jnp.float32
    )
    attended_cot = jnp.einsum(
        "to,io->ti", hidden_cot_low, w_proj, preferred_element_type=jnp.float32
    ).astype(jnp.bfloat16)
    attended_cot3 = attended_cot.reshape(tok_rows, head_count, HD)
    delta = jnp.einsum("qhd,qhd->hq", attended_cot3.astype(jnp.float32), out_full)
    key_back, value_back = (key_all, value_all)
    query_cot = jnp.zeros((tok_rows, head_count, HD), jnp.float32)
    key_pieces = []
    value_pieces = []
    empty_piece = jnp.zeros((key_span, head_count, HD), jnp.float32)
    for index in range(block_count):
        kstart = index * key_span

        def block_grads(q_acc, kstart=kstart):
            probs = probs_for(kstart, key_back)
            probs_low = probs.astype(jnp.bfloat16)
            key_piece = key_back[kstart : kstart + key_span].reshape(key_span, head_count, HD)
            value_piece = value_back[kstart : kstart + key_span].reshape(key_span, head_count, HD)
            prob_cot = jnp.einsum(
                "qhd,khd->hqk", attended_cot3, value_piece, preferred_element_type=jnp.float32
            )
            score_cot = (probs * (prob_cot - delta[..., None])).astype(jnp.bfloat16)
            q_acc = (
                q_acc
                + jnp.einsum(
                    "hqk,khd->qhd", score_cot, key_piece, preferred_element_type=jnp.float32
                )
                * 0.125
            )
            key_term = (
                jnp.einsum("hqk,qhd->khd", score_cot, queries3, preferred_element_type=jnp.float32)
                * 0.125
            )
            value_term = jnp.einsum(
                "hqk,qhd->khd", probs_low, attended_cot3, preferred_element_type=jnp.float32
            )
            return (q_acc, key_term, value_term)

        query_cot, key_term, value_term = lax.cond(
            useful(kstart), block_grads, lambda q_acc: (q_acc, empty_piece, empty_piece), query_cot
        )
        key_pieces.append(key_term.reshape(key_span, model_width))
        value_pieces.append(value_term.reshape(key_span, model_width))
    key_terms = jnp.concatenate(key_pieces, axis=0)
    value_terms = jnp.concatenate(value_pieces, axis=0)
    key_cot, value_cot = (
        lax.psum_scatter(
            key_terms.astype(jnp.bfloat16), "ctx", scatter_dimension=0, tiled=True
        ).astype(jnp.float32),
        lax.psum_scatter(
            value_terms.astype(jnp.bfloat16), "ctx", scatter_dimension=0, tiled=True
        ).astype(jnp.float32),
    )
    mixed_cot = jnp.concatenate(
        [query_cot.reshape(tok_rows, model_width), key_cot, value_cot], axis=1
    ).astype(jnp.bfloat16)
    qkv_grad = jnp.einsum("td,te->de", normed_low, mixed_cot, preferred_element_type=jnp.float32)
    normed_cot = jnp.einsum("te,de->td", mixed_cot, w_qkv, preferred_element_type=jnp.float32)
    norm_one_rows, attn_gain_grad, attn_shift_grad = norm_one_back(normed_cot)
    input_grad = (hidden_cot + norm_one_rows).astype(jnp.bfloat16)
    reduced = (
        lax.psum_scatter(attn_gain_grad, ("dp", "ctx"), scatter_dimension=0, tiled=True),
        lax.psum_scatter(attn_shift_grad, ("dp", "ctx"), scatter_dimension=0, tiled=True),
        lax.psum_scatter(qkv_grad, ("dp", "ctx"), scatter_dimension=0, tiled=True),
        lax.psum_scatter(proj_grad, ("dp", "ctx"), scatter_dimension=0, tiled=True),
        lax.psum_scatter(mlp_gain_grad, ("dp", "ctx"), scatter_dimension=0, tiled=True),
        lax.psum_scatter(mlp_shift_grad, ("dp", "ctx"), scatter_dimension=0, tiled=True),
        lax.psum_scatter(up_grad, ("dp", "ctx"), scatter_dimension=0, tiled=True),
        lax.psum_scatter(down_grad, ("dp", "ctx"), scatter_dimension=0, tiled=True),
    )
    return (
        block_out,
        input_grad,
        reduced[0],
        reduced[1],
        reduced[2],
        reduced[3],
        reduced[4],
        reduced[5],
        reduced[6],
        reduced[7],
    )


def fused_body(
    tokens, attn_gain, attn_shift, w_qkv, w_proj, mlp_gain, mlp_shift, w_up, w_down, upstream,
    clip_length, dataset_group, sample_weight,
):
    outs = fused_layer(
        [clip_length, dataset_group.reshape(1), sample_weight, tokens, upstream]
        + [attn_gain, attn_shift, mlp_gain, mlp_shift, w_qkv, w_proj, w_up, w_down]
    )
    return tuple(outs)


def solution(mesh):
    in_specs = (
        P(("dp", "ctx"), None),
        P(),
        P(),
        P(),
        P(),
        P(),
        P(),
        P(),
        P(),
        P(("dp", "ctx"), None),
        P("dp"),
        P("dp", None),
        P("dp"),
    )
    out_specs = (
        P(("dp", "ctx"), None),
        P(("dp", "ctx"), None),
        P(("dp", "ctx")),
        P(("dp", "ctx")),
        P(("dp", "ctx"), None),
        P(("dp", "ctx"), None),
        P(("dp", "ctx")),
        P(("dp", "ctx")),
        P(("dp", "ctx"), None),
        P(("dp", "ctx"), None),
    )
    fused = mesh.shape["dp"] == 8 and mesh.shape["ctx"] == 4
    body = fused_body if fused else general_body
    return jax.shard_map(body, mesh=mesh, in_specs=in_specs, out_specs=out_specs, check_vma=False)
```

```python
import jax
import jax.numpy as jnp
from jax import lax
from jax.experimental import pallas as pl
from jax.experimental.pallas import tpu as pltpu
from jax.sharding import PartitionSpec as P

HD = 64
NGROUPS = 4


EPSILON = 1e-05
NEG_FILL = -1e30
GELU_COEF = 0.7978845608028654


def layer_norm(values, gain_vec, shift_vec):
    average = jnp.mean(values, axis=-1, keepdims=True)
    centred = values - average
    spread = jnp.mean(centred * centred, axis=-1, keepdims=True)
    return centred * lax.rsqrt(spread + EPSILON) * gain_vec + shift_vec


def gelu(inputs):
    return (
        0.5 * inputs * (1.0 + jnp.tanh(GELU_COEF * (inputs + 0.044715 * inputs * inputs * inputs)))
    )


MESH = pl.DeviceIdType.MESH
BF16 = jnp.bfloat16
F32 = jnp.float32
ROWS = 256
WIDTH = 768
HIDDEN = 3072
HALF_HEADS = 6
HALF_WIDTH = 384
BLOCKS = ((192, 384), (48, 1536), (48, 384), (48, 1152))
ORDERS = (('zyx', 'xyz'), ('yxz', 'xyz'), ('zyx', 'zxy'), ('yxz', 'xyz'))


def dot_nn(left, right):
    return lax.dot_general(left, right, (((1,), (0,)), ((), ())), preferred_element_type=F32)


def dot_nt(left, right):
    return lax.dot_general(left, right, (((1,), (1,)), ((), ())), preferred_element_type=F32)


def dot_tn(left, right):
    return lax.dot_general(left, right, (((0,), (0,)), ((), ())), preferred_element_type=F32)


def dot_tt(left, right):
    return lax.dot_general(left, right, (((0,), (1,)), ((), ())), preferred_element_type=F32)


def device_at(z, y, x, core):
    return (z * 2 + y, x * 2 + core)


def normalise(values):
    average = jnp.mean(values, axis=-1, keepdims=True)
    centred = values - average
    spread = jnp.mean(centred * centred, axis=-1, keepdims=True)
    inverse = lax.rsqrt(spread + EPSILON)
    return centred * inverse, inverse


def normalise_back(cot, gain, unit, inverse):
    scaled = cot * gain
    first = jnp.mean(scaled, axis=-1, keepdims=True)
    second = jnp.mean(scaled * unit, axis=-1, keepdims=True)
    return inverse * (scaled - first - unit * second)


def loop(count, step, unroll=1):
    if unroll == 0:
        for i in range(count):
            step(i)
        return

    def wrapped(index, carry):
        step(index)
        return carry

    lax.fori_loop(0, count, wrapped, 0, unroll=unroll)


def at(start, size, unit):
    return pl.ds(pl.multiple_of(start, unit), size)


def layer_kernel(
    length_ref, group_ref, weight_ref, tok_in, ups_in, gain1_ref, shift1_ref, gain2_ref, shift2_ref,
    w_qkv, w_proj, w_up, w_down,
    block_out, input_grad, o_qk, o_pr, o_up, o_dn, o_vec,
    tok, ups, wq, wp, wu, wd, tokc, tokf, nc, nf, qkvt, kvft, bias, ec, ef, o1, m1, l1, f1, f2,
    attt, hid, n2, gel, dg, outh, upo, uph, ncot, hc, hl, mixc, mixf,
    cs, cr, vsend, vrecv,
    g_dn, g_up, g_pr, g_qk,
    c_dn, c_up, c_pr, c_qk, s_dn, s_up, s_pr, s_qk, h_dn, h_up, h_pr, h_qk,
    send_sem, recv_sem, misc_send, misc_recv, local_sem,
):
    dp, ctx = lax.axis_index("dp"), lax.axis_index("ctx")
    z, y, x, core = dp // 2, dp % 2, ctx // 2, ctx % 2
    mate = device_at(z, y, x, 1 - core)
    x_peer = device_at(z, y, 1 - x, core)
    y_peer = device_at(z, 1 - y, x, core)
    z_peers = [device_at((z + d) % 4, y, x, core) for d in (1, 2, 3)]
    own, oth = core * ROWS, (1 - core) * ROWS
    own_rows, oth_rows = at(own, ROWS, ROWS), at(oth, ROWS, ROWS)
    own_half, oth_half = at(core * HALF_WIDTH, HALF_WIDTH, 128), at((1 - core) * HALF_WIDTH, HALF_WIDTH, 128)
    length, group = length_ref[0], group_ref[0]
    gain1, shift1, gain2, shift2 = (
        ref[...].reshape(1, WIDTH) for ref in (gain1_ref, shift1_ref, gain2_ref, shift2_ref)
    )
    left, right = x == 0, x == 1

    def fetch(slot, src, dst):
        return pltpu.make_async_copy(src, dst, local_sem.at[slot])

    def weight_copies(name):
        if name == "qkv":
            return [
                fetch(i, w_qkv.at[:, at(i * WIDTH + core * HALF_WIDTH, HALF_WIDTH, 128)],
                      wq.at[:, pl.ds(i * HALF_WIDTH, HALF_WIDTH)])
                for i in range(3)
            ]
        if name == "proj":
            return [fetch(3, w_proj, wp)]
        if name == "up":
            return [fetch(4, w_up, wu)]
        return [fetch(5, w_down, wd)]

    def ask(*names):
        for name in names:
            for copy in weight_copies(name):
                copy.start()

    rows_in = [fetch(6, tok_in, tok), fetch(7, ups_in, ups)]
    rows_in[0].start()
    ask("qkv")
    rows_in[1].start()

    def arrive(name):
        for copy in weight_copies(name):
            copy.wait()

    diagonal = device_at(z, y, 1 - x, 1 - core)
    yz_peers = [device_at((z + d) % 4, 1 - y, x, core) for d in (1, 2, 3)]
    peers = [mate, x_peer, diagonal, y_peer] + z_peers + yz_peers
    barrier = pltpu.get_barrier_semaphore()
    for peer in peers:
        pl.semaphore_signal(barrier, inc=1, device_id=peer, device_id_type=MESH)
    pl.semaphore_wait(barrier, len(peers))

    def misc(slot, src, dst, target):
        return pltpu.make_async_remote_copy(
            src_ref=src, dst_ref=dst, send_sem=misc_send.at[slot], recv_sem=misc_recv.at[slot],
            device_id=target, device_id_type=MESH,
        )

    def piece(i, start=0):
        return at(start + i * 128, 128, 128)

    tok_far = [misc(28 + i, tok_in.at[piece(i)], tokf.at[piece(i, own)], x_peer) for i in range(2)]
    tok_mate = misc(1, tok_in, tokc, mate)
    tok_on = [misc(30 + i, tokf.at[piece(i, own)], tokf.at[piece(i, own)], mate) for i in range(2)]
    ups_mate = misc(3, ups_in.at[:, oth_half], outh.at[own_rows], mate)
    count_y = misc(4, cs.at[0], cr.at[0], y_peer)
    count_z = [misc(4 + d, cs.at[1], cr.at[d], z_peers[d - 1]) for d in (1, 2, 3)]
    att_rows = at(core * HALF_WIDTH, HALF_WIDTH, 128)
    att_mate = misc(8, attt.at[att_rows], attt.at[att_rows], mate)
    n2_mate = misc(9, n2.at[own_rows], n2.at[own_rows], mate)
    gel_mate = [
        misc(10 + i, gel.at[own_rows, pl.ds(1024 * i, 1024)], gel.at[own_rows, pl.ds(1024 * i, 1024)], mate)
        for i in range(3)
    ]
    up_mate = misc(13, upo.at[:, at((1 - core) * 1536, 1536, 128)], uph.at[own_rows], mate)
    hl_mate = misc(14, hl.at[own_rows], hl.at[own_rows], mate)
    nc_mate = misc(15, upo.at[:, :WIDTH], tokc, mate)
    nf_mate = misc(16, tokf.at[own_rows], tokf.at[own_rows], mate)
    nf_far = misc(17, tokf.at[own_rows], tokf.at[own_rows], x_peer)

    @pl.when(left)
    def _():
        for copy in tok_far:
            copy.start()

    tok_mate.start()
    ups_mate.start()
    lane = lax.broadcasted_iota(jnp.int32, (8, 128), 1)
    cs[0] = jnp.where(lane == group, length.astype(F32), 0.0)
    count_y.start()
    ask("proj", "up", "down")

    def first_norm(src, src_at, dst, dst_at, count=ROWS // 64):
        def step(i):
            unit, _ = normalise(src[at(src_at + i * 64, 64, 64), :].astype(F32))
            dst[at(dst_at + i * 64, 64, 64), :] = (unit * gain1 + shift1).astype(BF16)

        loop(count, step, 0)

    rows_in[0].wait()
    first_norm(tok, 0, nc, own)
    tok_mate.wait()
    first_norm(tokc, 0, nc, oth)
    arrive("qkv")

    def project(i):
        part = dot_tt(wq[:, at(i * HALF_WIDTH, HALF_WIDTH, 128)], nc[...])
        qkvt[at(i * HALF_WIDTH, HALF_WIDTH, 128), :] = (part * jnp.where(i == 0, 0.125, 1.0)).astype(BF16)

    loop(3, project, 0)

    key_at = lax.broadcasted_iota(jnp.int32, (512, 512), 0)
    query_at = lax.broadcasted_iota(jnp.int32, (512, 512), 1)
    bias[...] = jnp.where((key_at <= query_at) & (key_at + x * 512 < length), 0.0, NEG_FILL).astype(BF16)

    def attend_chip(h):
        r = h * 64
        keys, queries, values = qkvt[at(HALF_WIDTH + r, 64, 64), :], qkvt[at(r, 64, 64), :], qkvt[at(2 * HALF_WIDTH + r, 64, 64), :]
        for half in (0, 1):
            span, cols = 256 * (half + 1), slice(256 * half, 256 * half + 256)
            scores = dot_tn(keys[:, :span], queries[:, cols]) + bias[:span, cols].astype(F32)
            peak = jnp.max(scores, axis=0, keepdims=True)
            expo = jnp.exp(scores - peak)
            expo_low = expo.astype(BF16)
            m1[pl.ds(h, 1), cols] = peak
            l1[pl.ds(h, 1), cols] = jnp.sum(expo_low.astype(F32), axis=0, keepdims=True)
            ec[h, :span, cols] = expo_low
            o1[at(r, 64, 64), cols] = dot_nn(values[:, :span], expo_low)

    loop(HALF_HEADS, attend_chip, 0)

    rows_in[1].wait()
    count_y.wait()
    cs[1] = cs[0] + cr[0]
    for copy in count_z:
        copy.start()
    for copy in count_z:
        copy.wait()
    counts = cs[1] + cr[1] + cr[2] + cr[3]
    total = jnp.sum(counts, axis=1, keepdims=True)
    mine = jnp.sum(jnp.where(lane == group, counts, 0.0), axis=1, keepdims=True)
    scale = (weight_ref[0].astype(F32) * total / (NGROUPS * mine))[0:1, 0:1]
    row_at = lax.broadcasted_iota(jnp.int32, (ROWS, 1), 0) + x * 512
    own_scale = jnp.where(row_at + own < length, scale, 0.0)
    oth_scale = jnp.where(row_at + oth < length, scale, 0.0)
    hl[own_rows, :] = (ups[...].astype(F32) * own_scale).astype(BF16)
    outh[own_rows, :] = (ups[:, own_half].astype(F32) * own_scale).astype(BF16)
    ups_mate.wait()
    outh[oth_rows, :] = (outh[oth_rows, :].astype(F32) * oth_scale).astype(BF16)

    @pl.when(right)
    def _():
        def far_block(start):
            columns = at(start, ROWS, ROWS)

            def project_far(i):
                part = dot_tt(wq[:, at((i + 1) * HALF_WIDTH, HALF_WIDTH, 128)], nf[columns, :])
                kvft[at(i * HALF_WIDTH, HALF_WIDTH, 128), columns] = part.astype(BF16)

            loop(2, project_far, 0)

        for i in range(2):
            tok_far[i].wait_recv()
            tok_on[i].start()
            first_norm(tokf, own + i * 128, nf, own + i * 128, 2)
        far_block(own)
        for i in range(2):
            tok_on[i].wait()
            first_norm(tokf, oth + i * 128, nf, oth + i * 128, 2)
        far_block(oth)

        def attend_far(h):
            r = h * 64
            keys, queries, values = kvft[at(r, 64, 64), :], qkvt[at(r, 64, 64), :], kvft[at(HALF_WIDTH + r, 64, 64), :]
            for half in (0, 1):
                cols = slice(256 * half, 256 * half + 256)
                scores = dot_tn(keys, queries[:, cols])
                peak = jnp.max(scores, axis=0, keepdims=True)
                expo = jnp.exp(scores - peak)
                expo_low = expo.astype(BF16)
                expo_sum = jnp.sum(expo_low.astype(F32), axis=0, keepdims=True)
                ef[h, :, cols] = expo_low
                out = dot_nn(values, expo_low)
                old = m1[pl.ds(h, 1), cols]
                top = jnp.maximum(old, peak)
                old_part, new_part = jnp.exp(old - top), jnp.exp(peak - top)
                share = 1.0 / (l1[pl.ds(h, 1), cols] * old_part + expo_sum * new_part)
                f1[pl.ds(h, 1), cols] = old_part * share
                f2[pl.ds(h, 1), cols] = new_part * share
                o1[at(r, 64, 64), cols] = o1[at(r, 64, 64), cols] * (old_part * share) + out * (new_part * share)

        loop(HALF_HEADS, attend_far, 0)

    @pl.when(left)
    def _():
        nf[...] = jnp.zeros_like(nf)
        mixf[...] = jnp.zeros_like(mixf)

        def share_out(h):
            share = 1.0 / l1[pl.ds(h, 1), :]
            f1[pl.ds(h, 1), :] = share
            f2[pl.ds(h, 1), :] = jnp.zeros_like(share)
            o1[at(h * 64, 64, 64), :] = o1[at(h * 64, 64, 64), :] * share

        loop(HALF_HEADS, share_out)

    attt[att_rows, :] = o1[...].astype(BF16)
    att_mate.start()
    arrive("proj")
    att_mate.wait()

    for i in range(3):
        cols = slice(256 * i, 256 * i + 256)
        hid[:, cols] = tok[:, cols].astype(F32) + dot_tn(attt[:, own_rows], wp[:, cols])

    def second_norm(i):
        unit, _ = normalise(hid[at(i * 64, 64, 64), :])
        n2[at(own + i * 64, 64, 64), :] = (unit * gain2 + shift2).astype(BF16)

    loop(ROWS // 64, second_norm, 0)
    n2_mate.start()
    arrive("up")
    for third in range(3):

        def feed(i, third=third):
            cols = at(third * 1024 + i * 256, 256, 256)
            u = dot_nn(n2[own_rows, :], wu[:, cols])
            square = u * u
            bend = jnp.tanh(GELU_COEF * (u + 0.044715 * square * u))
            lift = 0.5 * (1.0 + bend)
            gel[own_rows, cols] = (u * lift).astype(BF16)
            slope = lift + 0.5 * u * (1.0 - bend * bend) * (GELU_COEF * (1.0 + 3 * 0.044715 * square))
            dg[:, cols] = slope.astype(BF16)

        loop(4, feed, 0)
        gel_mate[third].start()

    grads = (g_dn, g_up, g_pr, g_qk)
    outs = (o_dn, o_up, o_pr, o_qk)
    came, sent = (c_dn, c_up, c_pr, c_qk), (s_dn, s_up, s_pr, s_qk)
    hs = (h_dn, h_up, h_pr, h_qk)

    def remote(src, dst, w, slot, target):
        return pltpu.make_async_remote_copy(
            src_ref=src, dst_ref=dst, send_sem=send_sem.at[w, slot], recv_sem=recv_sem.at[w, slot],
            device_id=target, device_id_type=MESH,
        )

    def part(ref, w, index, count=1):
        rows = BLOCKS[w][0]
        return ref.at[at(index * rows, count * rows, 16)]

    def value(ref, w, index):
        rows = BLOCKS[w][0]
        return ref[at(index * rows, rows, 16), :].astype(F32)

    def keep(ref, w, index, result):
        rows = BLOCKS[w][0]
        ref[at(index * rows, rows, 16), :] = result.astype(BF16)

    class PlaneFirst:
        def __init__(self, w, x_first):
            self.w, self.x_first = w, x_first
            self.first, self.second = (x_peer, y_peer) if x_first else (y_peer, x_peer)
            self.kept = y if x_first else x

        def block(self, zz, j, mine):
            side = (x if mine else 1 - x) if self.x_first else (y if mine else 1 - y)
            return zz * 4 + (j * 2 + side if self.x_first else side * 2 + j)

        def first_copies(self, places):
            w = self.w
            return [
                remote(part(grads[w], w, self.block(zz, j, False)), part(came[w], w, zz * 2 + j), w, zz * 2 + j, self.first)
                for zz in places
                for j in range(2)
            ]

        def second_copy(self):
            w = self.w
            return remote(part(sent[w], w, 0, 4), part(came[w], w, 8, 4), w, 8, self.second)

        def third_copies(self):
            w = self.w
            return [
                remote(part(sent[w], w, 3 + d), part(came[w], w, 11 + d), w, 8 + d, z_peers[d - 1])
                for d in (1, 2, 3)
            ]

        def after_first(self, zz, j):
            w = self.w
            return value(grads[w], w, self.block(zz, j, True)) + value(came[w], w, zz * 2 + j)

        def after_second(self, zz):
            return self.after_first(zz, self.kept) + value(came[self.w], self.w, 8 + zz)

        def start_second(self):
            for copy in self.first_copies(range(4)):
                copy.wait()
            for zz in range(4):
                keep(sent[self.w], self.w, zz, self.after_first(zz, 1 - self.kept))
            self.second_copy().start()

        def start_third(self):
            self.second_copy().wait()
            for d, copy in zip((1, 2, 3), self.third_copies()):
                keep(sent[self.w], self.w, 3 + d, self.after_second((z + d) % 4))
                copy.start()

        def total(self):
            w = self.w
            for copy in self.third_copies():
                copy.wait()
            return self.after_second(z) + value(came[w], w, 12) + value(came[w], w, 13) + value(came[w], w, 14)

    class LineFirst:
        def __init__(self, w, x_second):
            self.w, self.x_second = w, x_second
            self.second, self.third = (x_peer, y_peer) if x_second else (y_peer, x_peer)
            self.kept = y if x_second else x

        def place(self, i, mine):
            side = (x if mine else 1 - x) if self.x_second else (y if mine else 1 - y)
            return i * 2 + side if self.x_second else side * 2 + i

        def first_copy(self, d):
            w = self.w
            return remote(part(grads[w], w, (z + d) % 4 * 4, 4), part(came[w], w, 4 * d - 4, 4), w, d - 1, z_peers[d - 1])

        def second_copy(self):
            w = self.w
            return remote(part(sent[w], w, 0, 2), part(came[w], w, 12, 2), w, 8, self.second)

        def third_copy(self):
            w = self.w
            return remote(part(sent[w], w, 2), part(came[w], w, 14), w, 9, self.third)

        def after_first(self, i, mine):
            w, b = self.w, self.place(i, mine)
            whole = value(grads[w], w, z * 4 + b)
            for d in range(3):
                whole = whole + value(came[w], w, 4 * d + b)
            return whole

        def start_second(self):
            for d in (1, 2, 3):
                self.first_copy(d).wait()
            for i in range(2):
                keep(sent[self.w], self.w, i, self.after_first(i, False))
            self.second_copy().start()

        def start_third(self):
            self.second_copy().wait()
            i = 1 - self.kept
            keep(sent[self.w], self.w, 2, self.after_first(i, True) + value(came[self.w], self.w, 12 + i))
            self.third_copy().start()

        def total(self):
            w = self.w
            self.third_copy().wait()
            return self.after_first(self.kept, True) + value(came[w], w, 12 + self.kept) + value(came[w], w, 14)

    def plan(w, order):
        return LineFirst(w, order == "zxy") if order[0] == "z" else PlaneFirst(w, order[0] == "x")

    plans = [[plan(w, order) for order in ORDERS[w]] for w in range(4)]

    def each_core(w, step):
        if ORDERS[w][0] == ORDERS[w][1]:
            step(plans[w][0])
            return
        for which in (0, 1):
            pl.when(core == which)(lambda which=which: step(plans[w][which]))

    def start_first(w, places):
        def step(plan):
            if isinstance(plan, PlaneFirst):
                for copy in plan.first_copies(places):
                    copy.start()
            elif 3 in places:
                for d in (1, 2, 3):
                    plan.first_copy(d).start()

        each_core(w, step)

    def start_second(w):
        each_core(w, lambda plan: plan.start_second())

    def start_third(w):
        each_core(w, lambda plan: plan.start_third())

    def places(w):
        parts = 3 if w == 3 else 1
        width = BLOCKS[w][1] // parts
        return [(pl.ds(i * width, width), at((2 * i + core) * width, width, 128)) for i in range(parts)]

    def last_copies(w):
        return [
            remote(hs[w].at[:, src], outs[w].at[:, dst], w, 12 + i, mate)
            for i, (src, dst) in enumerate(places(w))
        ]

    def start_last(w):
        rows = BLOCKS[w][0] // 2

        def step(plan):
            whole = plan.total()
            low_core = core == 0
            hs[w][...] = jnp.where(low_core, whole[rows:], whole[:rows])
            mine = jnp.where(low_core, whole[:rows], whole[rows:])
            parts = 3 if w == 3 else 1
            width = BLOCKS[w][1] // parts
            for i, (_, dst) in enumerate(places(w)):
                outs[w][:, dst] = mine[:, i * width : (i + 1) * width]

        each_core(w, step)
        for copy in last_copies(w):
            copy.start()

    def finish(w):
        for copy in last_copies(w):
            copy.wait()

    for copy in gel_mate:
        copy.wait()
    for zz in range(4):

        def down_rows(i, zz=zz):
            start = zz * WIDTH + i * 256
            g_dn[at(start, 256, 256), :] = dot_tn(gel[:, at(start, 256, 256)], outh[...]).astype(BF16)

        loop(3, down_rows, 0)
        start_first(0, (zz,))

    arrive("down")

    def gelu_back(cols):
        up_cot = dot_nt(hl[own_rows, :], wd[cols, :]) * dg[:, cols].astype(F32)
        up_cot = up_cot.astype(BF16)
        upo[:, cols] = up_cot
        return up_cot

    def back_other(i):
        gelu_back(at((1 - core) * 1536 + i * 256, 256, 256))

    def back_own(i):
        uph[own_rows, at(i * 256, 256, 256)] = gelu_back(at(core * 1536 + i * 256, 256, 256))

    loop(6, back_other, 0)
    up_mate.start()
    loop(6, back_own, 0)

    def n2_back(i):
        cols = at(i * 256, 256, 256)
        ncot[:, cols] = dot_nt(upo[...], wu[cols, :])

    loop(3, n2_back, 0)
    vsend[...] = jnp.zeros_like(vsend)

    def second_back(i):
        rows = at(i * 64, 64, 64)
        unit, inverse = normalise(hid[rows, :])
        cot = ncot[rows, :]
        position = lax.broadcasted_iota(jnp.int32, (64, 1), 0) + i * 64 + x * 512 + own
        out_cot = ups[rows, :].astype(F32) * jnp.where(position < length, scale, 0.0)
        hidden_cot = out_cot + normalise_back(cot, gain2, unit, inverse)
        hc[rows, :] = hidden_cot
        hl[at(own + i * 64, 64, 64), :] = hidden_cot.astype(BF16)
        vsend[0, 2:3, :] += jnp.sum(cot * unit, axis=0, keepdims=True)
        vsend[0, 3:4, :] += jnp.sum(cot, axis=0, keepdims=True)

    loop(ROWS // 64, second_back, 0)
    hl_mate.start()

    n2_mate.wait()
    up_mate.wait()
    for half in range(2):

        def up_columns(i, half=half):
            cols = at(i * 512, 512, 512)
            rows = slice(384 * half, 384 * half + 384)
            g_up[rows, cols] = dot_tn(n2[:, rows], uph[:, cols]).astype(BF16)

        loop(3, up_columns, 0)
        start_first(1, (2 * half, 2 * half + 1))

    hl_mate.wait()

    def proj_rows(i):
        rows = at(i * 256, 256, 256)
        g_pr[rows, :] = dot_nn(attt[rows, :], hl[:, own_half]).astype(BF16)

    loop(3, proj_rows, 0)
    start_first(2, range(4))
    attt[att_rows, :] = dot_nt(wp[att_rows, :], hl[...]).astype(BF16)

    def attend_back(h):
        r = h * 64
        rows = at(r, 64, 64)
        keys, queries, values = qkvt[at(HALF_WIDTH + r, 64, 64), :], qkvt[rows, :], qkvt[at(2 * HALF_WIDTH + r, 64, 64), :]
        cot = attt[at(core * HALF_WIDTH + r, 64, 64), :].astype(F32)
        near = (cot * f1[pl.ds(h, 1), :]).astype(BF16)
        delta = jnp.sum(near.astype(F32) * o1[rows, :], axis=0, keepdims=True)
        far = (cot * f2[pl.ds(h, 1), :]).astype(BF16)
        far_delta = jnp.sum(far.astype(F32) * o1[rows, :], axis=0, keepdims=True)
        key_terms, value_terms = [], []
        for half in (0, 1):
            span, cols = 256 * (half + 1), slice(256 * half, 256 * half + 256)
            expo = ec[h, :span, cols]
            prob_cot = dot_tn(values[:, :span], near[:, cols])
            score_cot = (expo.astype(F32) * (prob_cot - delta[:, cols])).astype(BF16)
            o1[rows, cols] = dot_nn(keys[:, :span], score_cot)
            key_terms.append(dot_nt(queries[:, cols], score_cot))
            value_terms.append(dot_nt(near[:, cols], expo))
        for start, terms in ((HALF_WIDTH, key_terms), (2 * HALF_WIDTH, value_terms)):
            mixc[at(start + r, 64, 64), :256] = (terms[0] + terms[1][:, :256]).astype(BF16)
            mixc[at(start + r, 64, 64), 256:] = terms[1][:, 256:].astype(BF16)

        @pl.when(right)
        def _():
            far_keys, far_values = kvft[rows, :], kvft[at(HALF_WIDTH + r, 64, 64), :]
            expo = ef[h]
            prob_cot = dot_tn(far_values, far)
            score_cot = (expo.astype(F32) * (prob_cot - far_delta)).astype(BF16)
            o1[rows, :] += dot_nn(far_keys, score_cot)
            mixf[rows, :] = dot_nt(queries, score_cot).astype(BF16)
            mixf[at(HALF_WIDTH + r, 64, 64), :] = dot_nt(far, expo).astype(BF16)

        mixc[rows, :] = (o1[rows, :] * 0.125).astype(BF16)

    def normed_cot(mixed, first_column, columns, store):
        def step(i):
            rows = at(i * 256, 256, 256)
            store(rows, dot_tt(mixed[:, columns], wq[rows, first_column:]))

        loop(3, step, 0)

    def store_to(ref, rows):
        def store(cols, value):
            ref[rows, cols] = value.astype(ref.dtype)

        return store

    clip_peers = [mate, x_peer, diagonal]
    other_clips = [y_peer] + z_peers + yz_peers

    def clip_sum(i):
        return misc(18 + i, vsend.at[0], vrecv.at[i], clip_peers[i])

    def all_sum(i):
        return misc(21 + i, vsend.at[1], vrecv.at[3 + i], other_clips[i])

    loop(HALF_HEADS, attend_back, 0)
    @pl.when(right)
    def _():
        normed_cot(mixf, HALF_WIDTH, oth_rows, store_to(tokf, own_rows))
        nf_mate.start()

    for half in range(2):
        cols = slice(384 * half, 384 * half + 384)
        g_qk[cols, :384] = dot_tt(nc[:, cols], mixc[:384, :]).astype(BF16)
        for i in range(2):
            g_qk[cols, 384 * (i + 1) : 384 * (i + 2)] = (
                dot_tt(nc[:, cols], mixc[384 * (i + 1) : 384 * (i + 2), :])
                + dot_tt(nf[:, cols], mixf[384 * i : 384 * (i + 1), :])
            ).astype(BF16)
        start_first(3, (2 * half, 2 * half + 1))

    normed_cot(mixc, 0, oth_rows, store_to(upo, at(0, ROWS, ROWS)))
    nc_mate.start()

    @pl.when(right)
    def _():
        normed_cot(mixf, HALF_WIDTH, own_rows, store_to(ncot, at(0, ROWS, ROWS)))
        nf_mate.wait()
        tokf[own_rows, :] = (ncot[...] + tokf[oth_rows, :].astype(F32)).astype(BF16)
        nf_far.start()

    normed_cot(mixc, 0, own_rows, store_to(ncot, at(0, ROWS, ROWS)))

    def block_rows(i):
        cols = at(i * 256, 256, 256)
        block_out[:, cols] = (hid[:, cols] + dot_nn(gel[own_rows, :], wd[:, cols])).astype(BF16)

    start_second(0)
    loop(3, block_rows, 0)
    start_second(1)
    start_second(2)
    start_third(0)
    start_third(1)
    start_second(3)
    nc_mate.wait()

    @pl.when(left)
    def _():
        nf_far.wait_recv()
        for copy in tok_far:
            copy.wait_send()

    @pl.when(right)
    def _():
        nf_far.wait_send()

    def first_back(i):
        rows = at(i * 64, 64, 64)
        unit, inverse = normalise(tok[rows, :].astype(F32))
        near = tokc[rows, :].astype(F32)
        far = tokf[at(own + i * 64, 64, 64), :].astype(F32)
        cot = ncot[rows, :] + near + jnp.where(left, far, 0.0)
        input_grad[rows, :] = (hc[rows, :] + normalise_back(cot, gain1, unit, inverse)).astype(BF16)
        vsend[0, 0:1, :] += jnp.sum(cot * unit, axis=0, keepdims=True)
        vsend[0, 1:2, :] += jnp.sum(cot, axis=0, keepdims=True)

    loop(ROWS // 64, first_back, 0)

    for i in range(3):
        clip_sum(i).start()
    start_third(2)
    for i in range(3):
        clip_sum(i).wait()
    vsend[1] = vsend[0] + vrecv[0] + vrecv[1] + vrecv[2]
    for i in range(7):
        all_sum(i).start()
    start_last(0)
    start_third(3)
    for i in range(7):
        all_sum(i).wait()
    sums = vsend[1]
    for i in range(7):
        sums = sums + vrecv[3 + i]
    rank = dp * 4 + ctx
    o_vec[...] = pltpu.roll(sums, lax.rem(WIDTH - rank * 24, WIDTH), 1)[:, :128]
    start_last(1)
    start_last(2)
    start_last(3)
    for w in range(4):
        finish(w)


def hand_out_kernel(
    block_out, input_grad, qk, pr, up, dn, vec,
    o_block, o_input, o_v0, o_v1, o_qk, o_pr, o_v2, o_v3, o_up, o_dn, sem,
):
    pairs = ((block_out, o_block), (input_grad, o_input), (qk, o_qk), (pr, o_pr), (up, o_up), (dn, o_dn))
    copies = [pltpu.make_async_copy(src, dst, sem.at[i]) for i, (src, dst) in enumerate(pairs)]
    for copy in copies:
        copy.start()
    for i, ref in enumerate((o_v0, o_v1, o_v2, o_v3)):
        ref[...] = vec[i, :24]
    for copy in copies:
        copy.wait()


def fused_layer(args):
    vmem, smem, anywhere = (
        pl.BlockSpec(memory_space=pltpu.VMEM),
        pl.BlockSpec(memory_space=pltpu.SMEM),
        pl.BlockSpec(memory_space=pl.ANY),
    )

    def low(*shape):
        return pltpu.VMEM(shape, BF16)

    def full(*shape):
        return pltpu.VMEM(shape, F32)

    def per_block(count):
        return [low(count * rows, width) for rows, width in BLOCKS]

    vector = jax.ShapeDtypeStruct((24,), F32)

    def grad_shape(w):
        return jax.ShapeDtypeStruct((BLOCKS[w][0] // 2, BLOCKS[w][1] * 2), F32)

    rows_out = jax.ShapeDtypeStruct((ROWS, WIDTH), BF16)
    made = pl.pallas_call(
        layer_kernel,
        out_shape=[
            rows_out, rows_out, grad_shape(3), grad_shape(2), grad_shape(1), grad_shape(0),
            jax.ShapeDtypeStruct((8, 128), F32),
        ],
        in_specs=[smem] * 3 + [anywhere] * 2 + [vmem] * 4 + [anywhere] * 4,
        out_specs=[vmem] * 7,
        scratch_shapes=[
            low(256, 768), low(256, 768),
            low(768, 1152), low(768, 768), low(768, 3072), low(3072, 768),
            low(256, 768), low(512, 768), low(512, 768), low(512, 768),
            low(1152, 512), low(768, 512), low(512, 512), low(6, 512, 512), low(6, 512, 512),
            full(384, 512), full(8, 512), full(8, 512), full(8, 512), full(8, 512),
            low(768, 512), full(256, 768), low(512, 768), low(512, 3072), low(256, 3072),
            low(512, 384), low(256, 3072), low(512, 1536), full(256, 768),
            full(256, 768), low(512, 768), low(1152, 512), low(768, 512),
            full(2, 8, 128), full(4, 8, 128), full(2, 8, 768), full(10, 8, 768),
            low(3072, 384), low(768, 1536), low(768, 384), low(768, 1152),
        ]
        + per_block(15) + per_block(7)
        + [pltpu.VMEM((block[0] // 2, block[1]), F32) for block in BLOCKS]
        + [
            pltpu.SemaphoreType.DMA((4, 15)),
            pltpu.SemaphoreType.DMA((4, 15)),
            pltpu.SemaphoreType.DMA((32,)),
            pltpu.SemaphoreType.DMA((32,)),
            pltpu.SemaphoreType.DMA((8,)),
        ],
        compiler_params=pltpu.CompilerParams(
            collective_id=0, has_side_effects=True, vmem_limit_bytes=60 * 1024 * 1024
        ),
    )(*args)
    return pl.pallas_call(
        hand_out_kernel,
        out_shape=[
            rows_out, rows_out, vector, vector, grad_shape(3), grad_shape(2), vector, vector,
            grad_shape(1), grad_shape(0),
        ],
        in_specs=[vmem] * 7,
        out_specs=[anywhere] * 2 + [vmem] * 2 + [anywhere] * 2 + [vmem] * 2 + [anywhere] * 2,
        scratch_shapes=[pltpu.SemaphoreType.DMA((6,))],
        compiler_params=pltpu.CompilerParams(vmem_limit_bytes=60 * 1024 * 1024),
    )(*made)


def general_body(
    tokens,
    attn_gain,
    attn_shift,
    w_qkv,
    w_proj,
    mlp_gain,
    mlp_shift,
    w_up,
    w_down,
    upstream,
    clip_length,
    dataset_group,
    sample_weight,
):
    tok_rows = tokens.shape[0]
    model_width = tokens.shape[1]
    head_count = model_width // HD
    ctx_count = lax.axis_size("ctx")
    seq_rows = tok_rows * ctx_count
    first_row = lax.axis_index("ctx") * tok_rows
    length = clip_length[0]
    key_span = min(seq_rows, max(tok_rows, 512))
    block_count = seq_rows // key_span
    query_pos = first_row + jnp.arange(tok_rows, dtype=jnp.int32)
    last_pos = first_row + tok_rows - 1
    onehot = (dataset_group[0, 0] == jnp.arange(NGROUPS, dtype=jnp.int32)).astype(jnp.float32)
    counts = lax.psum(onehot * length.astype(jnp.float32), "dp")
    total_all = jnp.sum(counts)
    clip_scale = (
        sample_weight[0].astype(jnp.float32) * total_all / (NGROUPS * jnp.sum(onehot * counts))
    )
    x_rows = tokens.astype(jnp.float32)
    normed, norm_one_back = jax.vjp(layer_norm, x_rows, attn_gain, attn_shift)
    normed_low = normed.astype(jnp.bfloat16)
    mixed_qkv = jnp.dot(normed_low, w_qkv, preferred_element_type=jnp.float32).astype(jnp.bfloat16)
    queries = mixed_qkv[:, :model_width]
    key_local = mixed_qkv[:, model_width : 2 * model_width]
    value_local = mixed_qkv[:, 2 * model_width :]
    key_all, value_all = (
        lax.all_gather(key_local, "ctx", axis=0, tiled=True),
        lax.all_gather(value_local, "ctx", axis=0, tiled=True),
    )
    queries3 = queries.reshape(tok_rows, head_count, HD)

    def scores_for(kstart, key_rows):
        piece = key_rows[kstart : kstart + key_span].reshape(key_span, head_count, HD)
        raw = (
            jnp.einsum("qhd,khd->hqk", queries3, piece, preferred_element_type=jnp.float32) * 0.125
        )
        key_pos = kstart + jnp.arange(key_span, dtype=jnp.int32)
        allowed = (key_pos[None, :] <= query_pos[:, None]) & (key_pos[None, :] < length)
        return (jnp.where(allowed[None], raw, NEG_FILL), allowed)

    def useful(kstart):
        return (kstart <= last_pos) & (kstart < length)

    peak = jnp.full((head_count, tok_rows), NEG_FILL, jnp.float32)
    exp_total = jnp.zeros((head_count, tok_rows), jnp.float32)
    for index in range(block_count):
        kstart = index * key_span

        def gather_stats(carry, kstart=kstart):
            old_peak, old_total = carry
            scores, allowed = scores_for(kstart, key_all)
            new_peak = jnp.maximum(old_peak, jnp.max(scores, axis=-1))
            expo_vals = jnp.where(allowed[None], jnp.exp(scores - new_peak[..., None]), 0.0)
            return (
                new_peak,
                old_total * jnp.exp(old_peak - new_peak) + jnp.sum(expo_vals, axis=-1),
            )

        peak, exp_total = lax.cond(
            useful(kstart), gather_stats, lambda carry: carry, (peak, exp_total)
        )

    def probs_for(kstart, key_rows):
        scores, allowed = scores_for(kstart, key_rows)
        return (
            jnp.where(allowed[None], jnp.exp(scores - peak[..., None]), 0.0) / exp_total[..., None]
        )

    out_high = jnp.zeros((tok_rows, head_count, HD), jnp.float32)
    out_rest = jnp.zeros((tok_rows, head_count, HD), jnp.float32)
    for index in range(block_count):
        kstart = index * key_span

        def add_values(carry, kstart=kstart):
            high_acc, rest_acc = carry
            probs = probs_for(kstart, key_all)
            probs_low = probs.astype(jnp.bfloat16)
            remainder = (probs - probs_low.astype(jnp.float32)).astype(jnp.bfloat16)
            piece = value_all[kstart : kstart + key_span].reshape(key_span, head_count, HD)
            high_acc = high_acc + jnp.einsum(
                "hqk,khd->qhd", probs_low, piece, preferred_element_type=jnp.float32
            )
            rest_acc = rest_acc + jnp.einsum(
                "hqk,khd->qhd", remainder, piece, preferred_element_type=jnp.float32
            )
            return (high_acc, rest_acc)

        out_high, out_rest = lax.cond(
            useful(kstart), add_values, lambda carry: carry, (out_high, out_rest)
        )
    attended_low = out_high.reshape(tok_rows, model_width).astype(jnp.bfloat16)
    out_full = out_high + out_rest
    hidden = x_rows + jnp.dot(attended_low, w_proj, preferred_element_type=jnp.float32)
    normed_two, norm_two_back = jax.vjp(layer_norm, hidden, mlp_gain, mlp_shift)
    normed_two_low = normed_two.astype(jnp.bfloat16)
    up_proj = jnp.dot(normed_two_low, w_up, preferred_element_type=jnp.float32)
    gelu_vals, gelu_back = jax.vjp(gelu, up_proj)
    gelu_low = gelu_vals.astype(jnp.bfloat16)
    block_out = (hidden + jnp.dot(gelu_low, w_down, preferred_element_type=jnp.float32)).astype(
        jnp.bfloat16
    )
    valid = query_pos < length
    out_cot = upstream.astype(jnp.float32) * jnp.where(valid, clip_scale, 0.0)[:, None]
    out_cot_low = out_cot.astype(jnp.bfloat16)
    down_grad = jnp.einsum("tf,td->fd", gelu_low, out_cot_low, preferred_element_type=jnp.float32)
    gelu_in = jnp.einsum("td,fd->tf", out_cot_low, w_down, preferred_element_type=jnp.float32)
    (up_cot,) = gelu_back(gelu_in)
    up_cot_low = up_cot.astype(jnp.bfloat16)
    up_grad = jnp.einsum(
        "td,tf->df", normed_two_low, up_cot_low, preferred_element_type=jnp.float32
    )
    normed_two_cot = jnp.einsum("tf,df->td", up_cot_low, w_up, preferred_element_type=jnp.float32)
    norm_two_rows, mlp_gain_grad, mlp_shift_grad = norm_two_back(normed_two_cot)
    hidden_cot = out_cot + norm_two_rows
    hidden_cot_low = hidden_cot.astype(jnp.bfloat16)
    proj_grad = jnp.einsum(
        "ti,to->io", attended_low, hidden_cot_low, preferred_element_type=jnp.float32
    )
    attended_cot = jnp.einsum(
        "to,io->ti", hidden_cot_low, w_proj, preferred_element_type=jnp.float32
    ).astype(jnp.bfloat16)
    attended_cot3 = attended_cot.reshape(tok_rows, head_count, HD)
    delta = jnp.einsum("qhd,qhd->hq", attended_cot3.astype(jnp.float32), out_full)
    key_back, value_back = (key_all, value_all)
    query_cot = jnp.zeros((tok_rows, head_count, HD), jnp.float32)
    key_pieces = []
    value_pieces = []
    empty_piece = jnp.zeros((key_span, head_count, HD), jnp.float32)
    for index in range(block_count):
        kstart = index * key_span

        def block_grads(q_acc, kstart=kstart):
            probs = probs_for(kstart, key_back)
            probs_low = probs.astype(jnp.bfloat16)
            key_piece = key_back[kstart : kstart + key_span].reshape(key_span, head_count, HD)
            value_piece = value_back[kstart : kstart + key_span].reshape(key_span, head_count, HD)
            prob_cot = jnp.einsum(
                "qhd,khd->hqk", attended_cot3, value_piece, preferred_element_type=jnp.float32
            )
            score_cot = (probs * (prob_cot - delta[..., None])).astype(jnp.bfloat16)
            q_acc = (
                q_acc
                + jnp.einsum(
                    "hqk,khd->qhd", score_cot, key_piece, preferred_element_type=jnp.float32
                )
                * 0.125
            )
            key_term = (
                jnp.einsum("hqk,qhd->khd", score_cot, queries3, preferred_element_type=jnp.float32)
                * 0.125
            )
            value_term = jnp.einsum(
                "hqk,qhd->khd", probs_low, attended_cot3, preferred_element_type=jnp.float32
            )
            return (q_acc, key_term, value_term)

        query_cot, key_term, value_term = lax.cond(
            useful(kstart), block_grads, lambda q_acc: (q_acc, empty_piece, empty_piece), query_cot
        )
        key_pieces.append(key_term.reshape(key_span, model_width))
        value_pieces.append(value_term.reshape(key_span, model_width))
    key_terms = jnp.concatenate(key_pieces, axis=0)
    value_terms = jnp.concatenate(value_pieces, axis=0)
    key_cot, value_cot = (
        lax.psum_scatter(
            key_terms.astype(jnp.bfloat16), "ctx", scatter_dimension=0, tiled=True
        ).astype(jnp.float32),
        lax.psum_scatter(
            value_terms.astype(jnp.bfloat16), "ctx", scatter_dimension=0, tiled=True
        ).astype(jnp.float32),
    )
    mixed_cot = jnp.concatenate(
        [query_cot.reshape(tok_rows, model_width), key_cot, value_cot], axis=1
    ).astype(jnp.bfloat16)
    qkv_grad = jnp.einsum("td,te->de", normed_low, mixed_cot, preferred_element_type=jnp.float32)
    normed_cot = jnp.einsum("te,de->td", mixed_cot, w_qkv, preferred_element_type=jnp.float32)
    norm_one_rows, attn_gain_grad, attn_shift_grad = norm_one_back(normed_cot)
    input_grad = (hidden_cot + norm_one_rows).astype(jnp.bfloat16)
    reduced = (
        lax.psum_scatter(attn_gain_grad, ("dp", "ctx"), scatter_dimension=0, tiled=True),
        lax.psum_scatter(attn_shift_grad, ("dp", "ctx"), scatter_dimension=0, tiled=True),
        lax.psum_scatter(qkv_grad, ("dp", "ctx"), scatter_dimension=0, tiled=True),
        lax.psum_scatter(proj_grad, ("dp", "ctx"), scatter_dimension=0, tiled=True),
        lax.psum_scatter(mlp_gain_grad, ("dp", "ctx"), scatter_dimension=0, tiled=True),
        lax.psum_scatter(mlp_shift_grad, ("dp", "ctx"), scatter_dimension=0, tiled=True),
        lax.psum_scatter(up_grad, ("dp", "ctx"), scatter_dimension=0, tiled=True),
        lax.psum_scatter(down_grad, ("dp", "ctx"), scatter_dimension=0, tiled=True),
    )
    return (
        block_out,
        input_grad,
        reduced[0],
        reduced[1],
        reduced[2],
        reduced[3],
        reduced[4],
        reduced[5],
        reduced[6],
        reduced[7],
    )


def fused_body(
    tokens, attn_gain, attn_shift, w_qkv, w_proj, mlp_gain, mlp_shift, w_up, w_down, upstream,
    clip_length, dataset_group, sample_weight,
):
    outs = fused_layer(
        [clip_length, dataset_group.reshape(1), sample_weight, tokens, upstream]
        + [attn_gain, attn_shift, mlp_gain, mlp_shift, w_qkv, w_proj, w_up, w_down]
    )
    return tuple(outs)


def solution(mesh):
    in_specs = (
        P(("dp", "ctx"), None),
        P(),
        P(),
        P(),
        P(),
        P(),
        P(),
        P(),
        P(),
        P(("dp", "ctx"), None),
        P("dp"),
        P("dp", None),
        P("dp"),
    )
    out_specs = (
        P(("dp", "ctx"), None),
        P(("dp", "ctx"), None),
        P(("dp", "ctx")),
        P(("dp", "ctx")),
        P(("dp", "ctx"), None),
        P(("dp", "ctx"), None),
        P(("dp", "ctx")),
        P(("dp", "ctx")),
        P(("dp", "ctx"), None),
        P(("dp", "ctx"), None),
    )
    fused = mesh.shape["dp"] == 8 and mesh.shape["ctx"] == 4
    body = fused_body if fused else general_body
    return jax.shard_map(body, mesh=mesh, in_specs=in_specs, out_specs=out_specs, check_vma=False)
```

```python
import jax
import jax.numpy as jnp
from jax import lax
from jax.experimental import pallas as pl
from jax.experimental.pallas import tpu as pltpu
from jax.sharding import PartitionSpec as P

HD = 64
NGROUPS = 4


EPSILON = 1e-05
NEG_FILL = -1e30
GELU_COEF = 0.7978845608028654


def layer_norm(values, gain_vec, shift_vec):
    average = jnp.mean(values, axis=-1, keepdims=True)
    centred = values - average
    spread = jnp.mean(centred * centred, axis=-1, keepdims=True)
    return centred * lax.rsqrt(spread + EPSILON) * gain_vec + shift_vec


def gelu(inputs):
    return (
        0.5 * inputs * (1.0 + jnp.tanh(GELU_COEF * (inputs + 0.044715 * inputs * inputs * inputs)))
    )


MESH = pl.DeviceIdType.MESH
BF16 = jnp.bfloat16
F32 = jnp.float32
ROWS = 256
WIDTH = 768
HIDDEN = 3072
HALF_HEADS = 6
HALF_WIDTH = 384
BLOCKS = ((192, 384), (48, 1536), (48, 384), (48, 1152))
ORDERS = (('zyx', 'xyz'), ('yxz', 'xyz'), ('zyx', 'zxy'), ('yxz', 'xyz'))


def dot_nn(left, right):
    return lax.dot_general(left, right, (((1,), (0,)), ((), ())), preferred_element_type=F32)


def dot_nt(left, right):
    return lax.dot_general(left, right, (((1,), (1,)), ((), ())), preferred_element_type=F32)


def dot_tn(left, right):
    return lax.dot_general(left, right, (((0,), (0,)), ((), ())), preferred_element_type=F32)


def dot_tt(left, right):
    return lax.dot_general(left, right, (((0,), (1,)), ((), ())), preferred_element_type=F32)


def device_at(z, y, x, core):
    return (z * 2 + y, x * 2 + core)


def normalise(values):
    average = jnp.mean(values, axis=-1, keepdims=True)
    centred = values - average
    spread = jnp.mean(centred * centred, axis=-1, keepdims=True)
    inverse = lax.rsqrt(spread + EPSILON)
    return centred * inverse, inverse


def normalise_back(cot, gain, unit, inverse):
    scaled = cot * gain
    first = jnp.mean(scaled, axis=-1, keepdims=True)
    second = jnp.mean(scaled * unit, axis=-1, keepdims=True)
    return inverse * (scaled - first - unit * second)


def loop(count, step, unroll=1):
    if unroll == 0:
        for i in range(count):
            step(i)
        return

    def wrapped(index, carry):
        step(index)
        return carry

    lax.fori_loop(0, count, wrapped, 0, unroll=unroll)


def at(start, size, unit):
    return pl.ds(pl.multiple_of(start, unit), size)


def layer_kernel(
    length_ref, group_ref, weight_ref, tok_in, ups_in, gain1_ref, shift1_ref, gain2_ref, shift2_ref,
    w_qkv, w_proj, w_up, w_down,
    block_out, input_grad, o_qk, o_pr, o_up, o_dn, o_vec,
    tok, ups, wq, wp, wu, wd, tokc, tokf, nc, nf, qkvt, kvft, bias, ec, ef, o1, m1, l1, f1, f2,
    attt, hid, n2, gel, dg, outh, upo, uph, ncot, hc, hl, mixc, mixf,
    cs, cr, vsend, vrecv,
    g_dn, g_up, g_pr, g_qk,
    c_dn, c_up, c_pr, c_qk, s_dn, s_up, s_pr, s_qk, h_dn, h_up, h_pr, h_qk,
    send_sem, recv_sem, misc_send, misc_recv, local_sem,
):
    dp, ctx = lax.axis_index("dp"), lax.axis_index("ctx")
    z, y, x, core = dp // 2, dp % 2, ctx // 2, ctx % 2
    mate = device_at(z, y, x, 1 - core)
    x_peer = device_at(z, y, 1 - x, core)
    y_peer = device_at(z, 1 - y, x, core)
    z_peers = [device_at((z + d) % 4, y, x, core) for d in (1, 2, 3)]
    own, oth = core * ROWS, (1 - core) * ROWS
    own_rows, oth_rows = at(own, ROWS, ROWS), at(oth, ROWS, ROWS)
    own_half, oth_half = at(core * HALF_WIDTH, HALF_WIDTH, 128), at((1 - core) * HALF_WIDTH, HALF_WIDTH, 128)
    length, group = length_ref[0], group_ref[0]
    gain1, shift1, gain2, shift2 = (
        ref[...].reshape(1, WIDTH) for ref in (gain1_ref, shift1_ref, gain2_ref, shift2_ref)
    )
    left, right = x == 0, x == 1

    def fetch(slot, src, dst):
        return pltpu.make_async_copy(src, dst, local_sem.at[slot])

    def weight_copies(name):
        if name == "qkv":
            return [
                fetch(i, w_qkv.at[:, at(i * WIDTH + core * HALF_WIDTH, HALF_WIDTH, 128)],
                      wq.at[:, pl.ds(i * HALF_WIDTH, HALF_WIDTH)])
                for i in range(3)
            ]
        if name == "proj":
            return [fetch(3, w_proj, wp)]
        if name == "up":
            return [fetch(4, w_up, wu)]
        return [fetch(5, w_down, wd)]

    def ask(*names):
        for name in names:
            for copy in weight_copies(name):
                copy.start()

    rows_in = [fetch(6, tok_in, tok), fetch(7, ups_in, ups)]
    rows_in[0].start()
    ask("qkv")
    rows_in[1].start()

    def arrive(name):
        for copy in weight_copies(name):
            copy.wait()

    diagonal = device_at(z, y, 1 - x, 1 - core)
    yz_peers = [device_at((z + d) % 4, 1 - y, x, core) for d in (1, 2, 3)]
    peers = [mate, x_peer, diagonal, y_peer] + z_peers + yz_peers
    barrier = pltpu.get_barrier_semaphore()
    for peer in peers:
        pl.semaphore_signal(barrier, inc=1, device_id=peer, device_id_type=MESH)
    pl.semaphore_wait(barrier, len(peers))

    def misc(slot, src, dst, target):
        return pltpu.make_async_remote_copy(
            src_ref=src, dst_ref=dst, send_sem=misc_send.at[slot], recv_sem=misc_recv.at[slot],
            device_id=target, device_id_type=MESH,
        )

    def piece(i, start=0):
        return at(start + i * 128, 128, 128)

    tok_far = [misc(28 + i, tok_in.at[piece(i)], tokf.at[piece(i, own)], x_peer) for i in range(2)]
    tok_mate = misc(1, tok_in, tokc, mate)
    tok_on = [misc(30 + i, tokf.at[piece(i, own)], tokf.at[piece(i, own)], mate) for i in range(2)]
    ups_mate = misc(3, ups_in.at[:, oth_half], outh.at[own_rows], mate)
    count_y = misc(4, cs.at[0], cr.at[0], y_peer)
    count_z = [misc(4 + d, cs.at[1], cr.at[d], z_peers[d - 1]) for d in (1, 2, 3)]
    att_rows = at(core * HALF_WIDTH, HALF_WIDTH, 128)
    att_mate = misc(8, attt.at[att_rows], attt.at[att_rows], mate)
    n2_mate = misc(9, n2.at[own_rows], n2.at[own_rows], mate)
    gel_mate = [
        misc(10 + i, gel.at[own_rows, pl.ds(1024 * i, 1024)], gel.at[own_rows, pl.ds(1024 * i, 1024)], mate)
        for i in range(3)
    ]
    up_mate = misc(13, upo.at[:, at((1 - core) * 1536, 1536, 128)], uph.at[own_rows], mate)
    hl_mate = misc(14, hl.at[own_rows], hl.at[own_rows], mate)
    nc_mate = misc(15, upo.at[:, :WIDTH], tokc, mate)
    nf_mate = misc(16, tokf.at[own_rows], tokf.at[own_rows], mate)
    nf_far = misc(17, tokf.at[own_rows], tokf.at[own_rows], x_peer)

    @pl.when(left)
    def _():
        for copy in tok_far:
            copy.start()

    tok_mate.start()
    ups_mate.start()
    lane = lax.broadcasted_iota(jnp.int32, (8, 128), 1)
    cs[0] = jnp.where(lane == group, length.astype(F32), 0.0)
    count_y.start()
    ask("proj", "up", "down")

    def first_norm(src, src_at, dst, dst_at, count=ROWS // 64):
        def step(i):
            unit, _ = normalise(src[at(src_at + i * 64, 64, 64), :].astype(F32))
            dst[at(dst_at + i * 64, 64, 64), :] = (unit * gain1 + shift1).astype(BF16)

        loop(count, step, 0)

    rows_in[0].wait()
    first_norm(tok, 0, nc, own)
    tok_mate.wait()
    first_norm(tokc, 0, nc, oth)
    arrive("qkv")

    def project(i):
        part = dot_tt(wq[:, at(i * HALF_WIDTH, HALF_WIDTH, 128)], nc[...])
        qkvt[at(i * HALF_WIDTH, HALF_WIDTH, 128), :] = (part * jnp.where(i == 0, 0.125, 1.0)).astype(BF16)

    loop(3, project, 0)

    key_at = lax.broadcasted_iota(jnp.int32, (512, 512), 0)
    query_at = lax.broadcasted_iota(jnp.int32, (512, 512), 1)
    bias[...] = jnp.where((key_at <= query_at) & (key_at + x * 512 < length), 0.0, NEG_FILL).astype(BF16)

    def attend_chip(h):
        r = h * 64
        keys, queries, values = qkvt[at(HALF_WIDTH + r, 64, 64), :], qkvt[at(r, 64, 64), :], qkvt[at(2 * HALF_WIDTH + r, 64, 64), :]
        for half in (0, 1):
            span, cols = 256 * (half + 1), slice(256 * half, 256 * half + 256)
            scores = dot_tn(keys[:, :span], queries[:, cols]) + bias[:span, cols].astype(F32)
            peak = jnp.max(scores, axis=0, keepdims=True)
            expo = jnp.exp(scores - peak)
            expo_low = expo.astype(BF16)
            m1[pl.ds(h, 1), cols] = peak
            l1[pl.ds(h, 1), cols] = jnp.sum(expo_low.astype(F32), axis=0, keepdims=True)
            ec[h, :span, cols] = expo_low
            o1[at(r, 64, 64), cols] = dot_nn(values[:, :span], expo_low)

    loop(HALF_HEADS, attend_chip, 0)

    rows_in[1].wait()
    count_y.wait()
    cs[1] = cs[0] + cr[0]
    for copy in count_z:
        copy.start()
    for copy in count_z:
        copy.wait()
    counts = cs[1] + cr[1] + cr[2] + cr[3]
    total = jnp.sum(counts, axis=1, keepdims=True)
    mine = jnp.sum(jnp.where(lane == group, counts, 0.0), axis=1, keepdims=True)
    scale = (weight_ref[0].astype(F32) * total / (NGROUPS * mine))[0:1, 0:1]
    row_at = lax.broadcasted_iota(jnp.int32, (ROWS, 1), 0) + x * 512
    own_scale = jnp.where(row_at + own < length, scale, 0.0)
    oth_scale = jnp.where(row_at + oth < length, scale, 0.0)
    hl[own_rows, :] = (ups[...].astype(F32) * own_scale).astype(BF16)
    outh[own_rows, :] = (ups[:, own_half].astype(F32) * own_scale).astype(BF16)
    ups_mate.wait()
    outh[oth_rows, :] = (outh[oth_rows, :].astype(F32) * oth_scale).astype(BF16)

    @pl.when(right)
    def _():
        def far_block(start):
            columns = at(start, ROWS, ROWS)

            def project_far(i):
                part = dot_tt(wq[:, at((i + 1) * HALF_WIDTH, HALF_WIDTH, 128)], nf[columns, :])
                kvft[at(i * HALF_WIDTH, HALF_WIDTH, 128), columns] = part.astype(BF16)

            loop(2, project_far, 0)

        for i in range(2):
            tok_far[i].wait_recv()
            tok_on[i].start()
            first_norm(tokf, own + i * 128, nf, own + i * 128, 2)
        far_block(own)
        for i in range(2):
            tok_on[i].wait()
            first_norm(tokf, oth + i * 128, nf, oth + i * 128, 2)
        far_block(oth)

        def attend_far(h):
            r = h * 64
            keys, queries, values = kvft[at(r, 64, 64), :], qkvt[at(r, 64, 64), :], kvft[at(HALF_WIDTH + r, 64, 64), :]
            for half in (0, 1):
                cols = slice(256 * half, 256 * half + 256)
                scores = dot_tn(keys, queries[:, cols])
                peak = jnp.max(scores, axis=0, keepdims=True)
                expo = jnp.exp(scores - peak)
                expo_low = expo.astype(BF16)
                expo_sum = jnp.sum(expo_low.astype(F32), axis=0, keepdims=True)
                ef[h, :, cols] = expo_low
                out = dot_nn(values, expo_low)
                old = m1[pl.ds(h, 1), cols]
                top = jnp.maximum(old, peak)
                old_part, new_part = jnp.exp(old - top), jnp.exp(peak - top)
                share = 1.0 / (l1[pl.ds(h, 1), cols] * old_part + expo_sum * new_part)
                f1[pl.ds(h, 1), cols] = old_part * share
                f2[pl.ds(h, 1), cols] = new_part * share
                o1[at(r, 64, 64), cols] = o1[at(r, 64, 64), cols] * (old_part * share) + out * (new_part * share)

        loop(HALF_HEADS, attend_far, 0)

    @pl.when(left)
    def _():
        nf[...] = jnp.zeros_like(nf)
        mixf[...] = jnp.zeros_like(mixf)

        def share_out(h):
            share = 1.0 / l1[pl.ds(h, 1), :]
            f1[pl.ds(h, 1), :] = share
            f2[pl.ds(h, 1), :] = jnp.zeros_like(share)
            o1[at(h * 64, 64, 64), :] = o1[at(h * 64, 64, 64), :] * share

        loop(HALF_HEADS, share_out)

    attt[att_rows, :] = o1[...].astype(BF16)
    att_mate.start()
    arrive("proj")
    att_mate.wait()

    for i in range(3):
        cols = slice(256 * i, 256 * i + 256)
        hid[:, cols] = tok[:, cols].astype(F32) + dot_tn(attt[:, own_rows], wp[:, cols])

    def second_norm(i):
        unit, _ = normalise(hid[at(i * 64, 64, 64), :])
        n2[at(own + i * 64, 64, 64), :] = (unit * gain2 + shift2).astype(BF16)

    loop(ROWS // 64, second_norm, 0)
    n2_mate.start()
    arrive("up")
    for third in range(3):

        def feed(i, third=third):
            cols = at(third * 1024 + i * 256, 256, 256)
            u = dot_nn(n2[own_rows, :], wu[:, cols])
            square = u * u
            bend = jnp.tanh(GELU_COEF * (u + 0.044715 * square * u))
            lift = 0.5 * (1.0 + bend)
            gel[own_rows, cols] = (u * lift).astype(BF16)
            slope = lift + 0.5 * u * (1.0 - bend * bend) * (GELU_COEF * (1.0 + 3 * 0.044715 * square))
            dg[:, cols] = slope.astype(BF16)

        loop(4, feed, 0)
        gel_mate[third].start()

    grads = (g_dn, g_up, g_pr, g_qk)
    outs = (o_dn, o_up, o_pr, o_qk)
    came, sent = (c_dn, c_up, c_pr, c_qk), (s_dn, s_up, s_pr, s_qk)
    hs = (h_dn, h_up, h_pr, h_qk)

    def remote(src, dst, w, slot, target):
        return pltpu.make_async_remote_copy(
            src_ref=src, dst_ref=dst, send_sem=send_sem.at[w, slot], recv_sem=recv_sem.at[w, slot],
            device_id=target, device_id_type=MESH,
        )

    def part(ref, w, index, count=1):
        rows = BLOCKS[w][0]
        return ref.at[at(index * rows, count * rows, 16)]

    def value(ref, w, index):
        rows = BLOCKS[w][0]
        return ref[at(index * rows, rows, 16), :].astype(F32)

    def keep(ref, w, index, result):
        rows = BLOCKS[w][0]
        ref[at(index * rows, rows, 16), :] = result.astype(BF16)

    class PlaneFirst:
        def __init__(self, w, x_first):
            self.w, self.x_first = w, x_first
            self.first, self.second = (x_peer, y_peer) if x_first else (y_peer, x_peer)
            self.kept = y if x_first else x

        def block(self, zz, j, mine):
            side = (x if mine else 1 - x) if self.x_first else (y if mine else 1 - y)
            return zz * 4 + (j * 2 + side if self.x_first else side * 2 + j)

        def first_copies(self, places):
            w = self.w
            return [
                remote(part(grads[w], w, self.block(zz, j, False)), part(came[w], w, zz * 2 + j), w, zz * 2 + j, self.first)
                for zz in places
                for j in range(2)
            ]

        def second_copy(self):
            w = self.w
            return remote(part(sent[w], w, 0, 4), part(came[w], w, 8, 4), w, 8, self.second)

        def third_copies(self):
            w = self.w
            return [
                remote(part(sent[w], w, 3 + d), part(came[w], w, 11 + d), w, 8 + d, z_peers[d - 1])
                for d in (1, 2, 3)
            ]

        def after_first(self, zz, j):
            w = self.w
            return value(grads[w], w, self.block(zz, j, True)) + value(came[w], w, zz * 2 + j)

        def after_second(self, zz):
            return self.after_first(zz, self.kept) + value(came[self.w], self.w, 8 + zz)

        def start_second(self):
            for copy in self.first_copies(range(4)):
                copy.wait()
            for zz in range(4):
                keep(sent[self.w], self.w, zz, self.after_first(zz, 1 - self.kept))
            self.second_copy().start()

        def start_third(self):
            self.second_copy().wait()
            for d, copy in zip((1, 2, 3), self.third_copies()):
                keep(sent[self.w], self.w, 3 + d, self.after_second((z + d) % 4))
                copy.start()

        def total(self):
            w = self.w
            for copy in self.third_copies():
                copy.wait()
            return self.after_second(z) + value(came[w], w, 12) + value(came[w], w, 13) + value(came[w], w, 14)

    class LineFirst:
        def __init__(self, w, x_second):
            self.w, self.x_second = w, x_second
            self.second, self.third = (x_peer, y_peer) if x_second else (y_peer, x_peer)
            self.kept = y if x_second else x

        def place(self, i, mine):
            side = (x if mine else 1 - x) if self.x_second else (y if mine else 1 - y)
            return i * 2 + side if self.x_second else side * 2 + i

        def first_copy(self, d):
            w = self.w
            return remote(part(grads[w], w, (z + d) % 4 * 4, 4), part(came[w], w, 4 * d - 4, 4), w, d - 1, z_peers[d - 1])

        def second_copy(self):
            w = self.w
            return remote(part(sent[w], w, 0, 2), part(came[w], w, 12, 2), w, 8, self.second)

        def third_copy(self):
            w = self.w
            return remote(part(sent[w], w, 2), part(came[w], w, 14), w, 9, self.third)

        def after_first(self, i, mine):
            w, b = self.w, self.place(i, mine)
            whole = value(grads[w], w, z * 4 + b)
            for d in range(3):
                whole = whole + value(came[w], w, 4 * d + b)
            return whole

        def start_second(self):
            for d in (1, 2, 3):
                self.first_copy(d).wait()
            for i in range(2):
                keep(sent[self.w], self.w, i, self.after_first(i, False))
            self.second_copy().start()

        def start_third(self):
            self.second_copy().wait()
            i = 1 - self.kept
            keep(sent[self.w], self.w, 2, self.after_first(i, True) + value(came[self.w], self.w, 12 + i))
            self.third_copy().start()

        def total(self):
            w = self.w
            self.third_copy().wait()
            return self.after_first(self.kept, True) + value(came[w], w, 12 + self.kept) + value(came[w], w, 14)

    def plan(w, order):
        return LineFirst(w, order == "zxy") if order[0] == "z" else PlaneFirst(w, order[0] == "x")

    plans = [[plan(w, order) for order in ORDERS[w]] for w in range(4)]

    def each_core(w, step):
        if ORDERS[w][0] == ORDERS[w][1]:
            step(plans[w][0])
            return
        for which in (0, 1):
            pl.when(core == which)(lambda which=which: step(plans[w][which]))

    def start_first(w, places):
        def step(plan):
            if isinstance(plan, PlaneFirst):
                for copy in plan.first_copies(places):
                    copy.start()
            else:
                for zz in places:
                    for d in (1, 2, 3):
                        pl.when((z + d) % 4 == zz)(lambda d=d: plan.first_copy(d).start())

        each_core(w, step)

    def start_second(w):
        each_core(w, lambda plan: plan.start_second())

    def start_third(w):
        each_core(w, lambda plan: plan.start_third())

    def places(w):
        parts = 3 if w == 3 else 1
        width = BLOCKS[w][1] // parts
        return [(pl.ds(i * width, width), at((2 * i + core) * width, width, 128)) for i in range(parts)]

    def last_copies(w):
        return [
            remote(hs[w].at[:, src], outs[w].at[:, dst], w, 12 + i, mate)
            for i, (src, dst) in enumerate(places(w))
        ]

    def start_last(w):
        rows = BLOCKS[w][0] // 2

        def step(plan):
            whole = plan.total()
            low_core = core == 0
            hs[w][...] = jnp.where(low_core, whole[rows:], whole[:rows])
            mine = jnp.where(low_core, whole[:rows], whole[rows:])
            parts = 3 if w == 3 else 1
            width = BLOCKS[w][1] // parts
            for i, (_, dst) in enumerate(places(w)):
                outs[w][:, dst] = mine[:, i * width : (i + 1) * width]

        each_core(w, step)
        for copy in last_copies(w):
            copy.start()

    def finish(w):
        for copy in last_copies(w):
            copy.wait()

    for zz in range(4):
        if zz < 3:
            gel_mate[zz].wait()

        def down_rows(i, zz=zz):
            start = zz * WIDTH + i * 256
            g_dn[at(start, 256, 256), :] = dot_tn(gel[:, at(start, 256, 256)], outh[...]).astype(BF16)

        loop(3, down_rows, 0)
        start_first(0, (zz,))

    arrive("down")

    def gelu_back(cols):
        up_cot = dot_nt(hl[own_rows, :], wd[cols, :]) * dg[:, cols].astype(F32)
        up_cot = up_cot.astype(BF16)
        upo[:, cols] = up_cot
        return up_cot

    def back_other(i):
        gelu_back(at((1 - core) * 1536 + i * 256, 256, 256))

    def back_own(i):
        uph[own_rows, at(i * 256, 256, 256)] = gelu_back(at(core * 1536 + i * 256, 256, 256))

    loop(6, back_other, 0)
    up_mate.start()
    loop(6, back_own, 0)

    def n2_back(i):
        cols = at(i * 256, 256, 256)
        ncot[:, cols] = dot_nt(upo[...], wu[cols, :])

    loop(3, n2_back, 0)
    vsend[...] = jnp.zeros_like(vsend)

    def second_back(i):
        rows = at(i * 64, 64, 64)
        unit, inverse = normalise(hid[rows, :])
        cot = ncot[rows, :]
        position = lax.broadcasted_iota(jnp.int32, (64, 1), 0) + i * 64 + x * 512 + own
        out_cot = ups[rows, :].astype(F32) * jnp.where(position < length, scale, 0.0)
        hidden_cot = out_cot + normalise_back(cot, gain2, unit, inverse)
        hc[rows, :] = hidden_cot
        hl[at(own + i * 64, 64, 64), :] = hidden_cot.astype(BF16)
        vsend[0, 2:3, :] += jnp.sum(cot * unit, axis=0, keepdims=True)
        vsend[0, 3:4, :] += jnp.sum(cot, axis=0, keepdims=True)

    loop(ROWS // 64, second_back, 0)
    hl_mate.start()

    n2_mate.wait()
    up_mate.wait()
    for half in range(2):

        def up_columns(i, half=half):
            cols = at(i * 512, 512, 512)
            rows = slice(384 * half, 384 * half + 384)
            g_up[rows, cols] = dot_tn(n2[:, rows], uph[:, cols]).astype(BF16)

        loop(3, up_columns, 0)
        start_first(1, (2 * half, 2 * half + 1))

    hl_mate.wait()

    def proj_rows(i):
        rows = at(i * 256, 256, 256)
        g_pr[rows, :] = dot_nn(attt[rows, :], hl[:, own_half]).astype(BF16)

    loop(3, proj_rows, 0)
    start_first(2, range(4))
    attt[att_rows, :] = dot_nt(wp[att_rows, :], hl[...]).astype(BF16)

    def attend_back(h):
        r = h * 64
        rows = at(r, 64, 64)
        keys, queries, values = qkvt[at(HALF_WIDTH + r, 64, 64), :], qkvt[rows, :], qkvt[at(2 * HALF_WIDTH + r, 64, 64), :]
        cot = attt[at(core * HALF_WIDTH + r, 64, 64), :].astype(F32)
        near = (cot * f1[pl.ds(h, 1), :]).astype(BF16)
        delta = jnp.sum(near.astype(F32) * o1[rows, :], axis=0, keepdims=True)
        far = (cot * f2[pl.ds(h, 1), :]).astype(BF16)
        far_delta = jnp.sum(far.astype(F32) * o1[rows, :], axis=0, keepdims=True)
        key_terms, value_terms = [], []
        for half in (0, 1):
            span, cols = 256 * (half + 1), slice(256 * half, 256 * half + 256)
            expo = ec[h, :span, cols]
            prob_cot = dot_tn(values[:, :span], near[:, cols])
            score_cot = (expo.astype(F32) * (prob_cot - delta[:, cols])).astype(BF16)
            o1[rows, cols] = dot_nn(keys[:, :span], score_cot)
            key_terms.append(dot_nt(queries[:, cols], score_cot))
            value_terms.append(dot_nt(near[:, cols], expo))
        for start, terms in ((HALF_WIDTH, key_terms), (2 * HALF_WIDTH, value_terms)):
            mixc[at(start + r, 64, 64), :256] = (terms[0] + terms[1][:, :256]).astype(BF16)
            mixc[at(start + r, 64, 64), 256:] = terms[1][:, 256:].astype(BF16)

        @pl.when(right)
        def _():
            far_keys, far_values = kvft[rows, :], kvft[at(HALF_WIDTH + r, 64, 64), :]
            expo = ef[h]
            prob_cot = dot_tn(far_values, far)
            score_cot = (expo.astype(F32) * (prob_cot - far_delta)).astype(BF16)
            o1[rows, :] += dot_nn(far_keys, score_cot)
            mixf[rows, :] = dot_nt(queries, score_cot).astype(BF16)
            mixf[at(HALF_WIDTH + r, 64, 64), :] = dot_nt(far, expo).astype(BF16)

        mixc[rows, :] = (o1[rows, :] * 0.125).astype(BF16)

    def normed_cot(mixed, first_column, columns, store):
        def step(i):
            rows = at(i * 256, 256, 256)
            store(rows, dot_tt(mixed[:, columns], wq[rows, first_column:]))

        loop(3, step, 0)

    def store_to(ref, rows):
        def store(cols, value):
            ref[rows, cols] = value.astype(ref.dtype)

        return store

    clip_peers = [mate, x_peer, diagonal]
    other_clips = [y_peer] + z_peers + yz_peers

    def clip_sum(i):
        return misc(18 + i, vsend.at[0], vrecv.at[i], clip_peers[i])

    def all_sum(i):
        return misc(21 + i, vsend.at[1], vrecv.at[3 + i], other_clips[i])

    loop(HALF_HEADS, attend_back, 0)
    @pl.when(right)
    def _():
        normed_cot(mixf, HALF_WIDTH, oth_rows, store_to(tokf, own_rows))
        nf_mate.start()

    for half in range(2):
        cols = slice(384 * half, 384 * half + 384)
        g_qk[cols, :384] = dot_tt(nc[:, cols], mixc[:384, :]).astype(BF16)
        for i in range(2):
            g_qk[cols, 384 * (i + 1) : 384 * (i + 2)] = (
                dot_tt(nc[:, cols], mixc[384 * (i + 1) : 384 * (i + 2), :])
                + dot_tt(nf[:, cols], mixf[384 * i : 384 * (i + 1), :])
            ).astype(BF16)
        start_first(3, (2 * half, 2 * half + 1))

    normed_cot(mixc, 0, oth_rows, store_to(upo, at(0, ROWS, ROWS)))
    nc_mate.start()

    @pl.when(right)
    def _():
        normed_cot(mixf, HALF_WIDTH, own_rows, store_to(ncot, at(0, ROWS, ROWS)))
        nf_mate.wait()
        tokf[own_rows, :] = (ncot[...] + tokf[oth_rows, :].astype(F32)).astype(BF16)
        nf_far.start()

    normed_cot(mixc, 0, own_rows, store_to(ncot, at(0, ROWS, ROWS)))

    def block_rows(i):
        cols = at(i * 256, 256, 256)
        block_out[:, cols] = (hid[:, cols] + dot_nn(gel[own_rows, :], wd[:, cols])).astype(BF16)

    start_second(0)
    loop(3, block_rows, 0)
    start_second(1)
    start_second(2)
    start_third(0)
    start_third(1)
    start_second(3)
    nc_mate.wait()

    @pl.when(left)
    def _():
        nf_far.wait_recv()
        for copy in tok_far:
            copy.wait_send()

    @pl.when(right)
    def _():
        nf_far.wait_send()

    def first_back(i):
        rows = at(i * 64, 64, 64)
        unit, inverse = normalise(tok[rows, :].astype(F32))
        near = tokc[rows, :].astype(F32)
        far = tokf[at(own + i * 64, 64, 64), :].astype(F32)
        cot = ncot[rows, :] + near + jnp.where(left, far, 0.0)
        input_grad[rows, :] = (hc[rows, :] + normalise_back(cot, gain1, unit, inverse)).astype(BF16)
        vsend[0, 0:1, :] += jnp.sum(cot * unit, axis=0, keepdims=True)
        vsend[0, 1:2, :] += jnp.sum(cot, axis=0, keepdims=True)

    loop(ROWS // 64, first_back, 0)

    for i in range(3):
        clip_sum(i).start()
    start_third(2)
    for i in range(3):
        clip_sum(i).wait()
    vsend[1] = vsend[0] + vrecv[0] + vrecv[1] + vrecv[2]
    for i in range(7):
        all_sum(i).start()
    start_last(0)
    start_third(3)
    for i in range(7):
        all_sum(i).wait()
    sums = vsend[1]
    for i in range(7):
        sums = sums + vrecv[3 + i]
    rank = dp * 4 + ctx
    o_vec[...] = pltpu.roll(sums, lax.rem(WIDTH - rank * 24, WIDTH), 1)[:, :128]
    start_last(1)
    start_last(2)
    start_last(3)
    for w in range(4):
        finish(w)


def hand_out_kernel(
    block_out, input_grad, qk, pr, up, dn, vec,
    o_block, o_input, o_v0, o_v1, o_qk, o_pr, o_v2, o_v3, o_up, o_dn, sem,
):
    pairs = ((block_out, o_block), (input_grad, o_input), (qk, o_qk), (pr, o_pr), (up, o_up), (dn, o_dn))
    copies = [pltpu.make_async_copy(src, dst, sem.at[i]) for i, (src, dst) in enumerate(pairs)]
    for copy in copies:
        copy.start()
    for i, ref in enumerate((o_v0, o_v1, o_v2, o_v3)):
        ref[...] = vec[i, :24]
    for copy in copies:
        copy.wait()


def fused_layer(args):
    vmem, smem, anywhere = (
        pl.BlockSpec(memory_space=pltpu.VMEM),
        pl.BlockSpec(memory_space=pltpu.SMEM),
        pl.BlockSpec(memory_space=pl.ANY),
    )

    def low(*shape):
        return pltpu.VMEM(shape, BF16)

    def full(*shape):
        return pltpu.VMEM(shape, F32)

    def per_block(count):
        return [low(count * rows, width) for rows, width in BLOCKS]

    vector = jax.ShapeDtypeStruct((24,), F32)

    def grad_shape(w):
        return jax.ShapeDtypeStruct((BLOCKS[w][0] // 2, BLOCKS[w][1] * 2), F32)

    rows_out = jax.ShapeDtypeStruct((ROWS, WIDTH), BF16)
    made = pl.pallas_call(
        layer_kernel,
        out_shape=[
            rows_out, rows_out, grad_shape(3), grad_shape(2), grad_shape(1), grad_shape(0),
            jax.ShapeDtypeStruct((8, 128), F32),
        ],
        in_specs=[smem] * 3 + [anywhere] * 2 + [vmem] * 4 + [anywhere] * 4,
        out_specs=[vmem] * 7,
        scratch_shapes=[
            low(256, 768), low(256, 768),
            low(768, 1152), low(768, 768), low(768, 3072), low(3072, 768),
            low(256, 768), low(512, 768), low(512, 768), low(512, 768),
            low(1152, 512), low(768, 512), low(512, 512), low(6, 512, 512), low(6, 512, 512),
            full(384, 512), full(8, 512), full(8, 512), full(8, 512), full(8, 512),
            low(768, 512), full(256, 768), low(512, 768), low(512, 3072), low(256, 3072),
            low(512, 384), low(256, 3072), low(512, 1536), full(256, 768),
            full(256, 768), low(512, 768), low(1152, 512), low(768, 512),
            full(2, 8, 128), full(4, 8, 128), full(2, 8, 768), full(10, 8, 768),
            low(3072, 384), low(768, 1536), low(768, 384), low(768, 1152),
        ]
        + per_block(15) + per_block(7)
        + [pltpu.VMEM((block[0] // 2, block[1]), F32) for block in BLOCKS]
        + [
            pltpu.SemaphoreType.DMA((4, 15)),
            pltpu.SemaphoreType.DMA((4, 15)),
            pltpu.SemaphoreType.DMA((32,)),
            pltpu.SemaphoreType.DMA((32,)),
            pltpu.SemaphoreType.DMA((8,)),
        ],
        compiler_params=pltpu.CompilerParams(
            collective_id=0, has_side_effects=True, vmem_limit_bytes=60 * 1024 * 1024
        ),
    )(*args)
    return pl.pallas_call(
        hand_out_kernel,
        out_shape=[
            rows_out, rows_out, vector, vector, grad_shape(3), grad_shape(2), vector, vector,
            grad_shape(1), grad_shape(0),
        ],
        in_specs=[vmem] * 7,
        out_specs=[anywhere] * 2 + [vmem] * 2 + [anywhere] * 2 + [vmem] * 2 + [anywhere] * 2,
        scratch_shapes=[pltpu.SemaphoreType.DMA((6,))],
        compiler_params=pltpu.CompilerParams(vmem_limit_bytes=60 * 1024 * 1024),
    )(*made)


def general_body(
    tokens,
    attn_gain,
    attn_shift,
    w_qkv,
    w_proj,
    mlp_gain,
    mlp_shift,
    w_up,
    w_down,
    upstream,
    clip_length,
    dataset_group,
    sample_weight,
):
    tok_rows = tokens.shape[0]
    model_width = tokens.shape[1]
    head_count = model_width // HD
    ctx_count = lax.axis_size("ctx")
    seq_rows = tok_rows * ctx_count
    first_row = lax.axis_index("ctx") * tok_rows
    length = clip_length[0]
    key_span = min(seq_rows, max(tok_rows, 512))
    block_count = seq_rows // key_span
    query_pos = first_row + jnp.arange(tok_rows, dtype=jnp.int32)
    last_pos = first_row + tok_rows - 1
    onehot = (dataset_group[0, 0] == jnp.arange(NGROUPS, dtype=jnp.int32)).astype(jnp.float32)
    counts = lax.psum(onehot * length.astype(jnp.float32), "dp")
    total_all = jnp.sum(counts)
    clip_scale = (
        sample_weight[0].astype(jnp.float32) * total_all / (NGROUPS * jnp.sum(onehot * counts))
    )
    x_rows = tokens.astype(jnp.float32)
    normed, norm_one_back = jax.vjp(layer_norm, x_rows, attn_gain, attn_shift)
    normed_low = normed.astype(jnp.bfloat16)
    mixed_qkv = jnp.dot(normed_low, w_qkv, preferred_element_type=jnp.float32).astype(jnp.bfloat16)
    queries = mixed_qkv[:, :model_width]
    key_local = mixed_qkv[:, model_width : 2 * model_width]
    value_local = mixed_qkv[:, 2 * model_width :]
    key_all, value_all = (
        lax.all_gather(key_local, "ctx", axis=0, tiled=True),
        lax.all_gather(value_local, "ctx", axis=0, tiled=True),
    )
    queries3 = queries.reshape(tok_rows, head_count, HD)

    def scores_for(kstart, key_rows):
        piece = key_rows[kstart : kstart + key_span].reshape(key_span, head_count, HD)
        raw = (
            jnp.einsum("qhd,khd->hqk", queries3, piece, preferred_element_type=jnp.float32) * 0.125
        )
        key_pos = kstart + jnp.arange(key_span, dtype=jnp.int32)
        allowed = (key_pos[None, :] <= query_pos[:, None]) & (key_pos[None, :] < length)
        return (jnp.where(allowed[None], raw, NEG_FILL), allowed)

    def useful(kstart):
        return (kstart <= last_pos) & (kstart < length)

    peak = jnp.full((head_count, tok_rows), NEG_FILL, jnp.float32)
    exp_total = jnp.zeros((head_count, tok_rows), jnp.float32)
    for index in range(block_count):
        kstart = index * key_span

        def gather_stats(carry, kstart=kstart):
            old_peak, old_total = carry
            scores, allowed = scores_for(kstart, key_all)
            new_peak = jnp.maximum(old_peak, jnp.max(scores, axis=-1))
            expo_vals = jnp.where(allowed[None], jnp.exp(scores - new_peak[..., None]), 0.0)
            return (
                new_peak,
                old_total * jnp.exp(old_peak - new_peak) + jnp.sum(expo_vals, axis=-1),
            )

        peak, exp_total = lax.cond(
            useful(kstart), gather_stats, lambda carry: carry, (peak, exp_total)
        )

    def probs_for(kstart, key_rows):
        scores, allowed = scores_for(kstart, key_rows)
        return (
            jnp.where(allowed[None], jnp.exp(scores - peak[..., None]), 0.0) / exp_total[..., None]
        )

    out_high = jnp.zeros((tok_rows, head_count, HD), jnp.float32)
    out_rest = jnp.zeros((tok_rows, head_count, HD), jnp.float32)
    for index in range(block_count):
        kstart = index * key_span

        def add_values(carry, kstart=kstart):
            high_acc, rest_acc = carry
            probs = probs_for(kstart, key_all)
            probs_low = probs.astype(jnp.bfloat16)
            remainder = (probs - probs_low.astype(jnp.float32)).astype(jnp.bfloat16)
            piece = value_all[kstart : kstart + key_span].reshape(key_span, head_count, HD)
            high_acc = high_acc + jnp.einsum(
                "hqk,khd->qhd", probs_low, piece, preferred_element_type=jnp.float32
            )
            rest_acc = rest_acc + jnp.einsum(
                "hqk,khd->qhd", remainder, piece, preferred_element_type=jnp.float32
            )
            return (high_acc, rest_acc)

        out_high, out_rest = lax.cond(
            useful(kstart), add_values, lambda carry: carry, (out_high, out_rest)
        )
    attended_low = out_high.reshape(tok_rows, model_width).astype(jnp.bfloat16)
    out_full = out_high + out_rest
    hidden = x_rows + jnp.dot(attended_low, w_proj, preferred_element_type=jnp.float32)
    normed_two, norm_two_back = jax.vjp(layer_norm, hidden, mlp_gain, mlp_shift)
    normed_two_low = normed_two.astype(jnp.bfloat16)
    up_proj = jnp.dot(normed_two_low, w_up, preferred_element_type=jnp.float32)
    gelu_vals, gelu_back = jax.vjp(gelu, up_proj)
    gelu_low = gelu_vals.astype(jnp.bfloat16)
    block_out = (hidden + jnp.dot(gelu_low, w_down, preferred_element_type=jnp.float32)).astype(
        jnp.bfloat16
    )
    valid = query_pos < length
    out_cot = upstream.astype(jnp.float32) * jnp.where(valid, clip_scale, 0.0)[:, None]
    out_cot_low = out_cot.astype(jnp.bfloat16)
    down_grad = jnp.einsum("tf,td->fd", gelu_low, out_cot_low, preferred_element_type=jnp.float32)
    gelu_in = jnp.einsum("td,fd->tf", out_cot_low, w_down, preferred_element_type=jnp.float32)
    (up_cot,) = gelu_back(gelu_in)
    up_cot_low = up_cot.astype(jnp.bfloat16)
    up_grad = jnp.einsum(
        "td,tf->df", normed_two_low, up_cot_low, preferred_element_type=jnp.float32
    )
    normed_two_cot = jnp.einsum("tf,df->td", up_cot_low, w_up, preferred_element_type=jnp.float32)
    norm_two_rows, mlp_gain_grad, mlp_shift_grad = norm_two_back(normed_two_cot)
    hidden_cot = out_cot + norm_two_rows
    hidden_cot_low = hidden_cot.astype(jnp.bfloat16)
    proj_grad = jnp.einsum(
        "ti,to->io", attended_low, hidden_cot_low, preferred_element_type=jnp.float32
    )
    attended_cot = jnp.einsum(
        "to,io->ti", hidden_cot_low, w_proj, preferred_element_type=jnp.float32
    ).astype(jnp.bfloat16)
    attended_cot3 = attended_cot.reshape(tok_rows, head_count, HD)
    delta = jnp.einsum("qhd,qhd->hq", attended_cot3.astype(jnp.float32), out_full)
    key_back, value_back = (key_all, value_all)
    query_cot = jnp.zeros((tok_rows, head_count, HD), jnp.float32)
    key_pieces = []
    value_pieces = []
    empty_piece = jnp.zeros((key_span, head_count, HD), jnp.float32)
    for index in range(block_count):
        kstart = index * key_span

        def block_grads(q_acc, kstart=kstart):
            probs = probs_for(kstart, key_back)
            probs_low = probs.astype(jnp.bfloat16)
            key_piece = key_back[kstart : kstart + key_span].reshape(key_span, head_count, HD)
            value_piece = value_back[kstart : kstart + key_span].reshape(key_span, head_count, HD)
            prob_cot = jnp.einsum(
                "qhd,khd->hqk", attended_cot3, value_piece, preferred_element_type=jnp.float32
            )
            score_cot = (probs * (prob_cot - delta[..., None])).astype(jnp.bfloat16)
            q_acc = (
                q_acc
                + jnp.einsum(
                    "hqk,khd->qhd", score_cot, key_piece, preferred_element_type=jnp.float32
                )
                * 0.125
            )
            key_term = (
                jnp.einsum("hqk,qhd->khd", score_cot, queries3, preferred_element_type=jnp.float32)
                * 0.125
            )
            value_term = jnp.einsum(
                "hqk,qhd->khd", probs_low, attended_cot3, preferred_element_type=jnp.float32
            )
            return (q_acc, key_term, value_term)

        query_cot, key_term, value_term = lax.cond(
            useful(kstart), block_grads, lambda q_acc: (q_acc, empty_piece, empty_piece), query_cot
        )
        key_pieces.append(key_term.reshape(key_span, model_width))
        value_pieces.append(value_term.reshape(key_span, model_width))
    key_terms = jnp.concatenate(key_pieces, axis=0)
    value_terms = jnp.concatenate(value_pieces, axis=0)
    key_cot, value_cot = (
        lax.psum_scatter(
            key_terms.astype(jnp.bfloat16), "ctx", scatter_dimension=0, tiled=True
        ).astype(jnp.float32),
        lax.psum_scatter(
            value_terms.astype(jnp.bfloat16), "ctx", scatter_dimension=0, tiled=True
        ).astype(jnp.float32),
    )
    mixed_cot = jnp.concatenate(
        [query_cot.reshape(tok_rows, model_width), key_cot, value_cot], axis=1
    ).astype(jnp.bfloat16)
    qkv_grad = jnp.einsum("td,te->de", normed_low, mixed_cot, preferred_element_type=jnp.float32)
    normed_cot = jnp.einsum("te,de->td", mixed_cot, w_qkv, preferred_element_type=jnp.float32)
    norm_one_rows, attn_gain_grad, attn_shift_grad = norm_one_back(normed_cot)
    input_grad = (hidden_cot + norm_one_rows).astype(jnp.bfloat16)
    reduced = (
        lax.psum_scatter(attn_gain_grad, ("dp", "ctx"), scatter_dimension=0, tiled=True),
        lax.psum_scatter(attn_shift_grad, ("dp", "ctx"), scatter_dimension=0, tiled=True),
        lax.psum_scatter(qkv_grad, ("dp", "ctx"), scatter_dimension=0, tiled=True),
        lax.psum_scatter(proj_grad, ("dp", "ctx"), scatter_dimension=0, tiled=True),
        lax.psum_scatter(mlp_gain_grad, ("dp", "ctx"), scatter_dimension=0, tiled=True),
        lax.psum_scatter(mlp_shift_grad, ("dp", "ctx"), scatter_dimension=0, tiled=True),
        lax.psum_scatter(up_grad, ("dp", "ctx"), scatter_dimension=0, tiled=True),
        lax.psum_scatter(down_grad, ("dp", "ctx"), scatter_dimension=0, tiled=True),
    )
    return (
        block_out,
        input_grad,
        reduced[0],
        reduced[1],
        reduced[2],
        reduced[3],
        reduced[4],
        reduced[5],
        reduced[6],
        reduced[7],
    )


def fused_body(
    tokens, attn_gain, attn_shift, w_qkv, w_proj, mlp_gain, mlp_shift, w_up, w_down, upstream,
    clip_length, dataset_group, sample_weight,
):
    outs = fused_layer(
        [clip_length, dataset_group.reshape(1), sample_weight, tokens, upstream]
        + [attn_gain, attn_shift, mlp_gain, mlp_shift, w_qkv, w_proj, w_up, w_down]
    )
    return tuple(outs)


def solution(mesh):
    in_specs = (
        P(("dp", "ctx"), None),
        P(),
        P(),
        P(),
        P(),
        P(),
        P(),
        P(),
        P(),
        P(("dp", "ctx"), None),
        P("dp"),
        P("dp", None),
        P("dp"),
    )
    out_specs = (
        P(("dp", "ctx"), None),
        P(("dp", "ctx"), None),
        P(("dp", "ctx")),
        P(("dp", "ctx")),
        P(("dp", "ctx"), None),
        P(("dp", "ctx"), None),
        P(("dp", "ctx")),
        P(("dp", "ctx")),
        P(("dp", "ctx"), None),
        P(("dp", "ctx"), None),
    )
    fused = mesh.shape["dp"] == 8 and mesh.shape["ctx"] == 4
    body = fused_body if fused else general_body
    return jax.shard_map(body, mesh=mesh, in_specs=in_specs, out_specs=out_specs, check_vma=False)
```
